32 devices in a mesh: rep: 4 (over y, x), fsdp: 8 (over z, core).
Axes of the slice: x: 2, y: 2, z: 4, core: 2. Of those that a mesh axis runs over, the one named last changes fastest.
Arguments:
- windows: bfloat16 [12544, 768], P(('rep', 'fsdp')), may hold values from -6 to 6
- slot_table: int32 [64], P(('rep', 'fsdp')), may hold values from 0 to 25, as said below
- cotangent: bfloat16 [12544, 768], P(('rep', 'fsdp')), may hold values from -6 to 6
- qkv_weight: bfloat16 [2, 768, 2304], P(None, 'fsdp'), may hold values from -0.21875 to 0.21875
- qv_bias: bfloat16 [2, 1536], P(None, 'fsdp'), may hold values from -1.1953125 to 1.1953125
- proj_weight: bfloat16 [2, 768, 768], P(None, 'fsdp'), may hold values from -0.875 to 0.875
- proj_bias: bfloat16 [2, 768], P(None, 'fsdp'), may hold values from -1.1953125 to 1.1953125
- norm1_gain: bfloat16 [2, 768], P(None, 'fsdp'), may hold values from 0.5 to 1.5
- norm1_bias: bfloat16 [2, 768], P(None, 'fsdp'), may hold values from -1.1953125 to 1.1953125
- norm2_gain: bfloat16 [2, 768], P(None, 'fsdp'), may hold values from 0.5 to 1.5
- norm2_bias: bfloat16 [2, 768], P(None, 'fsdp'), may hold values from -1.1953125 to 1.1953125
- fc1_weight: bfloat16 [2, 768, 3072], P(None, 'fsdp'), may hold values from -0.21875 to 0.21875
- fc1_bias: bfloat16 [2, 3072], P(None, 'fsdp'), may hold values from -1.1953125 to 1.1953125
- fc2_weight: bfloat16 [2, 3072, 768], P(None, 'fsdp'), may hold values from -0.109375 to 0.109375
- fc2_bias: bfloat16 [2, 768], P(None, 'fsdp'), may hold values from -1.1953125 to 1.1953125
- rel_height: bfloat16 [2, 1728], P(None, 'fsdp'), may hold values from -0.59765625 to 0.59765625
- rel_width: bfloat16 [2, 1728], P(None, 'fsdp'), may hold values from -0.59765625 to 0.59765625
Outputs:
- output: bfloat16 [12544, 768], P(('rep', 'fsdp'))
- input_grad: bfloat16 [12544, 768], P(('rep', 'fsdp'))
- qkv_weight_grad: float32 [2, 768, 2304], P(None, 'fsdp')
- qv_bias_grad: float32 [2, 1536], P(None, 'fsdp')
- proj_weight_grad: float32 [2, 768, 768], P(None, 'fsdp')
- proj_bias_grad: float32 [2, 768], P(None, 'fsdp')
- norm1_gain_grad: float32 [2, 768], P(None, 'fsdp')
- norm1_bias_grad: float32 [2, 768], P(None, 'fsdp')
- norm2_gain_grad: float32 [2, 768], P(None, 'fsdp')
- norm2_bias_grad: float32 [2, 768], P(None, 'fsdp')
- fc1_weight_grad: float32 [2, 768, 3072], P(None, 'fsdp')
- fc1_bias_grad: float32 [2, 3072], P(None, 'fsdp')
- fc2_weight_grad: float32 [2, 3072, 768], P(None, 'fsdp')
- fc2_bias_grad: float32 [2, 768], P(None, 'fsdp')
- rel_height_grad: float32 [2, 1728], P(None, 'fsdp')
- rel_width_grad: float32 [2, 1728], P(None, 'fsdp')
The draws below stay inside these ranges and needn't reach their ends.
Inputs may be any that keep to these rules, and one draw needn't show every extreme that they name: `slot_table`: entries 0 to 24 name a window's place in its image's 5 x 5 grid of windows, row by row; 25 marks an empty slot. Within each replica group the k-th window in order (images one after the other, each with all its windows in order, the last one possibly cut) stands on fsdp index k % 8 in its slot k // 8; each group fills at least half of its 16 slots and leaves at least one empty.
All inputs are finite; a program needn't handle non-finite values.
Results may differ from the reference program's by a relative error of at most 0.025.
Values may be sent and summed in bfloat16 or wider, within the bound.
No kernel may reach another device: no remote copies, remote signals or barrier semaphores. Data moves between devices by JAX's collectives and lax.ppermute only.
A program may use at most 256 MiB of HBM per device.

```python
import jax
import jax.numpy as jnp
from jax import lax

D = 768
HEADS = 12
HD = 64
FF = 3072
WINDOW = 14
SIDE = 64
LAYERS = 2
WIN_DEV = 2
GRID = 5
TOKW = 196
RELS = 27
SLOTS = 64
N_REP = 4
N_FSDP = 8


def draw_slot_table(key, part):
    key = jax.random.fold_in(key, 7)
    per_group = N_FSDP * WIN_DEV
    places = jnp.arange(N_REP * per_group, dtype=jnp.int32)
    group_of = places // per_group
    within = places % per_group
    dealt_order = within % WIN_DEV * N_FSDP + within // WIN_DEV
    filled = jax.random.randint(key, (N_REP,), (per_group + 1) // 2, per_group, dtype=jnp.int32)
    return jnp.where(dealt_order < filled[group_of], dealt_order % (GRID * GRID), GRID * GRID).astype(jnp.int32)


def block_levels(key, shape, cuts, low, largest):
    def one(dim, shards_of):
        draws = jax.random.uniform(jax.random.fold_in(jax.random.fold_in(key, 6), dim), (shards_of,), jnp.float32, low / len(cuts), largest / len(cuts))
        return jnp.repeat(jnp.exp(draws), shape[dim] // shards_of).reshape((-1,) + (1,) * (len(shape) - dim - 1))

    factor_of = one(*cuts[0])
    for cut in cuts[1:]:
        factor_of = factor_of * one(*cut)
    return factor_of


def bell_draw(key, shape, deviation, most, cuts=(), kind=jnp.bfloat16):
    level = block_levels(key, shape, cuts, -0.22, 0.18) if cuts else 1.0
    drawn = jax.random.normal(key, shape, jnp.float32) * deviation * level
    return jnp.minimum(jnp.maximum(drawn, -most), most).astype(kind)


def setup_inputs(seed: int = 0) -> dict:
    key_of = jax.random.split(jax.random.key(seed), 18)
    windows = bell_draw(key_of[0], (SLOTS * TOKW, D), 1.0, 6.0, ((0, 32),))
    slot_table = draw_slot_table(jax.random.fold_in(key_of[17], 71), 0)
    cotangent = bell_draw(key_of[2], (SLOTS * TOKW, D), 1.0, 6.0, ((0, 32),))
    qkv_weight = bell_draw(key_of[3], (LAYERS, D, 3 * D), D ** -0.5, 0.21875, ((1, 8),))
    qv_bias = bell_draw(key_of[4], (LAYERS, 2 * D), 0.2, 1.1953125, ((1, 8),))
    proj_weight = bell_draw(key_of[5], (LAYERS, D, D), (D // 16) ** -0.5, 0.875, ((1, 8),))
    proj_bias = bell_draw(key_of[6], (LAYERS, D), 0.2, 1.1953125, ((1, 8),))
    norm1_gain = jnp.clip(1.0 + 0.1 * jax.random.normal(key_of[7], (LAYERS, D), jnp.float32), 0.5, 1.5).astype(jnp.bfloat16)
    norm1_bias = bell_draw(key_of[8], (LAYERS, D), 0.2, 1.1953125, ((1, 8),))
    norm2_gain = jnp.clip(1.0 + 0.1 * jax.random.normal(key_of[9], (LAYERS, D), jnp.float32), 0.5, 1.5).astype(jnp.bfloat16)
    norm2_bias = bell_draw(key_of[10], (LAYERS, D), 0.2, 1.1953125, ((1, 8),))
    fc1_weight = bell_draw(key_of[11], (LAYERS, D, FF), D ** -0.5, 0.21875, ((1, 8),))
    fc1_bias = bell_draw(key_of[12], (LAYERS, FF), 0.2, 1.1953125, ((1, 8),))
    fc2_weight = bell_draw(key_of[13], (LAYERS, FF, D), FF ** -0.5, 0.109375, ((1, 8),))
    fc2_bias = bell_draw(key_of[14], (LAYERS, D), 0.2, 1.1953125, ((1, 8),))
    rel_height = bell_draw(key_of[15], (LAYERS, RELS * HD), 0.1, 0.59765625, ((1, 8),))
    rel_width = bell_draw(key_of[16], (LAYERS, RELS * HD), 0.1, 0.59765625, ((1, 8),))
    return dict(windows=windows, slot_table=slot_table, cotangent=cotangent, qkv_weight=qkv_weight, qv_bias=qv_bias, proj_weight=proj_weight, proj_bias=proj_bias, norm1_gain=norm1_gain, norm1_bias=norm1_bias, norm2_gain=norm2_gain, norm2_bias=norm2_bias, fc1_weight=fc1_weight, fc1_bias=fc1_bias, fc2_weight=fc2_weight, fc2_bias=fc2_bias, rel_height=rel_height, rel_width=rel_width)


HIGHEST = lax.Precision.HIGHEST
EPSILON = 1e-06

@jax.custom_vjp
def low(v):
    return lax.optimization_barrier(v.astype(jnp.bfloat16)).astype(jnp.float32)

@jax.custom_vjp
def low_back(v):
    return v

def low_keep(v):
    return (low(v), None)

def low_pass(kept, grad):
    return (grad,)

def back_keep(v):
    return (v, None)

def back_low(kept, grad):
    return (low(grad),)
low.defvjp(low_keep, low_pass)
low_back.defvjp(back_keep, back_low)

def norm_rows(values, gain, shift):
    centre = lax.optimization_barrier(jnp.mean(values, -1, keepdims=True))
    centered = values - centre
    spread = lax.optimization_barrier(jnp.mean(centered * centered, -1, keepdims=True))
    return centered * lax.rsqrt(spread + EPSILON) * gain + shift

def relative_rows(table_flat):
    table_rows = table_flat.reshape(2 * WINDOW - 1, HD)
    places = jnp.arange(WINDOW, dtype=jnp.int32)
    offsets = places[:, None] - places[None, :] + WINDOW - 1
    one_hot = (offsets[:, :, None] == jnp.arange(2 * WINDOW - 1, dtype=jnp.int32)[None, None, :]).astype(jnp.float32)
    return jnp.einsum('ikr,re->ike', one_hot, table_rows, precision=HIGHEST)

def window_mask(slot_table):
    places = jnp.arange(WINDOW, dtype=jnp.int32)
    rows_inside = slot_table[:, None] // GRID * WINDOW + places[None, :] < SIDE
    cols_inside = slot_table[:, None] % GRID * WINDOW + places[None, :] < SIDE
    both_inside = rows_inside[:, :, None] & cols_inside[:, None, :]
    return both_inside.astype(jnp.float32).reshape(slot_table.shape[0], WINDOW * WINDOW)

def project(values, weight):
    return jnp.einsum('bsd,de->bse', values, weight, precision=HIGHEST)

def window_layer(tokens, live_mask, layer_weights):
    qkv_weight, qv_bias, proj_weight, proj_bias, norm1_gain, norm1_bias, norm2_gain, norm2_bias, fc1_weight, fc1_bias, fc2_weight, fc2_bias, rel_height, rel_width = layer_weights
    model_width = tokens.shape[-1]
    blocks = tokens.shape[0]
    window_span = WINDOW * WINDOW
    live_rows = live_mask[:, :, None]
    normed = low(norm_rows(tokens, norm1_gain, norm1_bias) * live_rows)
    projected = project(normed, qkv_weight)
    query_rows = low(low_back(projected[:, :, :model_width] + qv_bias[:model_width]))
    key_rows = low(low_back(projected[:, :, model_width:2 * model_width]))
    value_rows = low(low_back(projected[:, :, 2 * model_width:] + qv_bias[model_width:]))
    query_rows = query_rows.reshape(blocks, window_span, HEADS, HD)
    key_rows = key_rows.reshape(blocks, window_span, HEADS, HD)
    value_rows = value_rows.reshape(blocks, window_span, HEADS, HD)
    heights = relative_rows(rel_height)
    widths = relative_rows(rel_width)
    query_grid = query_rows.reshape(blocks, WINDOW, WINDOW, HEADS, HD)
    along_height = jnp.einsum('bijhe,ike->bhijk', query_grid, heights, precision=HIGHEST)
    along_width = jnp.einsum('bijhe,jke->bhijk', query_grid, widths, precision=HIGHEST)
    products = jnp.einsum('bshe,bthe->bhst', query_rows, key_rows, precision=HIGHEST) * HD ** (-0.5)
    scores = products.reshape(blocks, HEADS, WINDOW, WINDOW, WINDOW, WINDOW)
    scores = scores + along_height[..., None] + along_width[..., None, :]
    scores = low_back(scores.reshape(blocks, HEADS, window_span, window_span))
    probs_low = low(jax.nn.softmax(scores, axis=-1))
    attended = jnp.einsum('bhst,bthe->bshe', probs_low, value_rows, precision=HIGHEST)
    attended = low(low_back(attended)).reshape(blocks, window_span, model_width)
    branch = low_back(project(attended, proj_weight) + proj_bias)
    middle = tokens + live_rows * branch
    hidden_in = low(norm_rows(middle, norm2_gain, norm2_bias))
    hidden = low_back(project(hidden_in, fc1_weight) + fc1_bias)
    activated = low(jax.nn.gelu(hidden, approximate=False))
    return middle + live_rows * low_back(project(activated, fc2_weight) + fc2_bias)

def reference(windows, slot_table, cotangent, qkv_weight, qv_bias, proj_weight, proj_bias, norm1_gain, norm1_bias, norm2_gain, norm2_bias, fc1_weight, fc1_bias, fc2_weight, fc2_bias, rel_height, rel_width):
    live_mask = window_mask(slot_table)
    model_width = windows.shape[1]
    window_span = WINDOW * WINDOW
    params = (qkv_weight.astype(jnp.float32), qv_bias.astype(jnp.float32), proj_weight.astype(jnp.float32), proj_bias.astype(jnp.float32), norm1_gain.astype(jnp.float32), norm1_bias.astype(jnp.float32), norm2_gain.astype(jnp.float32), norm2_bias.astype(jnp.float32), fc1_weight.astype(jnp.float32), fc1_bias.astype(jnp.float32), fc2_weight.astype(jnp.float32), fc2_bias.astype(jnp.float32), rel_height.astype(jnp.float32), rel_width.astype(jnp.float32))
    tokens = windows.astype(jnp.float32).reshape(-1, window_span, model_width)
    block_count = tokens.shape[0] // 8

    def forward(tokens, params):

        def block_fn(block_pair):
            block_value, block_mask = block_pair
            for layer_index in range(LAYERS):
                block_value = window_layer(block_value, block_mask, tuple((p[layer_index] for p in params)))
            return block_value
        result = lax.map(jax.checkpoint(block_fn), (tokens.reshape(block_count, 8, window_span, model_width), live_mask.reshape(block_count, 8, window_span)))
        return result.reshape(-1, model_width)
    result, pull_back = jax.vjp(forward, tokens, params)
    grad_tokens, grads = pull_back(cotangent.astype(jnp.float32))
    return (result.astype(jnp.bfloat16), grad_tokens.reshape(-1, model_width).astype(jnp.bfloat16), grads[0], grads[1], grads[2], grads[3], grads[4], grads[5], grads[6], grads[7], grads[8], grads[9], grads[10], grads[11], grads[12], grads[13])
```

```python
import functools

import jax
import jax.numpy as jnp
import numpy as np
from jax import lax
from jax.experimental import pallas as pl
from jax.experimental.pallas import tpu as pltpu
from jax.sharding import PartitionSpec as P

HEADS = 12
HD = 64
WINDOW = 14
SIDE = 64
LAYERS = 2
GRID = 5
RELS = 2 * WINDOW - 1
EPSILON = 1e-06
PITCH = 16
SPAN = WINDOW * PITCH
PAIRS = HEADS // 2
LANES = 2 * HD
F32 = jnp.float32
BF16 = jnp.bfloat16
CHUNK = 256
ROWS_STEP = 64
VMEM_LIMIT = 56 * 1024 * 1024


def dot_nn(a, b):
    return lax.dot_general(a, b, (((1,), (0,)), ((), ())), preferred_element_type=F32)


def dot_nt(a, b):
    return lax.dot_general(a, b, (((1,), (1,)), ((), ())), preferred_element_type=F32)


def dot_tn(a, b):
    return lax.dot_general(a, b, (((0,), (0,)), ((), ())), preferred_element_type=F32)


def norm_rows(values):
    centre = jnp.mean(values, -1, keepdims=True)
    centered = values - centre
    inverse = lax.rsqrt(jnp.mean(centered * centered, -1, keepdims=True) + EPSILON)
    return centered * inverse, inverse


def norm_back(grad, normed, inverse, gain):
    scaled = grad * gain
    return inverse * (
        scaled
        - jnp.mean(scaled, -1, keepdims=True)
        - normed * jnp.mean(scaled * normed, -1, keepdims=True)
    )


def each(count, step, body):
    def run(index, carry):
        body(pl.multiple_of(index * step, step))
        return carry

    lax.fori_loop(0, count, run, 0)


def each_index(count, body):
    def run(index, carry):
        body(index)
        return carry

    lax.fori_loop(0, count, run, 0)


def half_lane():
    return lax.broadcasted_iota(jnp.int32, (SPAN, LANES), 1)


def split_heads(pair):
    lane = half_lane()
    zero = jnp.zeros_like(pair)
    return jnp.concatenate(
        [jnp.where(lane < HD, pair, zero), jnp.where(lane < HD, zero, pair)], axis=0
    )


def join_heads(stacked):
    return jnp.where(half_lane() < HD, stacked[:SPAN], stacked[SPAN:])


def shift_rows(table):
    by_row = jnp.concatenate(
        [
            pltpu.roll(table[i * PITCH : (i + 1) * PITCH], i, axis=1) if i else table[:PITCH]
            for i in range(WINDOW)
        ],
        axis=0,
    )
    by_col = pltpu.roll(
        table.reshape(WINDOW, PITCH, LANES), 0, axis=2, stride=1, stride_axis=1
    ).reshape(SPAN, LANES)
    return jnp.where(half_lane() < HD, by_row, by_col)


def key_tables():
    ahead = np.zeros((SPAN, LANES), np.float32)
    back = np.zeros((SPAN, LANES), np.float32)
    for k in range(WINDOW):
        for m in range(PITCH):
            row = k * PITCH + m
            ahead[row, WINDOW - 1 + k] = 1.0
            back[row, WINDOW - 1 - k] = 1.0
            if m < WINDOW:
                ahead[row, HD + WINDOW - 1 + m] = 1.0
                back[row, HD + WINDOW - 1 - m] = 1.0
            else:
                ahead[row, LANES - 1] = -1e30
    return jnp.asarray(ahead, BF16), jnp.asarray(back, BF16)


def fetch(copies):
    for copy in copies:
        copy.start()


def attend_kernel(blocks, loader, *refs):
    (x_ref, live_ref, vec_ref, table_ref, keys_ref), refs = refs[:5], refs[5:]
    weight_refs, refs = refs[: blocks], refs[blocks:]
    (mid_ref, h1_ref, q_ref, k_ref, v_ref, p_ref, att_ref), refs = refs[:7], refs[7:]
    w_ref, sem = refs
    ready = loader(weight_refs, w_ref, sem)
    width = x_ref.shape[1]

    def first_norm(start):
        rows = pl.ds(start, ROWS_STEP)
        normed, _ = norm_rows(x_ref[rows, :].astype(F32))
        shaped = (normed * vec_ref[0:1, :] + vec_ref[1:2, :]) * live_ref[rows, :]
        h1_ref[rows, :] = shaped.astype(BF16)

    each(x_ref.shape[0] // ROWS_STEP, ROWS_STEP, first_norm)
    ready()
    for index, (out_ref, bias) in enumerate(((q_ref, 2), (k_ref, None), (v_ref, 3))):

        def project(start, index=index, out_ref=out_ref, bias=bias):
            cols = pl.ds(start, CHUNK)
            made = dot_nn(h1_ref[...], w_ref[index, :, cols])
            if bias is not None:
                made = made + vec_ref[bias : bias + 1, cols]
            out_ref[:, cols] = made.astype(BF16)

        each(width // CHUNK, CHUNK, project)

    def attend(index):
        rows = pl.ds(pl.multiple_of(index // PAIRS * SPAN, SPAN), SPAN)
        cols = pl.ds(pl.multiple_of(index % PAIRS * LANES, LANES), LANES)
        queries = q_ref[rows, cols]
        offsets = dot_nn(queries, table_ref[...])
        lane = half_lane()
        sides = []
        for half in range(2):
            moved = shift_rows(offsets[:, half * LANES : (half + 1) * LANES])
            sides.append(jnp.where(lane == LANES - 1, 1.0, moved).astype(BF16))
        left = jnp.concatenate(
            [split_heads(queries) * HD ** (-0.5), jnp.concatenate(sides, axis=0)], axis=1
        )
        right = jnp.concatenate([k_ref[rows, cols], keys_ref[...]], axis=1)
        scores = dot_nt(left, right)
        shifted = jnp.exp(scores - jnp.max(scores, -1, keepdims=True))
        probs = shifted * (1.0 / jnp.sum(shifted, -1, keepdims=True))
        low = probs.astype(BF16)
        p_ref[index] = low
        att_ref[rows, cols] = join_heads(dot_nn(low, v_ref[rows, cols])).astype(BF16)

    each_index(x_ref.shape[0] // SPAN * PAIRS, attend)

    def finish(start):
        cols = pl.ds(start, CHUNK)
        branch = dot_nn(att_ref[...], w_ref[3, :, cols]) + vec_ref[4:5, cols]
        mid_ref[:, cols] = x_ref[:, cols].astype(F32) + live_ref[...] * branch

    each(width // CHUNK, CHUNK, finish)


def mlp_kernel(blocks, loader, *refs):
    (mid_ref, live_ref, vec_ref, bias_ref), refs = refs[:4], refs[4:]
    weight_refs, refs = refs[: sum(blocks)], refs[sum(blocks) :]
    (out_ref, h2_ref, act_ref, slope_ref), refs = refs[:4], refs[4:]
    w1_ref, w2_ref, sem = refs
    ready1, ready2 = loader(weight_refs, w1_ref, w2_ref, sem)
    width = mid_ref.shape[1]
    hidden_width = act_ref.shape[1]

    def second_norm(start):
        rows = pl.ds(start, ROWS_STEP)
        normed, _ = norm_rows(mid_ref[rows, :])
        h2_ref[rows, :] = (normed * vec_ref[5:6, :] + vec_ref[6:7, :]).astype(BF16)

    each(mid_ref.shape[0] // ROWS_STEP, ROWS_STEP, second_norm)
    ready1()

    def expand(index):
        start = pl.multiple_of(index * CHUNK, CHUNK)
        cols = pl.ds(start, CHUNK)
        inner = pl.ds(pl.multiple_of(start % width, CHUNK), CHUNK)
        hidden = dot_nn(h2_ref[...], w1_ref[start // width, :, inner]) + bias_ref[:, cols]
        below = 0.5 * (1.0 + lax.erf(hidden * (0.5**0.5)))
        bell = jnp.exp(-0.5 * hidden * hidden) * (0.5 / np.pi) ** 0.5
        act_ref[:, cols] = (hidden * below).astype(BF16)
        slope_ref[:, cols] = (below + hidden * bell).astype(BF16)

    each_index(hidden_width // CHUNK, expand)
    ready2()

    def contract(start):
        cols = pl.ds(start, CHUNK)
        made = dot_nn(act_ref[...], w2_ref[:, cols]) + vec_ref[7:8, cols]
        out_ref[:, cols] = mid_ref[:, cols] + live_ref[...] * made

    each(width // CHUNK, CHUNK, contract)


def mlp_back_kernel(blocks, loader, *refs):
    (grad_ref, mid_ref, live_ref, vec_ref, h2_ref, act_ref, slope_ref), refs = refs[:7], refs[7:]
    weight_refs, refs = refs[: sum(blocks)], refs[sum(blocks) :]
    (dmid_ref, g1_ref, g2_ref, sums_ref, hsum_ref), refs = refs[:5], refs[5:]
    w1_ref, w2_ref, dm_ref, dh_ref, ds_ref, sem = refs
    ready1, ready2 = loader(weight_refs, w1_ref, w2_ref, sem)
    width = mid_ref.shape[1]
    hidden_width = act_ref.shape[1]
    count = mid_ref.shape[0] // ROWS_STEP

    dm_ref[...] = (live_ref[...] * grad_ref[...].astype(F32)).astype(BF16)

    def second_weight(start):
        rows = pl.ds(start, CHUNK)
        g2_ref[rows, :] = dot_tn(act_ref[:, rows], dm_ref[...]).astype(BF16)

    each(hidden_width // CHUNK, CHUNK, second_weight)
    sums_ref[...] = jnp.zeros_like(sums_ref)
    sums_ref[0:1, :] = jnp.sum(dm_ref[...].astype(F32), 0, keepdims=True)
    ready2()

    def inner_grad(start):
        cols = pl.ds(start, CHUNK)
        made = (dot_nt(dm_ref[...], w2_ref[cols, :]) * slope_ref[:, cols].astype(F32)).astype(BF16)
        dh_ref[:, cols] = made
        hsum_ref[:, cols] = jnp.sum(made.astype(F32), 0, keepdims=True)

    each(hidden_width // CHUNK, CHUNK, inner_grad)
    ready1()

    def first_weight(index):
        start = pl.multiple_of(index * CHUNK, CHUNK)
        inner = pl.ds(pl.multiple_of(start % width, CHUNK), CHUNK)
        g1_ref[start // width, :, inner] = dot_tn(
            h2_ref[...], dh_ref[:, pl.ds(start, CHUNK)]
        ).astype(BF16)

    each_index(hidden_width // CHUNK, first_weight)

    def back_in(start):
        rows = pl.ds(start, CHUNK)
        made = dot_nt(dh_ref[:, 0:width], w1_ref[0, rows, :])
        for block in range(1, hidden_width // width):
            made += dot_nt(
                dh_ref[:, block * width : (block + 1) * width], w1_ref[block, rows, :]
            )
        ds_ref[:, rows] = made

    each(width // CHUNK, CHUNK, back_in)

    def back_norm(start):
        rows = pl.ds(start, ROWS_STEP)
        normed, inverse = norm_rows(mid_ref[rows, :])
        grad = ds_ref[rows, :]
        sums_ref[1:2, :] += jnp.sum(grad * normed, 0, keepdims=True)
        sums_ref[2:3, :] += jnp.sum(grad, 0, keepdims=True)
        dmid_ref[rows, :] = grad_ref[rows, :].astype(F32) + norm_back(
            grad, normed, inverse, vec_ref[5:6, :]
        )

    each(count, ROWS_STEP, back_norm)


def attend_back_kernel(blocks, loader, *refs):
    (
        dmid_ref,
        x_ref,
        live_ref,
        vec_ref,
        table_ref,
        keys_ref,
        h1_ref,
        q_ref,
        k_ref,
        v_ref,
        p_ref,
        att_ref,
    ), refs = refs[:12], refs[12:]
    weight_refs, refs = refs[:blocks], refs[blocks:]
    (next_ref, g_ref, sums_ref, rel_ref), refs = refs[:4], refs[4:]
    w_ref, db_ref, da_ref, dq_ref, dk_ref, dv_ref, dh_ref, sem = refs
    ready = loader(weight_refs, w_ref, sem)
    width = x_ref.shape[1]
    count = x_ref.shape[0] // ROWS_STEP

    db_ref[...] = (live_ref[...] * dmid_ref[...]).astype(BF16)
    sums_ref[...] = jnp.zeros_like(sums_ref)
    sums_ref[0:1, :] = jnp.sum(db_ref[...].astype(F32), 0, keepdims=True)
    rel_ref[...] = jnp.zeros_like(rel_ref)

    def out_weight(start):
        cols = pl.ds(start, CHUNK)
        g_ref[3, :, cols] = dot_tn(att_ref[...], db_ref[:, cols]).astype(BF16)

    each(width // CHUNK, CHUNK, out_weight)
    ready()

    def back_out(start):
        rows = pl.ds(start, CHUNK)
        da_ref[:, rows] = dot_nt(db_ref[...], w_ref[3, rows, :]).astype(BF16)

    each(width // CHUNK, CHUNK, back_out)

    def attend(index):
        rows = pl.ds(pl.multiple_of(index // PAIRS * SPAN, SPAN), SPAN)
        cols = pl.ds(pl.multiple_of(index % PAIRS * LANES, LANES), LANES)
        low = p_ref[index]
        probs = low.astype(F32)
        outer = split_heads(da_ref[rows, cols])
        queries = split_heads(q_ref[rows, cols])
        d_probs = dot_nt(outer, v_ref[rows, cols])
        dv_ref[rows, cols] = dot_tn(low, outer).astype(BF16)
        mean = jnp.sum(d_probs * probs, -1, keepdims=True)
        d_scores = (probs * (d_probs - mean)).astype(BF16)
        both = dot_nn(d_scores, jnp.concatenate([k_ref[rows, cols], keys_ref[...]], axis=1))
        moved = [
            shift_rows(both[half * SPAN : (half + 1) * SPAN, LANES:]).astype(BF16)
            for half in range(2)
        ]
        rel_part = dot_nt(jnp.concatenate(moved, axis=1), table_ref[...])
        direct = join_heads(both[:, :LANES]) * HD ** (-0.5)
        dq_ref[rows, cols] = (direct + rel_part).astype(BF16)
        dk_ref[rows, cols] = (dot_tn(d_scores, queries) * HD ** (-0.5)).astype(BF16)
        rel_ref[...] += dot_tn(jnp.concatenate(moved, axis=0), queries)

    each_index(x_ref.shape[0] // SPAN * PAIRS, attend)
    sums_ref[1:2, :] = jnp.sum(dq_ref[...].astype(F32), 0, keepdims=True)
    sums_ref[2:3, :] = jnp.sum(dv_ref[...].astype(F32), 0, keepdims=True)
    for index, part_ref in enumerate((dq_ref, dk_ref, dv_ref)):

        def in_weight(start, index=index, part_ref=part_ref):
            cols = pl.ds(start, CHUNK)
            g_ref[index, :, cols] = dot_tn(h1_ref[...], part_ref[:, cols]).astype(BF16)

        each(width // CHUNK, CHUNK, in_weight)

    def back_in(start):
        rows = pl.ds(start, CHUNK)
        made = dot_nt(dq_ref[...], w_ref[0, rows, :])
        made += dot_nt(dk_ref[...], w_ref[1, rows, :])
        made += dot_nt(dv_ref[...], w_ref[2, rows, :])
        dh_ref[:, rows] = made * live_ref[...]

    each(width // CHUNK, CHUNK, back_in)

    def back_norm(start):
        rows = pl.ds(start, ROWS_STEP)
        normed, inverse = norm_rows(x_ref[rows, :].astype(F32))
        grad = dh_ref[rows, :]
        sums_ref[3:4, :] += jnp.sum(grad * normed, 0, keepdims=True)
        sums_ref[4:5, :] += jnp.sum(grad, 0, keepdims=True)
        next_ref[rows, :] = dmid_ref[rows, :] + norm_back(grad, normed, inverse, vec_ref[0:1, :])

    each(count, ROWS_STEP, back_norm)


VM = pl.BlockSpec(memory_space=pltpu.VMEM)
ANY = pl.BlockSpec(memory_space=pl.ANY)


def call(kernel, resident, pieces, outs, scratch, flops):
    moved = sum(a.size * a.dtype.itemsize for a in (*resident, *pieces, *outs))
    return pl.pallas_call(
        kernel,
        out_shape=tuple(outs),
        in_specs=[VM] * len(resident) + [ANY] * len(pieces),
        out_specs=tuple([VM] * len(outs)),
        scratch_shapes=scratch,
        compiler_params=pltpu.CompilerParams(vmem_limit_bytes=VMEM_LIMIT),
        cost_estimate=pl.CostEstimate(flops=int(flops), bytes_accessed=int(moved), transcendentals=0),
    )(*resident, *pieces)


def shape(dims, kind):
    return jax.ShapeDtypeStruct(tuple(dims), kind)


def whole_attention(weight_refs, w_ref, sem):
    qkv_ref, proj_ref = weight_refs
    width = w_ref.shape[1]
    copies = [
        pltpu.make_async_copy(qkv_ref.at[:, pl.ds(i * width, width)], w_ref.at[i], sem.at[i])
        for i in range(3)
    ]
    copies.append(pltpu.make_async_copy(proj_ref, w_ref.at[3], sem.at[3]))
    fetch(copies)

    def ready():
        for copy in copies:
            copy.wait()

    return ready


def whole_mlp(weight_refs, w1_ref, w2_ref, sem):
    fc1_ref, fc2_ref = weight_refs
    width = w1_ref.shape[1]
    first = [
        pltpu.make_async_copy(fc1_ref.at[:, pl.ds(i * width, width)], w1_ref.at[i], sem.at[i])
        for i in range(w1_ref.shape[0])
    ]
    second = [pltpu.make_async_copy(fc2_ref, w2_ref, sem.at[w1_ref.shape[0]])]
    fetch(first)
    fetch(second)

    def ready1():
        for copy in first:
            copy.wait()

    def ready2():
        for copy in second:
            copy.wait()

    return ready1, ready2


def attend_forward(x, live, vec, table, keys, pieces, loader):
    rows, width = x.shape
    outs = (
        shape((rows, width), F32),
        *[shape((rows, width), BF16)] * 4,
        shape((rows // SPAN * PAIRS, 2 * SPAN, SPAN), BF16),
        shape((rows, width), BF16),
    )
    scratch = [pltpu.VMEM((4, width, width), BF16), pltpu.SemaphoreType.DMA((len(pieces) + 2,))]
    return call(
        functools.partial(attend_kernel, len(pieces), loader),
        (x, live, vec, table, keys),
        pieces,
        outs,
        scratch,
        2 * rows * width * 4 * width,
    )


def mlp_forward(mid, live, vec, bias, pieces, loader, counts):
    rows, width = mid.shape
    hidden = bias.shape[1]
    outs = (
        shape((rows, width), F32),
        shape((rows, width), BF16),
        shape((rows, hidden), BF16),
        shape((rows, hidden), BF16),
    )
    scratch = [
        pltpu.VMEM((hidden // width, width, width), BF16),
        pltpu.VMEM((hidden, width), BF16),
        pltpu.SemaphoreType.DMA((8,)),
    ]
    return call(
        functools.partial(mlp_kernel, counts, loader),
        (mid, live, vec, bias),
        pieces,
        outs,
        scratch,
        4 * rows * width * hidden,
    )


def mlp_backward(grad, mid, live, vec, h2, act, slope, pieces, loader, counts):
    rows, width = mid.shape
    hidden = act.shape[1]
    outs = (
        shape((rows, width), F32),
        shape((hidden // width, width, width), BF16),
        shape((hidden, width), BF16),
        shape((8, width), F32),
        shape((1, hidden), F32),
    )
    scratch = [
        pltpu.VMEM((hidden // width, width, width), BF16),
        pltpu.VMEM((hidden, width), BF16),
        pltpu.VMEM((rows, width), BF16),
        pltpu.VMEM((rows, hidden), BF16),
        pltpu.VMEM((rows, width), F32),
        pltpu.SemaphoreType.DMA((8,)),
    ]
    return call(
        functools.partial(mlp_back_kernel, counts, loader),
        (grad, mid, live, vec, h2, act, slope),
        pieces,
        outs,
        scratch,
        8 * rows * width * hidden,
    )


def attend_backward(dmid, x, live, vec, table, keys, h1, q, k, v, p, att, pieces, loader):
    rows, width = x.shape
    outs = (
        shape((rows, width), F32),
        shape((4, width, width), BF16),
        shape((8, width), F32),
        shape((LANES, LANES), F32),
    )
    scratch = [
        pltpu.VMEM((4, width, width), BF16),
        *[pltpu.VMEM((rows, width), BF16)] * 5,
        pltpu.VMEM((rows, width), F32),
        pltpu.SemaphoreType.DMA((len(pieces) + 2,)),
    ]
    return call(
        functools.partial(attend_back_kernel, len(pieces), loader),
        (dmid, x, live, vec, table, keys, h1, q, k, v, p, att),
        pieces,
        outs,
        scratch,
        4 * rows * width * 4 * width,
    )


def live_rows(slot_table):
    places = jnp.arange(PITCH, dtype=jnp.int32)
    rows_inside = slot_table[:, None] // GRID * WINDOW + places[None, :WINDOW] < SIDE
    cols_inside = slot_table[:, None] % GRID * WINDOW + places[None, :] < SIDE
    cols_inside = cols_inside & (places < WINDOW)[None, :]
    both_inside = rows_inside[:, :, None] & cols_inside[:, None, :]
    return both_inside.astype(F32).reshape(slot_table.shape[0] * SPAN, 1)


def spread(values):
    width = values.shape[1]
    grid = values.reshape(-1, WINDOW, width)
    return jnp.pad(grid, ((0, 0), (0, PITCH - WINDOW), (0, 0))).reshape(-1, width)


def gather_back(values):
    width = values.shape[1]
    return values.reshape(-1, PITCH, width)[:, :WINDOW].reshape(-1, width)


def relative_tables(rel_height, rel_width):
    stacked = jnp.stack([rel_height, rel_width], 1).reshape(LAYERS, 2, RELS, HD)

    def spread_table(rows):
        padded = jnp.pad(rows, ((0, 0), (0, 0), (0, HD - RELS), (0, 0)))
        one = padded.reshape(LAYERS, LANES, HD).transpose(0, 2, 1)
        none = jnp.zeros_like(one)
        return jnp.concatenate(
            [jnp.concatenate([one, none], 2), jnp.concatenate([none, one], 2)], 1
        )

    return spread_table(stacked[:, :, ::-1]), spread_table(stacked)


SMALL = (
    "qv_bias", "proj_bias", "norm1_gain", "norm1_bias", "norm2_gain", "norm2_bias",
    "fc1_bias", "fc2_bias", "rel_height", "rel_width",
)


def gather_small(parts):
    packed = jnp.concatenate(parts, axis=1)
    whole = lax.all_gather(packed, "fsdp", axis=0, tiled=False)
    found = []
    start = 0
    for part in parts:
        size = part.shape[1]
        cut = whole[:, :, start : start + size]
        found.append(cut.transpose(1, 0, 2).reshape(LAYERS, -1))
        start += size
    return found


def on_device(
    windows, slot_table, cotangent, qkv_weight, qv_bias, proj_weight, proj_bias, norm1_gain,
    norm1_bias, norm2_gain, norm2_bias, fc1_weight, fc1_bias, fc2_weight, fc2_bias, rel_height,
    rel_width,
):
    width = windows.shape[1]
    live = live_rows(slot_table)
    (
        qv_bias_w, proj_bias_w, norm1_gain_w, norm1_bias_w, norm2_gain_w, norm2_bias_w,
        fc1_bias_w, fc2_bias_w, rel_height_w, rel_width_w,
    ) = gather_small((
        qv_bias, proj_bias, norm1_gain, norm1_bias, norm2_gain, norm2_bias, fc1_bias, fc2_bias,
        rel_height, rel_width,
    ))
    vec = jnp.stack(
        [norm1_gain_w, norm1_bias_w, qv_bias_w[:, :width], qv_bias_w[:, width:], proj_bias_w,
         norm2_gain_w, norm2_bias_w, fc2_bias_w], 1
    ).astype(F32)
    hidden_bias = fc1_bias_w.astype(F32)[:, None, :]
    ahead, back = relative_tables(rel_height_w, rel_width_w)
    keys_ahead, keys_back = key_tables()
    current = spread(windows).astype(F32)
    gathered = [
        tuple(
            lax.all_gather(w[layer], "fsdp", axis=0, tiled=True)
            for w in (qkv_weight, proj_weight, fc1_weight, fc2_weight)
        )
        for layer in range(LAYERS)
    ]
    kept = []
    for layer in range(LAYERS):
        qkv, proj, fc1, fc2 = gathered[layer]
        mid, h1, q, k, v, p, att = attend_forward(
            current, live, vec[layer], ahead[layer], keys_ahead, (qkv, proj), whole_attention
        )
        following, h2, act, slope = mlp_forward(
            mid, live, vec[layer], hidden_bias[layer], (fc1, fc2), whole_mlp, (1, 1)
        )
        kept.append((current, mid, h1, q, k, v, p, att, h2, act, slope))
        current = following
    output = gather_back(current).astype(BF16)
    grad = spread(cotangent).astype(F32)
    big = [None] * LAYERS
    small = [None] * LAYERS
    for layer in reversed(range(LAYERS)):
        qkv, proj, fc1, fc2 = gathered[layer]
        x, mid, h1, q, k, v, p, att, h2, act, slope = kept[layer]
        dmid, g1, g2, sums2, hsum = mlp_backward(
            grad, mid, live, vec[layer], h2, act, slope, (fc1, fc2), whole_mlp, (1, 1)
        )
        grad, g, sums1, rel = attend_backward(
            dmid, x, live, vec[layer], back[layer], keys_back, h1, q, k, v, p, att, (qkv, proj),
            whole_attention,
        )
        rel = rel[:, :HD] + rel[:, HD:]
        small[layer] = (
            jnp.concatenate([sums1[1], sums1[2]]), sums1[0], sums1[3], sums1[4], sums2[1],
            sums2[2], hsum[0], sums2[0], rel[:RELS].reshape(-1), rel[HD : HD + RELS].reshape(-1),
        )
        shards = lax.axis_size("fsdp")

        def reduce(value, axis):
            return lax.psum(
                lax.psum_scatter(value, "fsdp", scatter_dimension=axis, tiled=True), "rep"
            ).astype(F32)

        g = reduce(g, 1)
        g1 = reduce(g1, 1)
        big[layer] = (
            jnp.concatenate([g[0], g[1], g[2]], 1), g[3], jnp.concatenate(list(g1), 1),
            reduce(g2, 0),
        )
    shards = lax.axis_size("fsdp")
    packed = jnp.concatenate(
        [
            jnp.stack([small[layer][i] for layer in range(LAYERS)]).reshape(LAYERS, shards, -1)
            for i in range(len(SMALL))
        ],
        2,
    ).astype(BF16)
    mine = lax.psum(
        lax.psum_scatter(packed, "fsdp", scatter_dimension=1, tiled=True), "rep"
    ).astype(F32)[:, 0]
    cuts = np.cumsum([0] + [small[0][i].shape[0] // shards for i in range(len(SMALL))])
    tiny = [mine[:, cuts[i] : cuts[i + 1]] for i in range(len(SMALL))]
    qv, pb, n1g, n1b, n2g, n2b, f1b, f2b, rh, rw = tiny
    stacked = [jnp.stack([big[layer][i] for layer in range(LAYERS)]) for i in range(4)]
    input_grad = gather_back(grad).astype(BF16)
    return (
        output, input_grad, stacked[0], qv, stacked[1], pb, n1g, n1b, n2g, n2b, stacked[2], f1b,
        stacked[3], f2b, rh, rw,
    )


def solution(mesh):
    rows = P(("rep", "fsdp"), None)
    cube = P(None, "fsdp", None)
    flat = P(None, "fsdp")
    return jax.shard_map(
        on_device,
        mesh=mesh,
        in_specs=(
            rows, P(("rep", "fsdp")), rows, cube, flat, cube, flat, flat, flat, flat, flat, cube,
            flat, cube, flat, flat, flat,
        ),
        out_specs=(
            rows, rows, cube, flat, cube, flat, flat, flat, flat, flat, cube, flat, cube, flat,
            flat, flat,
        ),
        check_vma=False,
    )
```

```python
import functools

import jax
import jax.numpy as jnp
import numpy as np
from jax import lax
from jax.experimental import pallas as pl
from jax.experimental.pallas import tpu as pltpu
from jax.sharding import PartitionSpec as P

HEADS = 12
HD = 64
WINDOW = 14
SIDE = 64
LAYERS = 2
GRID = 5
RELS = 2 * WINDOW - 1
EPSILON = 1e-06
PITCH = 16
SPAN = WINDOW * PITCH
PAIRS = HEADS // 2
LANES = 2 * HD
F32 = jnp.float32
BF16 = jnp.bfloat16
CHUNK = 256
ROWS_STEP = 64
VMEM_LIMIT = 56 * 1024 * 1024
SLAB = 384
RIDERS = 8


def dot_nn(a, b):
    return lax.dot_general(a, b, (((1,), (0,)), ((), ())), preferred_element_type=F32)


def dot_nt(a, b):
    return lax.dot_general(a, b, (((1,), (1,)), ((), ())), preferred_element_type=F32)


def dot_tn(a, b):
    return lax.dot_general(a, b, (((0,), (0,)), ((), ())), preferred_element_type=F32)


def norm_rows(values):
    centre = jnp.mean(values, -1, keepdims=True)
    centered = values - centre
    inverse = lax.rsqrt(jnp.mean(centered * centered, -1, keepdims=True) + EPSILON)
    return centered * inverse, inverse


def norm_back(grad, normed, inverse, gain):
    scaled = grad * gain
    return inverse * (
        scaled
        - jnp.mean(scaled, -1, keepdims=True)
        - normed * jnp.mean(scaled * normed, -1, keepdims=True)
    )


def each(count, step, body):
    def run(index, carry):
        body(pl.multiple_of(index * step, step))
        return carry

    lax.fori_loop(0, count, run, 0)


def each_index(count, body):
    def run(index, carry):
        body(index)
        return carry

    lax.fori_loop(0, count, run, 0)


def half_lane():
    return lax.broadcasted_iota(jnp.int32, (SPAN, LANES), 1)


def split_heads(pair):
    lane = half_lane()
    zero = jnp.zeros_like(pair)
    return jnp.concatenate(
        [jnp.where(lane < HD, pair, zero), jnp.where(lane < HD, zero, pair)], axis=0
    )


def join_heads(stacked):
    return jnp.where(half_lane() < HD, stacked[:SPAN], stacked[SPAN:])


def shift_rows(table):
    by_row = jnp.concatenate(
        [
            pltpu.roll(table[i * PITCH : (i + 1) * PITCH], i, axis=1) if i else table[:PITCH]
            for i in range(WINDOW)
        ],
        axis=0,
    )
    by_col = pltpu.roll(
        table.reshape(WINDOW, PITCH, LANES), 0, axis=2, stride=1, stride_axis=1
    ).reshape(SPAN, LANES)
    return jnp.where(half_lane() < HD, by_row, by_col)


def key_tables():
    ahead = np.zeros((SPAN, LANES), np.float32)
    back = np.zeros((SPAN, LANES), np.float32)
    for k in range(WINDOW):
        for m in range(PITCH):
            row = k * PITCH + m
            ahead[row, WINDOW - 1 + k] = 1.0
            back[row, WINDOW - 1 - k] = 1.0
            if m < WINDOW:
                ahead[row, HD + WINDOW - 1 + m] = 1.0
                back[row, HD + WINDOW - 1 - m] = 1.0
            else:
                ahead[row, LANES - 1] = -1e30
    return jnp.asarray(ahead, BF16), jnp.asarray(back, BF16)


def fetch(copies):
    for copy in copies:
        copy.start()


def attend_kernel(source, *refs):
    (x_ref, live_ref, vec_ref, table_ref, keys_ref), refs = refs[:5], refs[5:]
    weight_refs, refs = refs[: source.count], refs[source.count :]
    (mid_ref, h1_ref, q_ref, k_ref, v_ref, p_ref, att_ref), refs = refs[:7], refs[7:]
    token_ref, w_ref, sem = refs
    token_ref[...] = jnp.zeros_like(token_ref)
    ready = source.load("attend", weight_refs, w_ref, sem)
    width = x_ref.shape[1]

    def first_norm(start):
        rows = pl.ds(start, ROWS_STEP)
        normed, _ = norm_rows(x_ref[rows, :].astype(F32))
        shaped = (normed * vec_ref[0:1, :] + vec_ref[1:2, :]) * live_ref[rows, :]
        h1_ref[rows, :] = shaped.astype(BF16)

    each(x_ref.shape[0] // ROWS_STEP, ROWS_STEP, first_norm)
    ready()
    for index, (out_ref, bias) in enumerate(((q_ref, 2), (k_ref, None), (v_ref, 3))):

        def project(start, index=index, out_ref=out_ref, bias=bias):
            cols = pl.ds(start, CHUNK)
            made = dot_nn(h1_ref[...], w_ref[index, :, cols])
            if bias is not None:
                made = made + vec_ref[bias : bias + 1, cols]
            out_ref[:, cols] = made.astype(BF16)

        each(width // CHUNK, CHUNK, project)

    def attend(index):
        rows = pl.ds(pl.multiple_of(index // PAIRS * SPAN, SPAN), SPAN)
        cols = pl.ds(pl.multiple_of(index % PAIRS * LANES, LANES), LANES)
        queries = q_ref[rows, cols]
        offsets = dot_nn(queries, table_ref[...])
        lane = half_lane()
        sides = []
        for half in range(2):
            moved = shift_rows(offsets[:, half * LANES : (half + 1) * LANES])
            sides.append(jnp.where(lane == LANES - 1, 1.0, moved).astype(BF16))
        left = jnp.concatenate(
            [split_heads(queries) * HD ** (-0.5), jnp.concatenate(sides, axis=0)], axis=1
        )
        right = jnp.concatenate([k_ref[rows, cols], keys_ref[...]], axis=1)
        scores = dot_nt(left, right)
        shifted = jnp.exp(scores - jnp.max(scores, -1, keepdims=True))
        probs = shifted * (1.0 / jnp.sum(shifted, -1, keepdims=True))
        low = probs.astype(BF16)
        p_ref[index] = low
        att_ref[rows, cols] = join_heads(dot_nn(low, v_ref[rows, cols])).astype(BF16)

    each_index(x_ref.shape[0] // SPAN * PAIRS, attend)

    def finish(start):
        cols = pl.ds(start, CHUNK)
        branch = dot_nn(att_ref[...], w_ref[3, :, cols]) + vec_ref[4:5, cols]
        mid_ref[:, cols] = x_ref[:, cols].astype(F32) + live_ref[...] * branch

    each(width // CHUNK, CHUNK, finish)


def mlp_kernel(plan, source, top, *refs):
    (mid_ref, live_ref, vec_ref, bias_ref), refs = refs[:4], refs[4:]
    if top:
        (grad_ref,), refs = refs[:1], refs[1:]
    weight_refs, refs = refs[: source.count], refs[source.count :]
    if top:
        (h2_ref, act_ref, slope_ref, sums_ref), refs = refs[:4], refs[4:]
        sink_refs, refs = refs[: plan.sinks], refs[plan.sinks :]
        (w1_ref, dm_ref, sem), refs = refs[:3], refs[3:]
        sink = plan.sink(sink_refs, refs)
    else:
        out_ref, h2_ref, act_ref, slope_ref, token_ref, w1_ref, w2_ref, sem, sem2 = refs
        token_ref[...] = jnp.zeros_like(token_ref)
    ready1 = source.load("fc1", weight_refs, w1_ref, sem)
    if not top:
        ready2 = source.load("fc2", weight_refs, w2_ref, sem2)
    width = mid_ref.shape[1]
    hidden_width = act_ref.shape[1]

    def second_norm(start):
        rows = pl.ds(start, ROWS_STEP)
        normed, _ = norm_rows(mid_ref[rows, :])
        h2_ref[rows, :] = (normed * vec_ref[5:6, :] + vec_ref[6:7, :]).astype(BF16)

    each(mid_ref.shape[0] // ROWS_STEP, ROWS_STEP, second_norm)
    ready1()

    def expand(index):
        start = pl.multiple_of(index * CHUNK, CHUNK)
        cols = pl.ds(start, CHUNK)
        inner = pl.ds(pl.multiple_of(start % width, CHUNK), CHUNK)
        hidden = dot_nn(h2_ref[...], w1_ref[start // width, :, inner]) + bias_ref[:, cols]
        below = 0.5 * (1.0 + lax.erf(hidden * (0.5**0.5)))
        bell = jnp.exp(-0.5 * hidden * hidden) * (0.5 / np.pi) ** 0.5
        act_ref[:, cols] = (hidden * below).astype(BF16)
        slope_ref[:, cols] = (below + hidden * bell).astype(BF16)

    each_index(hidden_width // CHUNK, expand)
    if top:
        sums_ref[...] = jnp.zeros_like(sums_ref)
        second_weight(grad_ref, live_ref, act_ref, dm_ref, sums_ref, sink)
        sink.start()
        sink.wait()
    else:
        ready2()
        contract(act_ref, w2_ref, vec_ref, mid_ref, live_ref, out_ref)


def contract(act_ref, w2_ref, vec_ref, mid_ref, live_ref, out_ref):
    def run(start):
        cols = pl.ds(start, CHUNK)
        made = dot_nn(act_ref[...], w2_ref[:, cols]) + vec_ref[7:8, cols]
        out_ref[:, cols] = mid_ref[:, cols] + live_ref[...] * made

    each(out_ref.shape[1] // CHUNK, CHUNK, run)


def out_kernel(source, act_ref, vec_ref, mid_ref, live_ref, *refs):
    weight_refs, (out_ref, w2_ref, sem) = refs[: source.count], refs[source.count :]
    source.load("fc2", weight_refs, w2_ref, sem)()
    contract(act_ref, w2_ref, vec_ref, mid_ref, live_ref, out_ref)


def second_weight(grad_ref, live_ref, act_ref, dm_ref, sums_ref, sink):
    dm_ref[...] = (live_ref[...] * grad_ref[...].astype(F32)).astype(BF16)
    sums_ref[0:1, :] = jnp.sum(dm_ref[...].astype(F32), 0, keepdims=True)

    def run(index):
        rows = pl.ds(pl.multiple_of(index * SLAB, SLAB), SLAB)
        sink.rows(index, dot_tn(act_ref[:, rows], dm_ref[...]).astype(BF16))

    each_index(act_ref.shape[1] // SLAB, run)


def hidden_back_kernel(plan, source, top, *refs):
    (grad_ref, live_ref, h2_ref, act_ref, slope_ref), refs = refs[:5], refs[5:]
    weight_refs, refs = refs[: source.count], refs[source.count :]
    (dh_ref, sums_ref, hsum_ref), refs = refs[:3], refs[3:]
    sink_refs, refs = refs[: plan.sinks], refs[plan.sinks :]
    if not top:
        more_refs, refs = refs[: plan.sinks], refs[plan.sinks :]
    (w2_ref, dm_ref, sem), refs = refs[:3], refs[3:]
    sink = plan.sink(sink_refs, refs)
    if not top:
        more = plan.sink(more_refs, refs[plan.sink_scratch :])
    ready = source.load("fc2", weight_refs, w2_ref, sem)
    width = h2_ref.shape[1]
    hidden_width = act_ref.shape[1]
    sums_ref[...] = jnp.zeros_like(sums_ref)
    if top:
        dm_ref[...] = (live_ref[...] * grad_ref[...].astype(F32)).astype(BF16)
    else:
        second_weight(grad_ref, live_ref, act_ref, dm_ref, sums_ref, more)
        more.start()
    ready()

    def inner_grad(start):
        cols = pl.ds(start, CHUNK)
        made = (dot_nt(dm_ref[...], w2_ref[cols, :]) * slope_ref[:, cols].astype(F32)).astype(BF16)
        dh_ref[:, cols] = made
        hsum_ref[:, cols] = jnp.sum(made.astype(F32), 0, keepdims=True)

    each(hidden_width // CHUNK, CHUNK, inner_grad)

    def first_weight(index):
        start = pl.multiple_of(index * CHUNK, CHUNK)
        inner = pl.ds(pl.multiple_of(start % width, CHUNK), CHUNK)
        sink.cols(
            start // width, inner, dot_tn(h2_ref[...], dh_ref[:, pl.ds(start, CHUNK)]).astype(BF16)
        )

    each_index(hidden_width // CHUNK, first_weight)
    sink.start()
    if not top:
        more.wait()
    sink.wait()


def middle_back_kernel(source, *refs):
    (grad_ref, mid_ref, vec_ref, dh_ref), refs = refs[:4], refs[4:]
    weight_refs, refs = refs[: source.count], refs[source.count :]
    dmid_ref, sums_ref, w1_ref, ds_ref, sem = refs
    source.load("fc1", weight_refs, w1_ref, sem)()
    width = mid_ref.shape[1]
    hidden_width = dh_ref.shape[1]

    def back_in(start):
        rows = pl.ds(start, CHUNK)
        made = dot_nt(dh_ref[:, 0:width], w1_ref[0, rows, :])
        for block in range(1, hidden_width // width):
            made += dot_nt(
                dh_ref[:, block * width : (block + 1) * width], w1_ref[block, rows, :]
            )
        ds_ref[:, rows] = made

    each(width // CHUNK, CHUNK, back_in)
    sums_ref[...] = jnp.zeros_like(sums_ref)

    def back_norm(start):
        rows = pl.ds(start, ROWS_STEP)
        normed, inverse = norm_rows(mid_ref[rows, :])
        grad = ds_ref[rows, :]
        sums_ref[1:2, :] += jnp.sum(grad * normed, 0, keepdims=True)
        sums_ref[2:3, :] += jnp.sum(grad, 0, keepdims=True)
        dmid_ref[rows, :] = grad_ref[rows, :].astype(F32) + norm_back(
            grad, normed, inverse, vec_ref[5:6, :]
        )

    each(mid_ref.shape[0] // ROWS_STEP, ROWS_STEP, back_norm)


def scores_back_kernel(source, *refs):
    (
        dmid_ref, live_ref, table_ref, keys_ref, q_ref, k_ref, v_ref, p_ref,
    ), refs = refs[:8], refs[8:]
    weight_refs, refs = refs[: source.count], refs[source.count :]
    db_ref, dq_ref, dk_ref, dv_ref, sums_ref, rel_ref, w_ref, da_ref, sem = refs
    ready = source.load("attend", weight_refs, w_ref, sem)
    width = dmid_ref.shape[1]
    db_ref[...] = (live_ref[...] * dmid_ref[...]).astype(BF16)
    sums_ref[...] = jnp.zeros_like(sums_ref)
    sums_ref[0:1, :] = jnp.sum(db_ref[...].astype(F32), 0, keepdims=True)
    rel_ref[...] = jnp.zeros_like(rel_ref)
    ready()

    def back_out(start):
        rows = pl.ds(start, CHUNK)
        da_ref[:, rows] = dot_nt(db_ref[...], w_ref[3, rows, :]).astype(BF16)

    each(width // CHUNK, CHUNK, back_out)

    def attend(index):
        rows = pl.ds(pl.multiple_of(index // PAIRS * SPAN, SPAN), SPAN)
        cols = pl.ds(pl.multiple_of(index % PAIRS * LANES, LANES), LANES)
        low = p_ref[index]
        probs = low.astype(F32)
        outer = split_heads(da_ref[rows, cols])
        queries = split_heads(q_ref[rows, cols])
        d_probs = dot_nt(outer, v_ref[rows, cols])
        dv_ref[rows, cols] = dot_tn(low, outer).astype(BF16)
        mean = jnp.sum(d_probs * probs, -1, keepdims=True)
        d_scores = (probs * (d_probs - mean)).astype(BF16)
        both = dot_nn(d_scores, jnp.concatenate([k_ref[rows, cols], keys_ref[...]], axis=1))
        moved = [
            shift_rows(both[half * SPAN : (half + 1) * SPAN, LANES:]).astype(BF16)
            for half in range(2)
        ]
        rel_part = dot_nt(jnp.concatenate(moved, axis=1), table_ref[...])
        direct = join_heads(both[:, :LANES]) * HD ** (-0.5)
        dq_ref[rows, cols] = (direct + rel_part).astype(BF16)
        dk_ref[rows, cols] = (dot_tn(d_scores, queries) * HD ** (-0.5)).astype(BF16)
        rel_ref[...] += dot_tn(jnp.concatenate(moved, axis=0), queries)

    each_index(dmid_ref.shape[0] // SPAN * PAIRS, attend)
    sums_ref[1:2, :] = jnp.sum(dq_ref[...].astype(F32), 0, keepdims=True)
    sums_ref[2:3, :] = jnp.sum(dv_ref[...].astype(F32), 0, keepdims=True)


def first_weights_kernel(plan, rotated, *refs):
    (h1_ref, att_ref, db_ref, dq_ref, dk_ref, dv_ref), refs = refs[:6], refs[6:]
    sink = plan.sink(refs[: plan.sinks], refs[plan.sinks :], rotated)
    pairs = ((h1_ref, dq_ref), (h1_ref, dk_ref), (h1_ref, dv_ref), (att_ref, db_ref))
    for index, (left_ref, right_ref) in enumerate(pairs):

        def weight(start, index=index, left_ref=left_ref, right_ref=right_ref):
            cols = pl.ds(start, CHUNK)
            sink.cols(index, cols, dot_tn(left_ref[...], right_ref[:, cols]).astype(BF16))

        each(h1_ref.shape[1] // CHUNK, CHUNK, weight)
    sink.start()
    sink.wait()


def first_back_kernel(source, *refs):
    (dmid_ref, x_ref, live_ref, vec_ref, dq_ref, dk_ref, dv_ref), refs = refs[:7], refs[7:]
    weight_refs, refs = refs[: source.count], refs[source.count :]
    next_ref, sums_ref, w_ref, dh_ref, sem = refs
    source.load("attend", weight_refs, w_ref, sem)()
    width = x_ref.shape[1]

    def back_in(start):
        rows = pl.ds(start, CHUNK)
        made = dot_nt(dq_ref[...], w_ref[0, rows, :])
        made += dot_nt(dk_ref[...], w_ref[1, rows, :])
        made += dot_nt(dv_ref[...], w_ref[2, rows, :])
        dh_ref[:, rows] = made * live_ref[...]

    each(width // CHUNK, CHUNK, back_in)
    sums_ref[...] = jnp.zeros_like(sums_ref)

    def back_norm(start):
        rows = pl.ds(start, ROWS_STEP)
        normed, inverse = norm_rows(x_ref[rows, :].astype(F32))
        grad = dh_ref[rows, :]
        sums_ref[3:4, :] += jnp.sum(grad * normed, 0, keepdims=True)
        sums_ref[4:5, :] += jnp.sum(grad, 0, keepdims=True)
        next_ref[rows, :] = dmid_ref[rows, :] + norm_back(grad, normed, inverse, vec_ref[0:1, :])

    each(x_ref.shape[0] // ROWS_STEP, ROWS_STEP, back_norm)


VM = pl.BlockSpec(memory_space=pltpu.VMEM)
ANY = pl.BlockSpec(memory_space=pl.ANY)


def shape(dims, kind):
    return jax.ShapeDtypeStruct(tuple(dims), kind)


class Source:
    def __init__(self, **parts):
        self.parts = parts
        self.arrays = []
        self.places = {}
        for name, (arrays, _, _) in parts.items():
            found = []
            for array in arrays:
                known = [i for i, other in enumerate(self.arrays) if other is array]
                if not known:
                    known = [len(self.arrays)]
                    self.arrays.append(array)
                found.append(known[0])
            self.places[name] = found
        self.count = len(self.arrays)

    def semaphores(self, name):
        whole = self.parts[name][1] is None
        return pltpu.SemaphoreType.DMA((4 if whole else 32,))

    def load(self, name, refs, target, sem):
        arrays, block, rotated = self.parts[name]
        refs = [refs[i] for i in self.places[name]]
        if block is None:
            pairs = whole_pairs(name, refs, target)
        else:
            pairs = piece_pairs(name, refs, target, block, rotated)
        copies = [
            pltpu.make_async_copy(given, taken, sem.at[i])
            for i, (given, taken) in enumerate(pairs)
        ]
        for copy in copies:
            copy.start()

        def ready():
            for copy in copies:
                copy.wait()

        return ready


def whole_pairs(name, refs, target):
    if name == "fc2":
        return [(refs[0], target)]
    width = target.shape[1]
    pairs = []
    for ref in refs:
        for start in range(0, ref.shape[1], width):
            pairs.append((ref.at[:, pl.ds(start, width)], target.at[len(pairs)]))
    return pairs


def position():
    shard = lax.axis_index("fsdp")
    return lax.axis_index("rep"), shard >> 1, shard & 1


def piece_pairs(name, refs, target, block, rotated):
    rep, level, core = position()
    pairs = []
    for parity in range(2):
        for part, (away, levels) in enumerate(
            ((0, range(4)), (1, range(4)), (2, range(4)), (3, range(2)), (3, range(2, 4)))
        ):
            ref = refs[parity * 5 + part]
            for place, step in enumerate(levels):
                source_level = (level - step) & 3 if rotated else step
                shard = source_level * 2 + (core ^ parity)
                kind = rep ^ away
                rows = target.shape[-2] // 8
                if name == "fc2":
                    span = rows // 4
                    start = shard * rows + kind * span
                    taken = target.at[pl.ds(pl.multiple_of(start, 16), span), :]
                else:
                    span = rows
                    start = pl.multiple_of(shard * span, 16)
                    taken = target.at[kind, pl.ds(start, span), :]
                pairs.append((ref.at[place, block, pl.ds(0, span), :], taken))
    return pairs


class WholeSink:
    def __init__(self, refs):
        self.ref = refs[0]

    def rows(self, index, value):
        self.ref[pl.ds(pl.multiple_of(index * SLAB, SLAB), SLAB), :] = value

    def cols(self, block, cols, value):
        self.ref[block, :, cols] = value

    def start(self):
        pass

    def wait(self):
        pass


class PieceSink:
    def __init__(self, refs, scratch, rotated):
        self.held, sem = scratch[:2]
        rep, level, core = position()
        self.copies = []
        for parity in range(2):
            for away in range(4):
                given = self.held.at[core ^ parity, rep ^ away]
                taken = refs[parity].at[away]
                moves = [(given, taken)]
                if rotated:
                    moves = [(given.at[(level + step) & 3], taken.at[step]) for step in range(4)]
                for move in moves:
                    self.copies.append(pltpu.make_async_copy(*move, sem.at[len(self.copies)]))

    def rows(self, index, value):
        span = self.held.shape[3]
        for block in range(4):
            self.held[index & 1, block, index >> 1] = value[block * span : (block + 1) * span]

    def cols(self, block, cols, value):
        span = self.held.shape[3]
        for shard in range(8):
            self.held[shard & 1, block, shard >> 1, :, cols] = value[
                shard * span : (shard + 1) * span
            ]

    def start(self):
        for copy in self.copies:
            copy.start()

    def wait(self):
        for copy in self.copies:
            copy.wait()


class WholePlan:
    sinks = 1
    sink_scratch = 0

    def sink(self, refs, scratch, rotated=False):
        return WholeSink(refs)

    def sink_outs(self, dims):
        return [shape(dims, BF16)], [VM], []


class PiecePlan:
    sinks = 2
    sink_scratch = 2

    def sink(self, refs, scratch, rotated=False):
        return PieceSink(refs, scratch, rotated)

    def sink_outs(self, dims):
        width = dims[-1]
        span = int(np.prod(dims)) // width // 32
        outs = [shape((4, 4, span, width), BF16)] * 2
        scratch = [pltpu.VMEM((2, 4, 4, span, width), BF16), pltpu.SemaphoreType.DMA((32,))]
        return outs, [ANY] * 2, scratch


def call(kernel, resident, source, outs, scratch, micros, sinks=(), after=()):
    specs = [VM] * len(outs)
    outs = list(outs)
    scratch = list(scratch)
    for more_outs, more_specs, more_scratch in sinks:
        outs += more_outs
        specs += more_specs
        scratch += more_scratch
    first = len(resident) + source.count

    def body(*refs):
        kernel(*refs[:first], *refs[first + len(after) :])

    return pl.pallas_call(
        body,
        out_shape=tuple(outs),
        in_specs=[VM] * len(resident) + [ANY] * (source.count + len(after)),
        out_specs=tuple(specs),
        scratch_shapes=scratch,
        compiler_params=pltpu.CompilerParams(vmem_limit_bytes=VMEM_LIMIT),
        cost_estimate=pl.CostEstimate(
            flops=int(micros * 1e9), bytes_accessed=1 << 20, transcendentals=0
        ),
    )(*resident, *source.arrays, *after)


def attend_forward(x, live, vec, table, keys, source, after):
    rows, width = x.shape
    outs = (
        shape((rows, width), F32),
        *[shape((rows, width), BF16)] * 4,
        shape((rows // SPAN * PAIRS, 2 * SPAN, SPAN), BF16),
        shape((rows, width), BF16),
        shape((8, LANES), F32),
    )
    scratch = [pltpu.VMEM((4, width, width), BF16), source.semaphores("attend")]
    return call(
        functools.partial(attend_kernel, source),
        (x, live, vec, table, keys), source, outs, scratch, 20, (), after,
    )


def mlp_forward(plan, top, mid, live, vec, bias, grad, source, after):
    rows, width = mid.shape
    hidden = bias.shape[1]
    outs = [
        shape((rows, width), BF16), shape((rows, hidden), BF16), shape((rows, hidden), BF16),
    ]
    scratch = [pltpu.VMEM((hidden // width, width, width), BF16)]
    resident = [mid, live, vec, bias]
    sinks = []
    if top:
        resident.append(grad)
        outs.append(shape((8, width), F32))
        scratch += [pltpu.VMEM((rows, width), BF16), source.semaphores("fc1")]
        sinks.append(plan.sink_outs((hidden, width)))
    else:
        outs.insert(0, shape((rows, width), F32))
        outs.append(shape((8, LANES), F32))
        scratch += [
            pltpu.VMEM((hidden, width), BF16), source.semaphores("fc1"),
            source.semaphores("fc2"),
        ]
    return call(
        functools.partial(mlp_kernel, plan, source, top),
        resident, source, outs, scratch, 16, sinks, after,
    )


def mlp_output(act, vec, mid, live, source, after):
    hidden, width = act.shape[1], mid.shape[1]
    scratch = [pltpu.VMEM((hidden, width), BF16), source.semaphores("fc2")]
    return call(
        functools.partial(out_kernel, source), (act, vec, mid, live), source,
        [shape(mid.shape, F32)], scratch, 5, (), after,
    )[0]


def hidden_backward(plan, top, grad, live, h2, act, slope, source, after):
    rows, width = h2.shape
    hidden = act.shape[1]
    outs = [shape((rows, hidden), BF16), shape((8, width), F32), shape((1, hidden), F32)]
    sinks = [plan.sink_outs((hidden // width, width, width))]
    if not top:
        sinks.append(plan.sink_outs((hidden, width)))
    scratch = [
        pltpu.VMEM((hidden, width), BF16), pltpu.VMEM((rows, width), BF16),
        source.semaphores("fc2"),
    ]
    return call(
        functools.partial(hidden_back_kernel, plan, source, top),
        (grad, live, h2, act, slope), source, outs, scratch, 15, sinks, after,
    )


def middle_backward(grad, mid, vec, dh, source, after):
    rows, width = mid.shape
    hidden = dh.shape[1]
    outs = [shape((rows, width), F32), shape((8, width), F32)]
    scratch = [
        pltpu.VMEM((hidden // width, width, width), BF16), pltpu.VMEM((rows, width), F32),
        source.semaphores("fc1"),
    ]
    return call(
        functools.partial(middle_back_kernel, source),
        (grad, mid, vec, dh), source, outs, scratch, 10, (), after,
    )


def scores_backward(dmid, live, table, keys, q, k, v, p, source, after):
    rows, width = dmid.shape
    outs = [*[shape((rows, width), BF16)] * 4, shape((8, width), F32), shape((LANES, LANES), F32)]
    scratch = [
        pltpu.VMEM((4, width, width), BF16), pltpu.VMEM((rows, width), BF16),
        source.semaphores("attend"),
    ]
    return call(
        functools.partial(scores_back_kernel, source),
        (dmid, live, table, keys, q, k, v, p), source, outs, scratch, 15, (), after,
    )


def first_weights(plan, rotated, h1, att, db, dq, dk, dv, after):
    width = h1.shape[1]
    return call(
        functools.partial(first_weights_kernel, plan, rotated), (h1, att, db, dq, dk, dv),
        Source(), [], [], 8, [plan.sink_outs((4, width, width))], after,
    )


def first_backward(dmid, x, live, vec, dq, dk, dv, source, after):
    rows, width = x.shape
    outs = [shape((rows, width), F32), shape((8, width), F32)]
    scratch = [
        pltpu.VMEM((4, width, width), BF16), pltpu.VMEM((rows, width), F32),
        source.semaphores("attend"),
    ]
    return call(
        functools.partial(first_back_kernel, source),
        (dmid, x, live, vec, dq, dk, dv), source, outs, scratch, 8, (), after,
    )


def live_rows(slot_table):
    places = jnp.arange(PITCH, dtype=jnp.int32)
    rows_inside = slot_table[:, None] // GRID * WINDOW + places[None, :WINDOW] < SIDE
    cols_inside = slot_table[:, None] % GRID * WINDOW + places[None, :] < SIDE
    cols_inside = cols_inside & (places < WINDOW)[None, :]
    both_inside = rows_inside[:, :, None] & cols_inside[:, None, :]
    return both_inside.astype(F32).reshape(slot_table.shape[0] * SPAN, 1)


def spread(values):
    width = values.shape[1]
    grid = values.reshape(-1, WINDOW, width)
    return jnp.pad(grid, ((0, 0), (0, PITCH - WINDOW), (0, 0))).reshape(-1, width)


def gather_back(values):
    width = values.shape[1]
    return values.reshape(-1, PITCH, width)[:, :WINDOW].reshape(-1, width)


def relative_tables(rel_height, rel_width):
    stacked = jnp.stack([rel_height, rel_width], 1).reshape(LAYERS, 2, RELS, HD)

    def spread_table(rows):
        padded = jnp.pad(rows, ((0, 0), (0, 0), (0, HD - RELS), (0, 0)))
        one = padded.reshape(LAYERS, LANES, HD).transpose(0, 2, 1)
        none = jnp.zeros_like(one)
        return jnp.concatenate(
            [jnp.concatenate([one, none], 2), jnp.concatenate([none, one], 2)], 1
        )

    return spread_table(stacked[:, :, ::-1]), spread_table(stacked)


def whole_weights(weights):
    qkv, proj, fc1, fc2 = weights
    layers = []
    for layer in range(LAYERS):
        q, p, a, b = (
            lax.all_gather(w[layer], "fsdp", axis=0, tiled=True) for w in (qkv, proj, fc1, fc2)
        )
        layers.append(
            dict(attend=((q, p), None, False), fc1=((a,), None, False), fc2=((b,), None, False))
        )
    return layers


def whole_small(parts):
    packed = jnp.concatenate(parts, axis=1)
    return lax.all_gather(packed, "fsdp", axis=0, tiled=False)


def whole_reduce(value, axis):
    return lax.psum(
        lax.psum_scatter(value, "fsdp", scatter_dimension=axis, tiled=True), "rep"
    ).astype(F32)


def whole_sums(grads, small):
    big = []
    for (g,), (g1,), (g2,) in grads:
        g, g1, g2 = whole_reduce(g, 1), whole_reduce(g1, 1), whole_reduce(g2, 0)
        big.append(
            (jnp.concatenate([g[0], g[1], g[2]], 1), g[3], jnp.concatenate(list(g1), 1), g2)
        )
    mine = whole_reduce(small.astype(BF16), 1)[:, 0]
    return big, mine


def permute(value, axis, move):
    return lax.ppermute(value, axis, [(i, move(i)) for i in range({"rep": 4, "fsdp": 8}[axis])])


def to_x(value):
    return permute(value, "rep", lambda i: i ^ 1)


def to_y(value):
    return permute(value, "rep", lambda i: i ^ 2)


def to_xy(value):
    return permute(value, "rep", lambda i: i ^ 3)


def to_core(value):
    return permute(value, "fsdp", lambda i: i ^ 1)


def to_level(value, step):
    return permute(value, "fsdp", lambda i: (i + 2 * step) % 8)


LEVELS = [[0, 2, 4, 6], [1, 3, 5, 7]]


def swap(value, flag, axis):
    first = lax.slice_in_dim(value, 0, 1, axis=axis)
    second = lax.slice_in_dim(value, 1, 2, axis=axis)
    return jnp.where(flag == 1, jnp.concatenate([second, first], axis), value)


def by_replica(value, rep):
    rest = value.shape[1:]
    value = value.reshape(2, 2, *rest)
    value = swap(swap(value, rep & 1, 1), rep >> 1, 0)
    return value.reshape(4, *rest)


def turn(value, start, axis):
    size = value.shape[axis]
    return lax.dynamic_slice_in_dim(
        jnp.concatenate([value, value], axis), start, size, axis
    )


def own_blocks(weights, layer, rep):
    qkv, proj, fc1, fc2 = (w[layer] for w in weights)
    width = proj.shape[1]
    span = proj.shape[0]
    first = lax.dynamic_slice_in_dim(jnp.concatenate([qkv, proj], 1), rep * width, width, 1)
    second = lax.dynamic_slice_in_dim(fc1, rep * width, width, 1)
    third = lax.dynamic_slice_in_dim(fc2, rep * span, span, 0)
    return first, second, third


class Across:
    def __init__(self, held):
        self.held = held
        self.x, self.y = to_x(held), to_y(held)

    def finish(self, token=None):
        low, high = self.y[:2], self.x[2:]
        if token is not None:
            low, high = low + token, high + token
        pieces = (self.held, self.x, self.y, to_x(low), to_y(high))
        return pieces + tuple(to_core(piece) for piece in pieces)


class PieceWeights:
    def __init__(self, weights, small):
        rep, level, core = position()
        blocks = [own_blocks(weights, layer, rep) for layer in range(LAYERS)]
        self.width = blocks[0][0].shape[1]
        self.size = small.shape[0] // 4
        rider = lax.dynamic_slice_in_dim(small, rep * self.size, self.size, 0)
        rider = jnp.pad(rider, (0, RIDERS * self.width - self.size)).reshape(RIDERS, self.width)
        first = jnp.concatenate([blocks[0][0], rider], 0)[None, None]
        held = jnp.concatenate([first] + [to_level(first, step) for step in (1, 2, 3)], 0)
        self.rest0 = self.levels(blocks[0][1:])
        self.rest1 = self.levels(blocks[1][:2])
        self.last = lax.all_gather(weights[3][1], "fsdp", axis=0, tiled=True)
        self.group_a = Across(held).finish()
        self.next_b = Across(self.rest0)
        span = blocks[0][0].shape[0]
        riders = jnp.stack(
            [
                jnp.concatenate(
                    [t[:, 0, span:] for t in self.group_a[5 * p : 5 * p + 5]], 0
                ).reshape(4, 4, RIDERS * self.width)[:, :, : self.size]
                for p in range(2)
            ]
        )
        riders = by_replica(swap(riders, core, 0).transpose(1, 0, 2, 3), rep)
        turned = jnp.concatenate([riders[:, :, i : i + 1] for i in (3, 2, 1, 0)], 2)
        riders = turn(turned, 3 - level, 2)
        self.small = riders.transpose(2, 1, 0, 3).reshape(8, LAYERS, -1)

    def levels(self, parts):
        span, width = parts[0].shape
        joined = lax.all_gather(
            jnp.concatenate(parts, 0), "fsdp", axis=0, tiled=True, axis_index_groups=LEVELS
        )
        return joined.reshape(4, len(parts), span, width)

    def before(self, name):
        if name == "attend_0":
            return (self.rest0,)
        if name == "mlp_0":
            return (self.next_c.held,)
        return ()

    def passed(self, name, token):
        if name == "attend_0":
            token = token[0, 0].astype(BF16)
            self.group_b = self.next_b.finish(token)
            self.next_c = Across(self.rest1 + token)
        if name == "mlp_0":
            self.group_c = self.next_c.finish(token[0, 0].astype(BF16))

    def source(self, layer, *names):
        if layer == 0:
            parts = dict(
                attend=lambda: (self.group_a, 0, True),
                fc1=lambda: (self.group_b, 0, False),
                fc2=lambda: (self.group_b, 1, False),
            )
        else:
            parts = dict(
                attend=lambda: (self.group_c, 0, False),
                fc1=lambda: (self.group_c, 1, False),
                fc2=lambda: ((self.last,), None, False),
            )
        return Source(**{name: parts[name]() for name in names})


class WholeWeights:
    def __init__(self, weights, small):
        self.small = whole_small(small)
        self.layers = whole_weights(weights)

    def before(self, name):
        return ()

    def passed(self, name, token):
        pass

    def source(self, layer, *names):
        return Source(**{name: self.layers[layer][name] for name in names})


class ReplicaSum:
    def __init__(self, pair):
        self.keep, send = pair
        self.got = to_core(send)
        self.step = 0

    def both(self, away, part):
        return self.keep[away, part].astype(F32) + self.got[away, part].astype(F32)

    def advance(self):
        low, high = slice(0, 2), slice(2, 4)
        self.step += 1
        if self.step == 1:
            send_x = jnp.stack([self.both(1, low), self.both(3, low)]).astype(BF16)
            send_y = jnp.stack([self.both(2, high), self.both(3, high)]).astype(BF16)
            self.x, self.y = to_x(send_x), to_y(send_y)
            return [send_x, send_y]
        if self.step == 2:
            send_y = (self.both(2, low) + self.x[1].astype(F32)).astype(BF16)
            send_x = (self.both(1, high) + self.y[1].astype(F32)).astype(BF16)
            self.last_y, self.last_x = to_y(send_y), to_x(send_x)
            return [send_x, send_y]
        self.result = jnp.concatenate(
            [
                self.both(0, low) + self.x[0].astype(F32) + self.last_y.astype(F32),
                self.both(0, high) + self.y[0].astype(F32) + self.last_x.astype(F32),
            ],
            0,
        ).astype(BF16)
        return [self.result]


def sum_levels(parts):
    joined = jnp.stack(parts, 1)
    _, count, span, width = joined.shape
    mine = lax.psum_scatter(
        joined.reshape(-1, width), "fsdp", scatter_dimension=0, tiled=True,
        axis_index_groups=LEVELS,
    )
    return lax.all_gather(mine, "rep", axis=0, tiled=True).reshape(4, count, span, width)


def ride_along(small, width, rep, level, core):
    size = small.shape[0] * small.shape[2] // 4
    flat = small.transpose(1, 0, 2).reshape(4, 2, 4, size)
    flat = jnp.pad(flat, ((0, 0), (0, 0), (0, 0), (0, RIDERS * width - size)))
    flat = turn(flat, level, 0).transpose(1, 2, 0, 3)
    flat = swap(flat, core, 0).transpose(1, 0, 2, 3)
    flat = by_replica(flat, rep).transpose(1, 0, 2, 3)
    return flat.reshape(2, 4, 4, RIDERS, width).astype(BF16)


class PieceSums:
    def __init__(self):
        self.open = []
        self.sums = {}
        self.top = None

    def add(self, name, pair):
        self.sums[name] = ReplicaSum(pair)

    def sum_top(self):
        self.top = sum_levels([self.sums[f"{n}_1"].result for n in ("fc2", "fc1", "attend")])

    def advance(self, *names):
        found = []
        for name in names:
            found += self.sums[name].advance()
        return found

    def finish(self, pair, small):
        rep, level, core = position()
        span, width = pair[0].shape[2:]
        riders = ride_along(small, width, rep, level, core)
        keep, send = pair
        self.add(
            "last",
            (jnp.concatenate([keep, riders[0]], 2), jnp.concatenate([send, riders[1]], 2)),
        )
        rest = sum_levels([self.sums[f"{n}_0"].result for n in ("fc2", "fc1")])
        self.advance("last")
        self.advance("last")
        self.advance("last")
        mine = self.sums["last"].result
        total = mine[0].astype(F32)
        for step in (1, 2, 3):
            total = total + to_level(mine[step], step).astype(F32)
        total = total.astype(BF16)
        last = jnp.stack([total, to_x(total), to_y(total), to_xy(total)])
        last = by_replica(last, rep).astype(F32)

        def named(first, second, third):
            first, second, third = (t.astype(F32) for t in (first, second, third))
            return (
                jnp.concatenate([first[0], first[1], first[2]], 1),
                first[3],
                jnp.concatenate(list(second), 1),
                third.reshape(-1, width),
            )

        size = small.shape[0] * small.shape[2] // 4
        tiny = last[:, span:].reshape(4, -1)[:, :size].reshape(LAYERS, -1)
        top = self.top
        return [
            named(last[:, :span], rest[:, 1], rest[:, 0]),
            named(top[:, 2], top[:, 1], top[:, 0]),
        ], tiny


class WholeSums:
    def __init__(self):
        self.pairs = {}

    def add(self, name, pair):
        self.pairs[name] = pair

    def advance(self, *names):
        return ()

    def sum_top(self):
        pass

    def finish(self, pair, small):
        grads = [
            (pair, self.pairs["fc1_0"], self.pairs["fc2_0"]),
            tuple(self.pairs[f"{name}_1"] for name in ("attend", "fc1", "fc2")),
        ]
        return whole_sums(grads, small)


def on_device(
    ring, windows, slot_table, cotangent, qkv_weight, qv_bias, proj_weight, proj_bias,
    norm1_gain, norm1_bias, norm2_gain, norm2_bias, fc1_weight, fc1_bias, fc2_weight, fc2_bias,
    rel_height, rel_width,
):
    width = windows.shape[1]
    weights = (qkv_weight, proj_weight, fc1_weight, fc2_weight)
    parts = (
        qv_bias, proj_bias, norm1_gain, norm1_bias, norm2_gain, norm2_bias, fc1_bias, fc2_bias,
        rel_height, rel_width,
    )
    cuts = np.cumsum([0] + [part.shape[1] for part in parts])
    if ring:
        plan, pending = PiecePlan(), PieceSums()
        held = PieceWeights(weights, jnp.concatenate(parts, 1).reshape(-1))
    else:
        plan, pending = WholePlan(), WholeSums()
        held = WholeWeights(weights, parts)
    small = held.small
    (
        qv_bias_w, proj_bias_w, norm1_gain_w, norm1_bias_w, norm2_gain_w, norm2_bias_w,
        fc1_bias_w, fc2_bias_w, rel_height_w, rel_width_w,
    ) = [
        small[:, :, a:b].transpose(1, 0, 2).reshape(LAYERS, -1) for a, b in zip(cuts, cuts[1:])
    ]
    vec = jnp.stack(
        [norm1_gain_w, norm1_bias_w, qv_bias_w[:, :width], qv_bias_w[:, width:], proj_bias_w,
         norm2_gain_w, norm2_bias_w, fc2_bias_w], 1
    ).astype(F32)
    hidden_bias = fc1_bias_w.astype(F32)[:, None, :]
    ahead, back = relative_tables(rel_height_w, rel_width_w)
    keys_ahead, keys_back = key_tables()
    live = live_rows(slot_table)
    current = spread(windows)
    grad = spread(cotangent)
    kept = []
    for layer in range(LAYERS):
        top = layer == LAYERS - 1
        mid, h1, q, k, v, p, att, token = attend_forward(
            current, live, vec[layer], ahead[layer], keys_ahead, held.source(layer, "attend"),
            held.before(f"attend_{layer}"),
        )
        held.passed(f"attend_{layer}", token)
        used = ("fc1",) if top else ("fc1", "fc2")
        made = mlp_forward(
            plan, top, mid, live, vec[layer], hidden_bias[layer], grad,
            held.source(layer, *used), held.before(f"mlp_{layer}"),
        )
        if top:
            h2, act, slope, top_sums = made[:4]
            pending.add("fc2_1", made[4:])
        else:
            following, h2, act, slope, token = made
            held.passed(f"mlp_{layer}", token)
        kept.append((current, mid, h1, q, k, v, p, att, h2, act, slope))
        current = following
    sums = [None] * LAYERS
    steps = {
        "hidden_1": (),
        "middle_1": ("fc2_1",),
        "scores_1": ("fc2_1", "fc1_1"),
        "weights_1": ("fc2_1", "fc1_1"),
        "first_1": ("fc1_1",),
        "hidden_0": ("attend_1",),
        "middle_0": ("attend_1",),
        "scores_0": ("attend_1", "fc2_0", "fc1_0"),
        "weights_0": ("fc2_0", "fc1_0"),
        "first_0": ("fc2_0", "fc1_0"),
    }
    for layer in reversed(range(LAYERS)):
        top = layer == LAYERS - 1
        x, mid, h1, q, k, v, p, att, h2, act, slope = kept[layer]
        made = hidden_backward(
            plan, top, grad, live, h2, act, slope, held.source(layer, "fc2"),
            pending.advance(*steps[f"hidden_{layer}"]),
        )
        dh, sums3, hsum = made[:3]
        pending.add(f"fc1_{layer}", made[3 : 3 + plan.sinks])
        if top:
            sums3 = top_sums
        else:
            pending.add("fc2_0", made[3 + plan.sinks :])
        dmid, sums2 = middle_backward(
            grad, mid, vec[layer], dh, held.source(layer, "fc1"),
            pending.advance(*steps[f"middle_{layer}"]),
        )
        db, dq, dk, dv, sums1, rel = scores_backward(
            dmid, live, back[layer], keys_back, q, k, v, p, held.source(layer, "attend"),
            pending.advance(*steps[f"scores_{layer}"]),
        )
        pair = first_weights(
            plan, ring and layer == 0, h1, att, db, dq, dk, dv,
            pending.advance(*steps[f"weights_{layer}"]),
        )
        if top:
            pending.add("attend_1", pair)
        grad, sums4 = first_backward(
            dmid, x, live, vec[layer], dq, dk, dv, held.source(layer, "attend"),
            pending.advance(*steps[f"first_{layer}"]),
        )
        if not top:
            pending.sum_top()
        rel = rel[:, :HD] + rel[:, HD:]
        sums[layer] = (
            jnp.concatenate([sums1[1], sums1[2]]), sums1[0], sums4[3], sums4[4], sums2[1],
            sums2[2], hsum[0], sums3[0], rel[:RELS].reshape(-1), rel[HD : HD + RELS].reshape(-1),
        )
    output = gather_back(
        mlp_output(
            kept[-1][9], vec[-1], kept[-1][1], live, held.source(LAYERS - 1, "fc2"), (grad,)
        )
    ).astype(BF16)
    input_grad = gather_back(grad).astype(BF16)
    shards = lax.axis_size("fsdp")
    packed = jnp.concatenate(
        [
            jnp.stack([sums[layer][i] for layer in range(LAYERS)]).reshape(LAYERS, shards, -1)
            for i in range(len(parts))
        ],
        2,
    )
    big, mine = pending.finish(pair, packed)
    qv, pb, n1g, n1b, n2g, n2b, f1b, f2b, rh, rw = [
        mine[:, a:b] for a, b in zip(cuts, cuts[1:])
    ]
    stacked = [jnp.stack([big[layer][i] for layer in range(LAYERS)]) for i in range(4)]
    return (
        output, input_grad, stacked[0], qv, stacked[1], pb, n1g, n1b, n2g, n2b, stacked[2], f1b,
        stacked[3], f2b, rh, rw,
    )


def solution(mesh):
    rows = P(("rep", "fsdp"), None)
    cube = P(None, "fsdp", None)
    flat = P(None, "fsdp")
    ring = mesh.shape["rep"] == 4 and mesh.shape["fsdp"] == 8
    return jax.shard_map(
        functools.partial(on_device, ring),
        mesh=mesh,
        in_specs=(
            rows, P(("rep", "fsdp")), rows, cube, flat, cube, flat, flat, flat, flat, flat, cube,
            flat, cube, flat, flat, flat,
        ),
        out_specs=(
            rows, rows, cube, flat, cube, flat, flat, flat, flat, flat, cube, flat, cube, flat,
            flat, flat,
        ),
        check_vma=False,
    )
```

```python
import functools

import jax
import jax.numpy as jnp
import numpy as np
from jax import lax
from jax.experimental import pallas as pl
from jax.experimental.pallas import tpu as pltpu
from jax.sharding import PartitionSpec as P

HEADS = 12
HD = 64
WINDOW = 14
SIDE = 64
LAYERS = 2
GRID = 5
RELS = 2 * WINDOW - 1
EPSILON = 1e-06
PITCH = 16
SPAN = WINDOW * PITCH
PAIRS = HEADS // 2
LANES = 2 * HD
F32 = jnp.float32
BF16 = jnp.bfloat16
CHUNK = 768
ROWS_STEP = 64
VMEM_LIMIT = 56 * 1024 * 1024
SLAB = 384
RIDERS = 8
LARGE = 256 * 1024


def dot_nn(a, b):
    return lax.dot_general(a, b, (((1,), (0,)), ((), ())), preferred_element_type=F32)


def dot_nt(a, b):
    return lax.dot_general(a, b, (((1,), (1,)), ((), ())), preferred_element_type=F32)


def dot_tn(a, b):
    return lax.dot_general(a, b, (((0,), (0,)), ((), ())), preferred_element_type=F32)


def norm_rows(values):
    centre = jnp.mean(values, -1, keepdims=True)
    centered = values - centre
    inverse = lax.rsqrt(jnp.mean(centered * centered, -1, keepdims=True) + EPSILON)
    return centered * inverse, inverse


def norm_back(grad, normed, inverse, gain):
    scaled = grad * gain
    return inverse * (
        scaled
        - jnp.mean(scaled, -1, keepdims=True)
        - normed * jnp.mean(scaled * normed, -1, keepdims=True)
    )


def each(count, step, body):
    def run(index, carry):
        body(pl.multiple_of(index * step, step))
        return carry

    lax.fori_loop(0, count, run, 0)


def each_index(count, body):
    def run(index, carry):
        body(index)
        return carry

    lax.fori_loop(0, count, run, 0)


def in_fours(count, body):
    def several(index):
        for i in range(4):
            body(4 * index + i)

    each_index(count // 4, several)


def half_lane():
    return lax.broadcasted_iota(jnp.int32, (SPAN, LANES), 1)


def split_heads(pair):
    lane = half_lane()
    zero = jnp.zeros_like(pair)
    return jnp.concatenate(
        [jnp.where(lane < HD, pair, zero), jnp.where(lane < HD, zero, pair)], axis=0
    )


def join_heads(stacked):
    return jnp.where(half_lane() < HD, stacked[:SPAN], stacked[SPAN:])


def shift_rows(table):
    by_row = jnp.concatenate(
        [
            pltpu.roll(table[i * PITCH : (i + 1) * PITCH], i, axis=1) if i else table[:PITCH]
            for i in range(WINDOW)
        ],
        axis=0,
    )
    by_col = pltpu.roll(
        table.reshape(WINDOW, PITCH, LANES), 0, axis=2, stride=1, stride_axis=1
    ).reshape(SPAN, LANES)
    return jnp.where(half_lane() < HD, by_row, by_col)


def key_tables():
    ahead = np.zeros((SPAN, LANES), np.float32)
    back = np.zeros((SPAN, LANES), np.float32)
    for k in range(WINDOW):
        for m in range(PITCH):
            row = k * PITCH + m
            ahead[row, WINDOW - 1 + k] = 1.0
            back[row, WINDOW - 1 - k] = 1.0
            if m < WINDOW:
                ahead[row, HD + WINDOW - 1 + m] = 1.0
                back[row, HD + WINDOW - 1 - m] = 1.0
            else:
                ahead[row, LANES - 1] = -1e30
    return jnp.asarray(ahead, BF16), jnp.asarray(back, BF16)


class Flow:
    def __init__(self, ins, in_sem, outs, out_sem):
        self.ins = {}
        for i, (given, taken) in enumerate(ins):
            copy = pltpu.make_async_copy(given, taken, in_sem.at[i])
            copy.start()
            self.ins[id(taken)] = copy
        self.outs = {
            id(made): pltpu.make_async_copy(made, given, out_sem.at[i])
            for i, (made, given) in enumerate(outs)
        }
        self.sent = []

    def need(self, *refs):
        for ref in refs:
            copy = self.ins.pop(id(ref), None)
            if copy is not None:
                copy.wait()

    def emit(self, *refs):
        for ref in refs:
            copy = self.outs.pop(id(ref), None)
            if copy is not None:
                copy.start()
                self.sent.append(copy)

    def finish(self):
        for copy in self.ins.values():
            copy.wait()
        for copy in self.outs.values():
            copy.start()
        for copy in (*self.outs.values(), *self.sent):
            copy.wait()


def attend_kernel(source, flow, *refs):
    (x_ref, live_ref, vec_ref, table_ref, keys_ref), refs = refs[:5], refs[5:]
    weight_refs, refs = refs[: source.count], refs[source.count :]
    (mid_ref, h1_ref, q_ref, k_ref, v_ref, p_ref, att_ref), refs = refs[:7], refs[7:]
    token_ref, w_ref, sem = refs
    token_ref[...] = jnp.zeros_like(token_ref)
    ready = source.load("attend", weight_refs, w_ref, sem)
    width = x_ref.shape[1]
    flow.need(x_ref)

    def first_norm(start):
        rows = pl.ds(start, ROWS_STEP)
        normed, _ = norm_rows(x_ref[rows, :].astype(F32))
        shaped = (normed * vec_ref[0:1, :] + vec_ref[1:2, :]) * live_ref[rows, :]
        h1_ref[rows, :] = shaped.astype(BF16)

    each(x_ref.shape[0] // ROWS_STEP, ROWS_STEP, first_norm)
    flow.emit(h1_ref)
    ready()
    for index, (out_ref, bias) in enumerate(((q_ref, 2), (k_ref, None), (v_ref, 3))):

        def project(start, index=index, out_ref=out_ref, bias=bias):
            cols = pl.ds(start, CHUNK)
            made = dot_nn(h1_ref[...], w_ref[index, :, cols])
            if bias is not None:
                made = made + vec_ref[bias : bias + 1, cols]
            out_ref[:, cols] = made.astype(BF16)

        each(width // CHUNK, CHUNK, project)
        flow.emit(out_ref)

    def attend(index):
        rows = pl.ds(pl.multiple_of(index // PAIRS * SPAN, SPAN), SPAN)
        cols = pl.ds(pl.multiple_of(index % PAIRS * LANES, LANES), LANES)
        queries = q_ref[rows, cols]
        offsets = dot_nn(queries, table_ref[...])
        lane = half_lane()
        sides = []
        for half in range(2):
            moved = shift_rows(offsets[:, half * LANES : (half + 1) * LANES])
            sides.append(jnp.where(lane == LANES - 1, 1.0, moved).astype(BF16))
        left = jnp.concatenate(
            [split_heads(queries) * HD ** (-0.5), jnp.concatenate(sides, axis=0)], axis=1
        )
        right = jnp.concatenate([k_ref[rows, cols], keys_ref[...]], axis=1)
        scores = dot_nt(left, right)
        shifted = jnp.exp(scores - jnp.max(scores, -1, keepdims=True))
        probs = shifted * (1.0 / jnp.sum(shifted, -1, keepdims=True))
        low = probs.astype(BF16)
        p_ref[index] = low
        att_ref[rows, cols] = join_heads(dot_nn(low, v_ref[rows, cols])).astype(BF16)

    in_fours(x_ref.shape[0] // SPAN * PAIRS, attend)
    flow.emit(p_ref, att_ref)

    def finish(start):
        cols = pl.ds(start, CHUNK)
        branch = dot_nn(att_ref[...], w_ref[3, :, cols]) + vec_ref[4:5, cols]
        mid_ref[:, cols] = x_ref[:, cols].astype(F32) + live_ref[...] * branch

    each(width // CHUNK, CHUNK, finish)


def mlp_kernel(plan, source, top, flow, *refs):
    (mid_ref, live_ref, vec_ref, bias_ref), refs = refs[:4], refs[4:]
    if top:
        (grad_ref,), refs = refs[:1], refs[1:]
    weight_refs, refs = refs[: source.count], refs[source.count :]
    if top:
        (h2_ref, act_ref, slope_ref, sums_ref), refs = refs[:4], refs[4:]
        sink_refs, refs = refs[: plan.sinks], refs[plan.sinks :]
        (w1_ref, dm_ref, sem), refs = refs[:3], refs[3:]
        sink = plan.sink(sink_refs, refs, False)
    else:
        out_ref, h2_ref, act_ref, slope_ref, w1_ref, w2_ref, sem, sem2 = refs
    ready1 = source.load("fc1", weight_refs, w1_ref, sem)
    if not top:
        ready2 = source.load("fc2", weight_refs, w2_ref, sem2)
    width = mid_ref.shape[1]
    hidden_width = act_ref.shape[1]
    flow.need(mid_ref)

    def second_norm(start):
        rows = pl.ds(start, ROWS_STEP)
        normed, _ = norm_rows(mid_ref[rows, :])
        h2_ref[rows, :] = (normed * vec_ref[5:6, :] + vec_ref[6:7, :]).astype(BF16)

    each(mid_ref.shape[0] // ROWS_STEP, ROWS_STEP, second_norm)
    flow.emit(h2_ref)
    ready1()

    def expand(index):
        start = pl.multiple_of(index * CHUNK, CHUNK)
        cols = pl.ds(start, CHUNK)
        inner = pl.ds(pl.multiple_of(start % width, CHUNK), CHUNK)
        hidden = dot_nn(h2_ref[...], w1_ref[start // width, :, inner]) + bias_ref[:, cols]
        below = 0.5 * (1.0 + lax.erf(hidden * (0.5**0.5)))
        bell = jnp.exp(-0.5 * hidden * hidden) * (0.5 / np.pi) ** 0.5
        act_ref[:, cols] = (hidden * below).astype(BF16)
        slope_ref[:, cols] = (below + hidden * bell).astype(BF16)

    each_index(hidden_width // CHUNK, expand)
    flow.emit(act_ref, slope_ref)
    if top:
        sums_ref[...] = jnp.zeros_like(sums_ref)
        flow.need(grad_ref)
        second_weight(grad_ref, live_ref, act_ref, dm_ref, sums_ref, sink)
        sink.wait()
    else:
        ready2()
        contract(act_ref, w2_ref, vec_ref, mid_ref, live_ref, out_ref)


def contract(act_ref, w2_ref, vec_ref, mid_ref, live_ref, out_ref):
    def run(start):
        cols = pl.ds(start, CHUNK)
        made = dot_nn(act_ref[...], w2_ref[:, cols]) + vec_ref[7:8, cols]
        out_ref[:, cols] = mid_ref[:, cols] + live_ref[...] * made

    each(out_ref.shape[1] // CHUNK, CHUNK, run)


def out_kernel(source, flow, act_ref, vec_ref, mid_ref, live_ref, *refs):
    weight_refs, (out_ref, w2_ref, sem) = refs[: source.count], refs[source.count :]
    source.load("fc2", weight_refs, w2_ref, sem)()
    flow.need(act_ref, mid_ref)
    contract(act_ref, w2_ref, vec_ref, mid_ref, live_ref, out_ref)


def second_weight(grad_ref, live_ref, act_ref, dm_ref, sums_ref, sink):
    dm_ref[...] = (live_ref[...] * grad_ref[...].astype(F32)).astype(BF16)
    sums_ref[7:8, :] = jnp.sum(dm_ref[...].astype(F32), 0, keepdims=True)

    def run(index):
        rows = pl.ds(pl.multiple_of(index * SLAB, SLAB), SLAB)
        sink.rows(index, dot_tn(act_ref[:, rows], dm_ref[...]).astype(BF16))

    each_index(act_ref.shape[1] // SLAB, run)
    sink.send_all()


def hidden_back(flow, ready, sink, h2_ref, slope_ref, dh_ref, hsum_ref, w2_ref, dm_ref):
    width = h2_ref.shape[1]
    hidden_width = slope_ref.shape[1]
    flow.need(slope_ref)
    ready()

    def inner_grad(start):
        cols = pl.ds(start, CHUNK)
        made = (dot_nt(dm_ref[...], w2_ref[cols, :]) * slope_ref[:, cols].astype(F32)).astype(BF16)
        dh_ref[:, cols] = made
        hsum_ref[:, cols] = jnp.sum(made.astype(F32), 0, keepdims=True)

    each(hidden_width // CHUNK, CHUNK, inner_grad)
    flow.emit(dh_ref)
    flow.need(h2_ref)
    for block in range(hidden_width // width):

        def first_weight(start, block=block):
            cols = pl.ds(start, CHUNK)
            outer = pl.ds(pl.multiple_of(block * width + start, CHUNK), CHUNK)
            sink.cols(block, cols, dot_tn(h2_ref[...], dh_ref[:, outer]).astype(BF16))

        each(width // CHUNK, CHUNK, first_weight)
        sink.send(block)


def hidden_back_kernel(plan, source, flow, *refs):
    (grad_ref, act_ref, live_ref, h2_ref, slope_ref), refs = refs[:5], refs[5:]
    weight_refs, refs = refs[: source.count], refs[source.count :]
    (dh_ref, sums_ref, hsum_ref), refs = refs[:3], refs[3:]
    sink_refs, (w2_ref, dm_ref, sem), refs = refs[:2], refs[2:5], refs[5:]
    more, sink = plan.two_sinks(sink_refs, refs, True)
    ready = source.load("fc2", weight_refs, w2_ref, sem)
    sums_ref[...] = jnp.zeros_like(sums_ref)
    flow.need(grad_ref, act_ref)
    second_weight(grad_ref, live_ref, act_ref, dm_ref, sums_ref, more)
    hidden_back(flow, ready, sink, h2_ref, slope_ref, dh_ref, hsum_ref, w2_ref, dm_ref)
    more.wait()
    sink.wait()


def middle_back_kernel(source, flow, *refs):
    (grad_ref, mid_ref, vec_ref, dh_ref), refs = refs[:4], refs[4:]
    weight_refs, refs = refs[: source.count], refs[source.count :]
    dmid_ref, sums_ref, w1_ref, ds_ref, sem = refs
    ready = source.load("fc1", weight_refs, w1_ref, sem)
    flow.need(dh_ref)
    sums_ref[...] = jnp.zeros_like(sums_ref)
    middle_back(
        flow, ready, grad_ref, mid_ref, vec_ref, dh_ref, dmid_ref, sums_ref, w1_ref, ds_ref
    )


def middle_back(
    flow, ready, grad_ref, mid_ref, vec_ref, dh_ref, dmid_ref, sums_ref, w1_ref, ds_ref
):
    width = mid_ref.shape[1]
    hidden_width = dh_ref.shape[1]
    ready()

    def back_in(start):
        rows = pl.ds(start, CHUNK)
        made = dot_nt(dh_ref[:, 0:width], w1_ref[0, rows, :])
        for block in range(1, hidden_width // width):
            made += dot_nt(
                dh_ref[:, block * width : (block + 1) * width], w1_ref[block, rows, :]
            )
        ds_ref[:, rows] = made

    each(width // CHUNK, CHUNK, back_in)
    flow.need(mid_ref, grad_ref)

    def back_norm(start):
        rows = pl.ds(start, ROWS_STEP)
        normed, inverse = norm_rows(mid_ref[rows, :])
        grad = ds_ref[rows, :]
        sums_ref[5:6, :] += jnp.sum(grad * normed, 0, keepdims=True)
        sums_ref[6:7, :] += jnp.sum(grad, 0, keepdims=True)
        dmid_ref[rows, :] = grad_ref[rows, :].astype(F32) + norm_back(
            grad, normed, inverse, vec_ref[5:6, :]
        )

    each(mid_ref.shape[0] // ROWS_STEP, ROWS_STEP, back_norm)


def top_back_kernel(plan, source, flow, *refs):
    (grad_ref, mid_ref, live_ref, vec_ref, h2_ref, slope_ref), refs = refs[:6], refs[6:]
    weight_refs, refs = refs[: source.count], refs[source.count :]
    (dmid_ref, sums_ref, hsum_ref), refs = refs[:3], refs[3:]
    sink_refs, refs = refs[: plan.sinks], refs[plan.sinks :]
    (w1_ref, w2_ref, dm_ref, dh_ref, ds_ref, sem, sem2), refs = refs[:7], refs[7:]
    sink = plan.sink(sink_refs, refs, False)
    ready2 = source.load("fc2", weight_refs, w2_ref, sem2)
    ready1 = source.load("fc1", weight_refs, w1_ref, sem)
    sums_ref[...] = jnp.zeros_like(sums_ref)
    flow.need(grad_ref)
    dm_ref[...] = (live_ref[...] * grad_ref[...].astype(F32)).astype(BF16)
    hidden_back(flow, ready2, sink, h2_ref, slope_ref, dh_ref, hsum_ref, w2_ref, dm_ref)
    middle_back(
        flow, ready1, grad_ref, mid_ref, vec_ref, dh_ref, dmid_ref, sums_ref, w1_ref, ds_ref
    )
    sink.wait()


def scores_back_kernel(source, flow, *refs):
    (
        dmid_ref, live_ref, table_ref, keys_ref, q_ref, k_ref, v_ref, p_ref,
    ), refs = refs[:8], refs[8:]
    weight_refs, refs = refs[: source.count], refs[source.count :]
    db_ref, dq_ref, dk_ref, dv_ref, sums_ref, rel_ref, w_ref, da_ref, sem = refs
    ready = source.load("proj", weight_refs, w_ref, sem)
    width = dmid_ref.shape[1]
    flow.need(dmid_ref)
    db_ref[...] = (live_ref[...] * dmid_ref[...]).astype(BF16)
    flow.emit(db_ref)
    sums_ref[...] = jnp.zeros_like(sums_ref)
    sums_ref[0:1, :] = jnp.sum(db_ref[...].astype(F32), 0, keepdims=True)
    rel_ref[...] = jnp.zeros_like(rel_ref)
    ready()

    def back_out(start):
        rows = pl.ds(start, CHUNK)
        da_ref[:, rows] = dot_nt(db_ref[...], w_ref[rows, :]).astype(BF16)

    each(width // CHUNK, CHUNK, back_out)
    flow.need(v_ref, p_ref, k_ref, q_ref)

    def attend(index):
        rows = pl.ds(pl.multiple_of(index // PAIRS * SPAN, SPAN), SPAN)
        cols = pl.ds(pl.multiple_of(index % PAIRS * LANES, LANES), LANES)
        low = p_ref[index]
        probs = low.astype(F32)
        outer = split_heads(da_ref[rows, cols])
        queries = split_heads(q_ref[rows, cols])
        d_probs = dot_nt(outer, v_ref[rows, cols])
        dv_ref[rows, cols] = dot_tn(low, outer).astype(BF16)
        mean = jnp.sum(d_probs * probs, -1, keepdims=True)
        d_scores = (probs * (d_probs - mean)).astype(BF16)
        both = dot_nn(d_scores, jnp.concatenate([k_ref[rows, cols], keys_ref[...]], axis=1))
        moved = [
            shift_rows(both[half * SPAN : (half + 1) * SPAN, LANES:]).astype(BF16)
            for half in range(2)
        ]
        rel_part = dot_nt(jnp.concatenate(moved, axis=1), table_ref[...])
        direct = join_heads(both[:, :LANES]) * HD ** (-0.5)
        dq_ref[rows, cols] = (direct + rel_part).astype(BF16)
        dk_ref[rows, cols] = (dot_tn(d_scores, queries) * HD ** (-0.5)).astype(BF16)
        rel_ref[...] += dot_tn(jnp.concatenate(moved, axis=0), queries)

    in_fours(dmid_ref.shape[0] // SPAN * PAIRS, attend)
    flow.emit(dq_ref, dk_ref, dv_ref)
    sums_ref[1:2, :] = jnp.sum(dq_ref[...].astype(F32), 0, keepdims=True)
    sums_ref[2:3, :] = jnp.sum(dv_ref[...].astype(F32), 0, keepdims=True)


def first_weights(flow, sink, h1_ref, att_ref, db_ref, dq_ref, dk_ref, dv_ref):
    pairs = ((h1_ref, dq_ref), (h1_ref, dk_ref), (h1_ref, dv_ref), (att_ref, db_ref))
    for index, (left_ref, right_ref) in enumerate(pairs):
        flow.need(left_ref, right_ref)

        def weight(start, index=index, left_ref=left_ref, right_ref=right_ref):
            cols = pl.ds(start, CHUNK)
            sink.cols(index, cols, dot_tn(left_ref[...], right_ref[:, cols]).astype(BF16))

        each(h1_ref.shape[1] // CHUNK, CHUNK, weight)
        sink.send(index)


def first_weights_kernel(plan, flow, *refs):
    sink = plan.sink(refs[6 : 6 + plan.sinks], refs[6 + plan.sinks :], True)
    first_weights(flow, sink, *refs[:6])
    sink.wait()


def first_back(
    flow, ready, dmid_ref, x_ref, live_ref, vec_ref, dq_ref, dk_ref, dv_ref, next_ref, sums_ref,
    w_ref, dh_ref,
):
    width = x_ref.shape[1]
    flow.need(dq_ref, dk_ref, dv_ref)
    ready()

    def back_in(start):
        rows = pl.ds(start, CHUNK)
        made = dot_nt(dq_ref[...], w_ref[0, rows, :])
        made += dot_nt(dk_ref[...], w_ref[1, rows, :])
        made += dot_nt(dv_ref[...], w_ref[2, rows, :])
        dh_ref[:, rows] = made * live_ref[...]

    each(width // CHUNK, CHUNK, back_in)
    flow.need(x_ref, dmid_ref)
    sums_ref[...] = jnp.zeros_like(sums_ref)

    def back_norm(start):
        rows = pl.ds(start, ROWS_STEP)
        normed, inverse = norm_rows(x_ref[rows, :].astype(F32))
        grad = dh_ref[rows, :]
        sums_ref[3:4, :] += jnp.sum(grad * normed, 0, keepdims=True)
        sums_ref[4:5, :] += jnp.sum(grad, 0, keepdims=True)
        next_ref[rows, :] = dmid_ref[rows, :] + norm_back(grad, normed, inverse, vec_ref[0:1, :])

    each(x_ref.shape[0] // ROWS_STEP, ROWS_STEP, back_norm)


def first_back_kernel(source, flow, *refs):
    ins, refs = refs[:7], refs[7:]
    weight_refs, refs = refs[: source.count], refs[source.count :]
    next_ref, sums_ref, w_ref, dh_ref, sem = refs
    ready = source.load("attend", weight_refs, w_ref, sem)
    first_back(flow, ready, *ins, next_ref, sums_ref, w_ref, dh_ref)


def first_all_kernel(plan, source, flow, *refs):
    (dmid_ref, x_ref, live_ref, vec_ref, h1_ref, att_ref, db_ref), refs = refs[:7], refs[7:]
    (dq_ref, dk_ref, dv_ref), refs = refs[:3], refs[3:]
    weight_refs, refs = refs[: source.count], refs[source.count :]
    (next_ref, sums_ref), refs = refs[:2], refs[2:]
    sink_refs, refs = refs[: plan.sinks], refs[plan.sinks :]
    (w_ref, dh_ref, sem), refs = refs[:3], refs[3:]
    sink = plan.sink(sink_refs, refs, True)
    ready = source.load("attend", weight_refs, w_ref, sem)
    first_weights(flow, sink, h1_ref, att_ref, db_ref, dq_ref, dk_ref, dv_ref)
    first_back(
        flow, ready, dmid_ref, x_ref, live_ref, vec_ref, dq_ref, dk_ref, dv_ref, next_ref,
        sums_ref, w_ref, dh_ref,
    )
    sink.wait()


VM = pl.BlockSpec(memory_space=pltpu.VMEM)
ANY = pl.BlockSpec(memory_space=pltpu.HBM)


def shape(dims, kind):
    return jax.ShapeDtypeStruct(tuple(dims), kind)


class Source:
    def __init__(self, **parts):
        self.parts = parts
        self.arrays = []
        self.places = {}
        for name, (arrays, _, _) in parts.items():
            found = []
            for array in arrays:
                known = [i for i, other in enumerate(self.arrays) if other is array]
                if not known:
                    known = [len(self.arrays)]
                    self.arrays.append(array)
                found.append(known[0])
            self.places[name] = found
        self.count = len(self.arrays)

    def semaphores(self, name):
        whole = self.parts[name][1] is None
        return pltpu.SemaphoreType.DMA((4 if whole else 8 if name == "proj" else 32,))

    def load(self, name, refs, target, sem):
        arrays, offset, rotated = self.parts[name]
        refs = [refs[i] for i in self.places[name]]
        if offset is not None and name == "proj":
            return load_proj(refs, target, offset, rotated, sem)
        if offset is None:
            pairs = whole_pairs(name, refs, target)
        else:
            pairs = [pair for _, _, pair in piece_pairs(name, refs, target, offset, rotated)]
        copies = [
            pltpu.make_async_copy(given, taken, sem.at[i])
            for i, (given, taken) in enumerate(pairs)
        ]
        for copy in copies:
            copy.start()

        def ready():
            for copy in copies:
                copy.wait()

        return ready


def whole_pairs(name, refs, target):
    if name == "fc2":
        return [(refs[0], target)]
    if name == "proj":
        return [(refs[1], target)]
    width = target.shape[1]
    pairs = []
    for ref in refs:
        for start in range(0, ref.shape[1], width):
            pairs.append((ref.at[:, pl.ds(start, width)], target.at[len(pairs)]))
    return pairs


def position():
    shard = lax.axis_index("fsdp")
    return lax.axis_index("rep"), shard >> 1, shard & 1


def piece_pairs(name, refs, target, offset, rotated):
    rep, level, core = position()
    pairs = []
    rows = target.shape[-2] // 8
    span = rows // 4 if name == "fc2" else rows
    for parity in range(2):
        for part, (away, levels) in enumerate(
            ((0, range(4)), (1, range(4)), (2, range(4)), (3, range(2)), (3, range(2, 4)))
        ):
            ref = refs[parity * 5 + part]
            for place, step in enumerate(levels):
                source_level = (level - step) & 3 if rotated else step
                shard = source_level * 2 + (core ^ parity)
                kind = rep ^ away
                if name == "fc2":
                    start = pl.multiple_of(shard * rows + kind * span, 16)
                    taken = target.at[pl.ds(start, span), :]
                else:
                    start = pl.multiple_of(shard * span, 16)
                    whole = target if name == "proj" else target.at[kind]
                    taken = whole.at[pl.ds(start, span), :]
                given = ref.at[place, pl.ds(offset, span), :]
                pairs.append((away, parity * 4 + step, (given, taken)))
    return pairs


def load_proj(refs, target, offset, rotated, sem):
    rep = lax.axis_index("rep")
    pairs = piece_pairs("proj", refs, target, offset, rotated)
    for away in range(4):

        @pl.when((rep ^ away) == 3)
        def _(away=away):
            for other, slot, pair in pairs:
                if other == away:
                    pltpu.make_async_copy(*pair, sem.at[slot]).start()

    def ready():
        for away, slot, pair in pairs:
            if away == 0:
                pltpu.make_async_copy(*pair, sem.at[slot]).wait()

    return ready


class WholeSink:
    def __init__(self, refs, scratch):
        self.ref = refs[0]
        self.held, self.sem = scratch[:2]
        self.sent = []

    def rows(self, index, value):
        self.held[pl.ds(pl.multiple_of(index * SLAB, SLAB), SLAB), :] = value

    def cols(self, block, cols, value):
        self.held[block, :, cols] = value

    def copy(self, given, taken):
        copy = pltpu.make_async_copy(given, taken, self.sem.at[len(self.sent)])
        copy.start()
        self.sent.append(copy)

    def send(self, block):
        self.copy(self.held.at[block], self.ref.at[block])

    def send_all(self):
        self.copy(self.held, self.ref)

    def wait(self):
        for copy in self.sent:
            copy.wait()


class PieceSink:
    def __init__(self, refs, scratch, rotated, offset=0):
        self.refs, self.rotated, self.offset = refs, rotated, offset
        self.held, self.sem = scratch[:2]
        self.position = position()
        self.sent = []

    def rows(self, index, value):
        span = self.held.shape[3]
        for block in range(4):
            self.held[index & 1, block, index >> 1] = value[block * span : (block + 1) * span]

    def cols(self, block, cols, value):
        span = self.held.shape[3]
        for shard in range(8):
            self.held[shard & 1, block, shard >> 1, :, cols] = value[
                shard * span : (shard + 1) * span
            ]

    def send(self, block):
        rep, level, core = self.position
        for parity in range(2):
            given = self.held.at[core ^ parity, block]
            span = self.held.shape[3]
            taken = self.refs[parity].at[rep ^ block, :, pl.ds(self.offset, span)]
            moves = [(given, taken)]
            if self.rotated:
                moves = [(given.at[(level + step) & 3], taken.at[step]) for step in range(4)]
            for move in moves:
                copy = pltpu.make_async_copy(*move, self.sem.at[len(self.sent)])
                copy.start()
                self.sent.append(copy)

    def send_all(self):
        for block in range(4):
            self.send(block)

    def wait(self):
        for copy in self.sent:
            copy.wait()


class WholePlan:
    sinks = 1

    def sink(self, refs, scratch, rotated=False):
        return WholeSink(refs, scratch)

    def sink_outs(self, dims):
        return [shape(dims, BF16)], [ANY], [pltpu.VMEM(dims, BF16), pltpu.SemaphoreType.DMA((4,))]

    def two_sinks(self, refs, scratch, rotated):
        return WholeSink(refs[:1], scratch), WholeSink(refs[1:], scratch[2:])

    def two_outs(self, hidden, width):
        one = self.sink_outs((hidden, width))
        two = self.sink_outs((hidden // width, width, width))
        return one[0] + two[0], one[1] + two[1], one[2] + two[2]


class PiecePlan:
    sinks = 2

    def sink(self, refs, scratch, rotated=False):
        return PieceSink(refs, scratch, rotated)

    def sink_outs(self, dims):
        width = dims[-1]
        span = int(np.prod(dims)) // width // 32
        outs = [shape((4, 4, span, width), BF16)] * 2
        scratch = [pltpu.VMEM((2, 4, 4, span, width), BF16), pltpu.SemaphoreType.DMA((32,))]
        return outs, [ANY] * 2, scratch

    def two_sinks(self, refs, scratch, rotated):
        span = scratch[0].shape[3]
        return PieceSink(refs, scratch, rotated), PieceSink(refs, scratch[2:], rotated, span)

    def two_outs(self, hidden, width):
        span = hidden // 32
        outs = [shape((4, 4, 2 * span, width), BF16)] * 2
        scratch = [pltpu.VMEM((2, 4, 4, span, width), BF16), pltpu.SemaphoreType.DMA((32,))] * 2
        return outs, [ANY] * 2, scratch


def large(array):
    return int(np.prod(array.shape)) * np.dtype(array.dtype).itemsize >= LARGE


def call(kernel, resident, source, outs, scratch, micros, sinks=(), after=()):
    sink_outs, sink_specs, sink_scratch = [], [], []
    for more_outs, more_specs, more_scratch in sinks:
        sink_outs += more_outs
        sink_specs += more_specs
        sink_scratch += more_scratch
    in_moves = [i for i, a in enumerate(resident) if large(a)]
    out_moves = [i for i, a in enumerate(outs) if large(a)]
    buffers = [pltpu.VMEM(resident[i].shape, resident[i].dtype) for i in in_moves]
    buffers += [pltpu.VMEM(outs[i].shape, outs[i].dtype) for i in out_moves]
    semaphores = [
        pltpu.SemaphoreType.DMA((max(len(moves), 1),)) for moves in (in_moves, out_moves)
    ]
    count = len(resident)
    first = count + source.count

    def body(*refs):
        ins, weights = list(refs[:count]), refs[count:first]
        refs = refs[first + len(after) :]
        made, refs = list(refs[: len(outs)]), refs[len(outs) :]
        sunk, refs = refs[: len(sink_outs)], refs[len(sink_outs) :]
        held, refs = refs[: len(buffers)], refs[len(buffers) :]
        in_sem, out_sem, *rest = refs
        in_held, out_held = held[: len(in_moves)], held[len(in_moves) :]
        flow = Flow(
            [(ins[i], ref) for i, ref in zip(in_moves, in_held)],
            in_sem,
            [(ref, made[i]) for i, ref in zip(out_moves, out_held)],
            out_sem,
        )
        for i, ref in zip(in_moves, in_held):
            ins[i] = ref
        for i, ref in zip(out_moves, out_held):
            made[i] = ref
        kernel(flow, *ins, *weights, *made, *sunk, *rest)
        flow.finish()

    run = pl.pallas_call(
        body,
        out_shape=tuple([*outs, *sink_outs]),
        in_specs=[ANY if large(a) else VM for a in resident]
        + [ANY] * (source.count + len(after)),
        out_specs=tuple([*[ANY if large(a) else VM for a in outs], *sink_specs]),
        scratch_shapes=[*buffers, *semaphores, *scratch, *sink_scratch],
        compiler_params=pltpu.CompilerParams(vmem_limit_bytes=VMEM_LIMIT),
        cost_estimate=pl.CostEstimate(
            flops=int(micros * 1e9), bytes_accessed=1 << 20, transcendentals=0
        ),
    )
    return run(*resident, *source.arrays, *after)


def attend_forward(x, live, vec, table, keys, source, after):
    rows, width = x.shape
    outs = (
        shape((rows, width), F32),
        *[shape((rows, width), BF16)] * 4,
        shape((rows // SPAN * PAIRS, 2 * SPAN, SPAN), BF16),
        shape((rows, width), BF16),
        shape((8, LANES), F32),
    )
    scratch = [pltpu.VMEM((4, width, width), BF16), source.semaphores("attend")]
    return call(
        functools.partial(attend_kernel, source),
        (x, live, vec, table, keys), source, outs, scratch, 20, (), after,
    )


def mlp_forward(plan, top, mid, live, vec, bias, grad, source, after):
    rows, width = mid.shape
    hidden = bias.shape[1]
    outs = [
        shape((rows, width), BF16), shape((rows, hidden), BF16), shape((rows, hidden), BF16),
    ]
    scratch = [pltpu.VMEM((hidden // width, width, width), BF16)]
    resident = [mid, live, vec, bias]
    sinks = []
    if top:
        resident.append(grad)
        outs.append(shape((8, width), F32))
        scratch += [pltpu.VMEM((rows, width), BF16), source.semaphores("fc1")]
        sinks.append(plan.sink_outs((hidden, width)))
    else:
        outs.insert(0, shape((rows, width), F32))
        scratch += [
            pltpu.VMEM((hidden, width), BF16), source.semaphores("fc1"),
            source.semaphores("fc2"),
        ]
    return call(
        functools.partial(mlp_kernel, plan, source, top),
        resident, source, outs, scratch, 16, sinks, after,
    )


def mlp_output(act, vec, mid, live, source, after):
    hidden, width = act.shape[1], mid.shape[1]
    scratch = [pltpu.VMEM((hidden, width), BF16), source.semaphores("fc2")]
    return call(
        functools.partial(out_kernel, source), (act, vec, mid, live), source,
        [shape(mid.shape, F32)], scratch, 5, (), after,
    )[0]


def hidden_backward(plan, grad, act, live, h2, slope, source, after):
    rows, width = h2.shape
    hidden = slope.shape[1]
    outs = [shape((rows, hidden), BF16), shape((8, width), F32), shape((1, hidden), F32)]
    scratch = [
        pltpu.VMEM((hidden, width), BF16), pltpu.VMEM((rows, width), BF16),
        source.semaphores("fc2"),
    ]
    return call(
        functools.partial(hidden_back_kernel, plan, source),
        (grad, act, live, h2, slope), source, outs, scratch, 18,
        [plan.two_outs(hidden, width)], after,
    )


def top_backward(plan, grad, mid, live, vec, h2, slope, source, after):
    rows, width = mid.shape
    hidden = slope.shape[1]
    outs = [shape((rows, width), F32), shape((8, width), F32), shape((1, hidden), F32)]
    scratch = [
        pltpu.VMEM((hidden // width, width, width), BF16), pltpu.VMEM((hidden, width), BF16),
        pltpu.VMEM((rows, width), BF16), pltpu.VMEM((rows, hidden), BF16),
        pltpu.VMEM((rows, width), F32), source.semaphores("fc1"), source.semaphores("fc2"),
    ]
    return call(
        functools.partial(top_back_kernel, plan, source),
        (grad, mid, live, vec, h2, slope), source, outs, scratch, 19,
        [plan.sink_outs((hidden // width, width, width))], after,
    )


def middle_backward(grad, mid, vec, dh, source, after):
    rows, width = mid.shape
    hidden = dh.shape[1]
    outs = [shape((rows, width), F32), shape((8, width), F32)]
    scratch = [
        pltpu.VMEM((hidden // width, width, width), BF16), pltpu.VMEM((rows, width), F32),
        source.semaphores("fc1"),
    ]
    return call(
        functools.partial(middle_back_kernel, source),
        (grad, mid, vec, dh), source, outs, scratch, 10, (), after,
    )


def scores_backward(dmid, live, table, keys, q, k, v, p, source, after):
    rows, width = dmid.shape
    outs = [*[shape((rows, width), BF16)] * 4, shape((8, width), F32), shape((LANES, LANES), F32)]
    scratch = [
        pltpu.VMEM((width, width), BF16), pltpu.VMEM((rows, width), BF16),
        source.semaphores("proj"),
    ]
    return call(
        functools.partial(scores_back_kernel, source),
        (dmid, live, table, keys, q, k, v, p), source, outs, scratch, 15, (), after,
    )


def weights_backward(plan, h1, att, db, dq, dk, dv, after):
    width = h1.shape[1]
    return call(
        functools.partial(first_weights_kernel, plan), (h1, att, db, dq, dk, dv),
        Source(), [], [], 8, [plan.sink_outs((4, width, width))], after,
    )


def first_backward(dmid, x, live, vec, dq, dk, dv, source, after):
    rows, width = x.shape
    outs = [shape((rows, width), F32), shape((8, width), F32)]
    scratch = [
        pltpu.VMEM((4, width, width), BF16), pltpu.VMEM((rows, width), F32),
        source.semaphores("attend"),
    ]
    return call(
        functools.partial(first_back_kernel, source),
        (dmid, x, live, vec, dq, dk, dv), source, outs, scratch, 10, (), after,
    )


def first_all_backward(plan, dmid, x, live, vec, h1, att, db, dq, dk, dv, source, after):
    rows, width = x.shape
    outs = [shape((rows, width), F32), shape((8, width), F32)]
    scratch = [
        pltpu.VMEM((4, width, width), BF16), pltpu.VMEM((rows, width), F32),
        source.semaphores("attend"),
    ]
    return call(
        functools.partial(first_all_kernel, plan, source),
        (dmid, x, live, vec, h1, att, db, dq, dk, dv), source, outs, scratch, 14,
        [plan.sink_outs((4, width, width))], after,
    )


def live_rows(slot_table):
    places = jnp.arange(PITCH, dtype=jnp.int32)
    rows_inside = slot_table[:, None] // GRID * WINDOW + places[None, :WINDOW] < SIDE
    cols_inside = slot_table[:, None] % GRID * WINDOW + places[None, :] < SIDE
    cols_inside = cols_inside & (places < WINDOW)[None, :]
    both_inside = rows_inside[:, :, None] & cols_inside[:, None, :]
    return both_inside.astype(F32).reshape(slot_table.shape[0] * SPAN, 1)


def spread(values):
    width = values.shape[1]
    grid = values.reshape(-1, WINDOW, width)
    return jnp.pad(grid, ((0, 0), (0, PITCH - WINDOW), (0, 0))).reshape(-1, width)


def gather_back(values):
    width = values.shape[1]
    return values.reshape(-1, PITCH, width)[:, :WINDOW].reshape(-1, width)


def relative_tables(rel_height, rel_width):
    stacked = jnp.stack([rel_height, rel_width], 1).reshape(LAYERS, 2, RELS, HD)

    def spread_table(rows):
        padded = jnp.pad(rows, ((0, 0), (0, 0), (0, HD - RELS), (0, 0)))
        one = padded.reshape(LAYERS, LANES, HD).transpose(0, 2, 1)
        none = jnp.zeros_like(one)
        return jnp.concatenate(
            [jnp.concatenate([one, none], 2), jnp.concatenate([none, one], 2)], 1
        )

    return spread_table(stacked[:, :, ::-1]), spread_table(stacked)


def whole_weights(weights):
    qkv, proj, fc1, fc2 = weights
    layers = []
    for layer in range(LAYERS):
        q, p, a, b = (
            lax.all_gather(w[layer], "fsdp", axis=0, tiled=True) for w in (qkv, proj, fc1, fc2)
        )
        layers.append(
            dict(attend=((q, p), None, False), proj=((q, p), None, False), fc1=((a,), None, False), fc2=((b,), None, False))
        )
    return layers


def whole_small(parts):
    packed = jnp.concatenate(parts, axis=1)
    return lax.all_gather(packed, "fsdp", axis=0, tiled=False)


def whole_reduce(value, axis):
    return lax.psum(lax.psum_scatter(value, "fsdp", scatter_dimension=axis, tiled=True), "rep")


def whole_sums(grads):
    (g,), (g2, g1) = grads
    return whole_reduce(g, 1), whole_reduce(g1, 1), whole_reduce(g2, 0)


def named(g, g1, g2):
    return jnp.concatenate([g[0], g[1], g[2]], 1), g[3], jnp.concatenate(list(g1), 1), g2


def permute(value, axis, move):
    return lax.ppermute(value, axis, [(i, move(i)) for i in range({"rep": 4, "fsdp": 8}[axis])])


def to_x(value):
    return permute(value, "rep", lambda i: i ^ 1)


def to_y(value):
    return permute(value, "rep", lambda i: i ^ 2)


def to_xy(value):
    return permute(value, "rep", lambda i: i ^ 3)


def to_core(value):
    return permute(value, "fsdp", lambda i: i ^ 1)


def to_level(value, step):
    return permute(value, "fsdp", lambda i: (i + 2 * step) % 8)


LEVELS = [[0, 2, 4, 6], [1, 3, 5, 7]]


def nothing(value):
    return jnp.minimum(jnp.abs(value), 0)


def swap(value, flag, axis):
    first = lax.slice_in_dim(value, 0, 1, axis=axis)
    second = lax.slice_in_dim(value, 1, 2, axis=axis)
    return jnp.where(flag == 1, jnp.concatenate([second, first], axis), value)


def by_replica(value, rep):
    rest = value.shape[1:]
    value = value.reshape(2, 2, *rest)
    value = swap(swap(value, rep & 1, 1), rep >> 1, 0)
    return value.reshape(4, *rest)


def turn(value, start, axis):
    size = value.shape[axis]
    return lax.dynamic_slice_in_dim(
        jnp.concatenate([value, value], axis), start, size, axis
    )


def own_blocks(weights, layer, rep):
    qkv, proj, fc1, fc2 = (w[layer] for w in weights)
    width = proj.shape[1]
    span = proj.shape[0]
    first = lax.dynamic_slice_in_dim(jnp.concatenate([qkv, proj], 1), rep * width, width, 1)
    second = lax.dynamic_slice_in_dim(fc1, rep * width, width, 1)
    third = lax.dynamic_slice_in_dim(fc2, rep * span, span, 0)
    return first, second, third


class Across:
    def __init__(self, held):
        self.held = held
        self.x, self.y = to_x(held), to_y(held)

    def cross(self, token=None):
        low, high = self.y[:2], self.x[2:]
        if token is not None:
            low, high = low + token, high + token
        self.low, self.high = to_x(low), to_y(high)
        return low, high

    def finish(self, token=None):
        low, high = self.low, self.high
        if token is not None:
            low, high = low + token, high + token
        pieces = (self.held, self.x, self.y, low, high)
        return pieces + tuple(to_core(piece) for piece in pieces)


class PieceWeights:
    def __init__(self, weights, small):
        rep, level, core = position()
        blocks = [own_blocks(weights, layer, rep) for layer in range(LAYERS)]
        span, width = blocks[0][0].shape
        size = small.shape[0] // 4
        rider = lax.dynamic_slice_in_dim(small, rep * size, size, 0)
        rider = jnp.pad(rider, (0, RIDERS * width - size)).reshape(RIDERS, width)
        first = jnp.concatenate([*blocks[0][:2], rider], 0)[None]
        self.span = span
        held = jnp.concatenate([first] + [to_level(first, step) for step in (1, 2, 3)], 0)
        self.rest = lax.all_gather(
            jnp.concatenate([blocks[0][2], blocks[1][0]], 0) + nothing(held[3, 0, 0]), "fsdp",
            axis=0, tiled=True, axis_index_groups=LEVELS,
        ).reshape(4, 2 * span, width)
        self.fc1 = lax.all_gather(
            weights[2][1] + nothing(self.rest[0, 0, 0]), "fsdp", axis=0, tiled=True
        )
        self.fc2 = lax.all_gather(
            weights[3][1] + nothing(self.fc1[0, 0]), "fsdp", axis=0, tiled=True
        )
        one = Across(held)
        one.cross()
        self.one = one.finish()
        riders = jnp.stack(
            [
                jnp.concatenate([t[:, 2 * span :] for t in self.one[5 * p : 5 * p + 5]], 0).reshape(
                    4, 4, RIDERS * width
                )[:, :, :size]
                for p in range(2)
            ]
        )
        riders = by_replica(swap(riders, core, 0).transpose(1, 0, 2, 3), rep)
        turned = jnp.concatenate([riders[:, :, i : i + 1] for i in (3, 2, 1, 0)], 2)
        riders = turn(turned, 3 - level, 2)
        self.small = riders.transpose(2, 1, 0, 3).reshape(8, LAYERS, -1)

    def before(self, name):
        if name == "attend_0":
            self.next = Across(self.rest)
            return (self.rest,)
        if name == "mlp_0":
            self.two = self.next.finish()
        return ()

    def passed(self, name, token):
        if name == "attend_0":
            self.next.cross(token[0, 0].astype(BF16))

    def source(self, layer, *names):
        if layer == 0:
            parts = dict(
                attend=lambda: (self.one, 0, True),
                proj=lambda: (self.one, 0, True),
                fc1=lambda: (self.one, self.span, True),
                fc2=lambda: (self.two, 0, False),
            )
        else:
            parts = dict(
                attend=lambda: (self.two, self.span, False),
                proj=lambda: (self.two, self.span, False),
                fc1=lambda: ((self.fc1,), None, False),
                fc2=lambda: ((self.fc2,), None, False),
            )
        return Source(**{name: parts[name]() for name in names})


class WholeWeights:
    def __init__(self, weights, small):
        self.small = whole_small(small)
        self.layers = whole_weights(weights)

    def before(self, name):
        return ()

    def passed(self, name, token):
        pass

    def source(self, layer, *names):
        return Source(**{name: self.layers[layer][name] for name in names})


class ReplicaSum:
    def __init__(self, *pairs):
        self.pairs = [(keep, to_core(send)) for keep, send in pairs]
        self.step = 0

    def both(self, away, part):
        sums = [
            keep[away, part].astype(F32) + got[away, part].astype(F32) for keep, got in self.pairs
        ]
        return sums[0] if len(sums) == 1 else jnp.concatenate(sums, -2)

    def advance(self):
        low, high = slice(0, 2), slice(2, 4)
        self.step += 1
        if self.step == 1:
            send_x = self.both(slice(1, 4, 2), low).astype(BF16)
            send_y = self.both(slice(2, 4), high).astype(BF16)
            self.x, self.y = to_x(send_x), to_y(send_y)
            return [send_x, send_y]
        if self.step == 2:
            send_y = (self.both(2, low) + self.x[1].astype(F32)).astype(BF16)
            send_x = (self.both(1, high) + self.y[1].astype(F32)).astype(BF16)
            self.last_y, self.last_x = to_y(send_y), to_x(send_x)
            return [send_x, send_y]
        if self.step == 4:
            low, high = self.result
            sends = (low[1], high[0], high[1])
            self.levels = [to_level(send, step + 1) for step, send in enumerate(sends)]
            return list(sends)
        if self.step == 5:
            total = self.result[0][0].astype(F32)
            for got in self.levels:
                total = total + got.astype(F32)
            self.total = total.astype(BF16)
            return [self.total]
        self.result = [
            (self.both(0, low) + self.x[0].astype(F32) + self.last_y.astype(F32)).astype(BF16),
            (self.both(0, high) + self.y[0].astype(F32) + self.last_x.astype(F32)).astype(BF16),
        ]
        return self.result


class PieceSums:
    def __init__(self, plan):
        self.plan = plan
        self.sums = {}

    def add(self, name, pair):
        self.sums[name] = ReplicaSum(pair)

    def advance(self, *names):
        found = []
        for name in names:
            found += self.sums[name].advance()
        return found

    def finish(self, sums, top):
        last = self.sums["attend"]
        riders = ReplicaSum(pack_riders(self.plan, sums))
        span, width = last.pairs[0][0].shape[2:]
        last.advance()
        for _ in range(3):
            riders.advance()
        self.advance("mlp", "mlp", "mlp")
        last.advance()
        last.advance()
        first = last.result[0][0, 0, 0]
        last.result = [jnp.concatenate(pair, 1) for pair in zip(last.result, riders.result)]
        last.advance()
        late = to_replicas(self.sums["mlp"].total + nothing(first))
        last.advance()
        self.token = first
        g, g1, g2 = top
        big = assemble_late(g1, g2, late)
        return assemble_last(to_replicas(last.total), g), big


def to_replicas(value):
    return value, to_x(value), to_y(value), to_xy(value)


def load_replicas(refs, held, sem):
    rep = lax.axis_index("rep")
    copies = [
        pltpu.make_async_copy(ref, held.at[rep ^ away], sem.at[away])
        for away, ref in enumerate(refs)
    ]
    for copy in copies:
        copy.start()
    return copies


def late_kernel(flow, g1_ref, g2_ref, *refs):
    held, sem = refs[6:]
    fc1_ref, fc2_ref = refs[4:6]
    copies = load_replicas(refs[:4], held, sem)
    width = fc2_ref.shape[2]
    span = g1_ref.shape[1]
    flow.need(g1_ref, g2_ref)
    fc2_ref[1] = g2_ref[...].astype(F32)
    for block in range(4):
        fc1_ref[1, :, block * width : (block + 1) * width] = g1_ref[block].astype(F32)
    for copy in copies:
        copy.wait()
    for block in range(4):
        fc1_ref[0, :, block * width : (block + 1) * width] = held[block, span:].astype(F32)
        fc2_ref[0, block * span : (block + 1) * span, :] = held[block, :span].astype(F32)


def assemble_late(g1, g2, late):
    _, span, width = g1.shape
    return call(
        late_kernel, (g1, g2), Pieces(late),
        [shape((LAYERS, span, 4 * width), F32), shape((LAYERS, 4 * span, width), F32)],
        [pltpu.VMEM((4, *late[0].shape), BF16), pltpu.SemaphoreType.DMA((4,))], 4,
    )


class Pieces:
    def __init__(self, arrays):
        self.arrays, self.count = arrays, len(arrays)


def last_kernel(flow, g_ref, *refs):
    last_refs, refs = refs[:4], refs[4:]
    (qkv_ref, proj_ref), refs = refs[:2], refs[2:]
    small_refs, (held, sem) = refs[:10], refs[10:]
    copies = load_replicas(last_refs, held, sem)
    width = proj_ref.shape[2]
    span = g_ref.shape[1]
    flow.need(g_ref)

    def put(layer, source):
        for block in range(3):
            qkv_ref[layer, :, block * width : (block + 1) * width] = source[
                block, :span
            ].astype(F32)
        proj_ref[layer] = source[3, :span].astype(F32)

    put(1, g_ref)
    for copy in copies:
        copy.wait()
    put(0, held)
    unit = width // 8
    heads = held[0, span:].astype(F32)
    others = held[1, span:].astype(F32)
    rel = held[2, span:].astype(F32)
    qv, pb, n1g, n1b, n2g, n2b, f1b, f2b, rh, rw = small_refs
    size = rh.shape[1]
    for layer in range(LAYERS):
        for ref, row in ((pb, 0), (n1g, 3), (n1b, 4), (n2g, 5), (n2b, 6), (f2b, 7)):
            ref[layer : layer + 1, :] = heads[row : row + 1, layer * unit : (layer + 1) * unit]
        qv[layer : layer + 1, :] = others[layer : layer + 1, : 2 * unit]
        f1b[layer : layer + 1, :] = others[layer : layer + 1, 2 * unit : 6 * unit]
        rh[layer : layer + 1, :] = rel[2 * layer : 2 * layer + 1, :size]
        rw[layer : layer + 1, :] = rel[2 * layer + 1 : 2 * layer + 2, :size]


def assemble_last(last, g):
    _, span, width = g.shape
    unit = width // 8
    sizes = (2 * unit, *[unit] * 5, 4 * unit, unit, RELS * HD // 8, RELS * HD // 8)
    outs = [shape((LAYERS, span, 3 * width), F32), shape((LAYERS, span, width), F32)]
    outs += [shape((LAYERS, size), F32) for size in sizes]
    return call(
        last_kernel, (g,), Pieces(last), outs,
        [pltpu.VMEM((4, *last[0].shape), BF16), pltpu.SemaphoreType.DMA((4,))], 4,
    )


def pack_kernel(plan, flow, *refs):
    (
        (heads_ref, hidden_ref, rel_ref), (heads1_ref, hidden1_ref, rel1_ref)
    ), refs = (refs[:3], refs[3:6]), refs[6:]
    sink = plan.sink(refs[: plan.sinks], refs[plan.sinks :], True)
    held = sink.held
    held[...] = jnp.zeros_like(held)
    layers = ((heads_ref, hidden_ref, rel_ref), (heads1_ref, hidden1_ref, rel1_ref))
    span = heads_ref.shape[1] // 8
    for layer, (heads, hidden, rel) in enumerate(layers):
        for shard in range(8):
            core, level = shard & 1, shard >> 1
            cut = heads[:, shard * span : (shard + 1) * span]
            held[core, 0, level, :, layer * span : (layer + 1) * span] = cut.astype(BF16)
            first = shard % 4 * 2 * span
            row = 1 if shard < 4 else 2
            pair = heads[row : row + 1, first : first + 2 * span]
            held[core, 1, level, layer : layer + 1, 0 : 2 * span] = pair.astype(BF16)
            start = shard * 4 * span
            held[core, 1, level, layer : layer + 1, 2 * span : 6 * span] = hidden[
                :, start : start + 4 * span
            ].astype(BF16)
            held[core, 2, level, 2 * layer : 2 * layer + 2, 0 : rel.shape[2]] = rel[
                shard
            ].astype(BF16)
    sink.send_all()
    sink.wait()


def pack_riders(plan, sums):
    resident = []
    width = sums[0][0].shape[1]
    for heads, hidden, rel in sums:
        resident += [heads, hidden, rel]
    return call(
        functools.partial(pack_kernel, plan), resident, Source(), [], [], 3,
        [plan.sink_outs((32, RIDERS, width))],
    )


class WholeSums:
    def __init__(self, plan):
        self.pairs = {}

    def add(self, name, pair):
        self.pairs[name] = pair

    def advance(self, *names):
        return ()

    def finish(self, sums, top):
        self.token = sums[0][0]
        big = [named(*whole_sums((self.pairs["attend"], self.pairs["mlp"]))), named(*top)]
        shards = lax.axis_size("fsdp")
        parts = []
        for heads, hidden, rel in sums:
            rel = rel.transpose(1, 0, 2).reshape(2, -1)
            rows = (
                jnp.concatenate([heads[1], heads[2]]), heads[0], heads[3], heads[4], heads[5],
                heads[6], hidden[0], heads[7], rel[0], rel[1],
            )
            parts.append([row.reshape(shards, -1) for row in rows])
        cuts = np.cumsum([0] + [part.shape[1] for part in parts[0]])
        small = jnp.stack([jnp.concatenate(rows, 1) for rows in parts])
        mine = whole_reduce(small.astype(BF16), 1).astype(F32)[:, 0]
        stacked = [
            jnp.stack([big[layer][i] for layer in range(LAYERS)]).astype(F32) for i in range(4)
        ]
        small = [mine[:, a:b] for a, b in zip(cuts, cuts[1:])]
        return (*stacked[:2], *small), stacked[2:]


def on_device(
    ring, windows, slot_table, cotangent, qkv_weight, qv_bias, proj_weight, proj_bias,
    norm1_gain, norm1_bias, norm2_gain, norm2_bias, fc1_weight, fc1_bias, fc2_weight, fc2_bias,
    rel_height, rel_width,
):
    width = windows.shape[1]
    weights = (qkv_weight, proj_weight, fc1_weight, fc2_weight)
    parts = (
        qv_bias, proj_bias, norm1_gain, norm1_bias, norm2_gain, norm2_bias, fc1_bias, fc2_bias,
        rel_height, rel_width,
    )
    cuts = np.cumsum([0] + [part.shape[1] for part in parts])
    if ring:
        plan = PiecePlan()
        pending = PieceSums(plan)
        held = PieceWeights(weights, jnp.concatenate(parts, 1).reshape(-1))
    else:
        plan = WholePlan()
        pending = WholeSums(plan)
        held = WholeWeights(weights, parts)
    small = held.small
    (
        qv_bias_w, proj_bias_w, norm1_gain_w, norm1_bias_w, norm2_gain_w, norm2_bias_w,
        fc1_bias_w, fc2_bias_w, rel_height_w, rel_width_w,
    ) = [
        small[:, :, a:b].transpose(1, 0, 2).reshape(LAYERS, -1) for a, b in zip(cuts, cuts[1:])
    ]
    vec = jnp.stack(
        [norm1_gain_w, norm1_bias_w, qv_bias_w[:, :width], qv_bias_w[:, width:], proj_bias_w,
         norm2_gain_w, norm2_bias_w, fc2_bias_w], 1
    ).astype(F32)
    hidden_bias = fc1_bias_w.astype(F32)[:, None, :]
    ahead, back = relative_tables(rel_height_w, rel_width_w)
    keys_ahead, keys_back = key_tables()
    live = live_rows(slot_table)
    current = spread(windows)
    grad = spread(cotangent)
    whole = WholePlan()
    kept = []
    for layer in range(LAYERS):
        top = layer == LAYERS - 1
        after = held.before(f"attend_{layer}")
        if layer == 0:
            after = (*after, back)
        mid, h1, q, k, v, p, att, token = attend_forward(
            current, live, vec[layer], ahead[layer], keys_ahead, held.source(layer, "attend"),
            after,
        )
        held.passed(f"attend_{layer}", token)
        used = ("fc1",) if top else ("fc1", "fc2")
        after = held.before(f"mlp_{layer}")
        made = mlp_forward(
            whole, top, mid, live, vec[layer], hidden_bias[layer], grad,
            held.source(layer, *used), after,
        )
        following = None
        if top:
            h2, act, slope, top_sums, top_g2 = made
        else:
            following, h2, act, slope = made
        kept.append((current, mid, h1, q, k, v, p, att, h2, act, slope))
        current = following
    sums = [None] * LAYERS
    steps = {"scores_0": ("mlp",), "first_0": ("mlp",)}

    def ahead_of(name):
        return pending.advance(*steps.get(name, ()))

    for layer in reversed(range(LAYERS)):
        top = layer == LAYERS - 1
        x, mid, h1, q, k, v, p, att, h2, act, slope = kept[layer]
        if top:
            dmid, sums2, hsum, top_g1 = top_backward(
                whole, grad, mid, live, vec[layer], h2, slope, held.source(layer, "fc1", "fc2"),
                (),
            )
            sums3 = top_sums
        else:
            dh, sums3, hsum, *pair = hidden_backward(
                plan, grad, act, live, h2, slope, held.source(layer, "fc2"), ()
            )
            pending.add("mlp", pair)
            dmid, sums2 = middle_backward(
                grad, mid, vec[layer], dh, held.source(layer, "fc1"), ()
            )
        db, dq, dk, dv, sums1, rel = scores_backward(
            dmid, live, back[layer], keys_back, q, k, v, p, held.source(layer, "proj"),
            ahead_of(f"scores_{layer}"),
        )
        if top:
            grad, sums4, top_g = first_all_backward(
                whole, dmid, x, live, vec[layer], h1, att, db, dq, dk, dv,
                held.source(layer, "attend"), (),
            )
            top_sum = whole_sums(((top_g,), (top_g2, top_g1)))
        else:
            pair = weights_backward(plan, h1, att, db, dq, dk, dv, ())
            pending.add("attend", pair)
            grad, sums4 = first_backward(
                dmid, x, live, vec[layer], dq, dk, dv, held.source(layer, "attend"),
                ahead_of("first_0"),
            )
        rel = rel[:, :HD] + rel[:, HD:]
        rel = jnp.stack([rel[:RELS].reshape(8, -1), rel[HD : HD + RELS].reshape(8, -1)], 1)
        sums[layer] = (sums1 + sums2 + sums3 + sums4, hsum, rel)
    input_grad = gather_back(grad).astype(BF16)
    (qkv_grad, proj_grad, *small), (fc1_grad, fc2_grad) = pending.finish(sums, top_sum)
    output = gather_back(
        mlp_output(
            kept[-1][9], vec[-1], kept[-1][1], live, held.source(LAYERS - 1, "fc2"),
            (pending.token.reshape(1, -1),),
        )
    ).astype(BF16)
    qv, pb, n1g, n1b, n2g, n2b, f1b, f2b, rh, rw = small
    return (
        output, input_grad, qkv_grad, qv, proj_grad, pb, n1g, n1b, n2g, n2b, fc1_grad, f1b,
        fc2_grad, f2b, rh, rw,
    )


def solution(mesh):
    rows = P(("rep", "fsdp"), None)
    cube = P(None, "fsdp", None)
    flat = P(None, "fsdp")
    ring = mesh.shape["rep"] == 4 and mesh.shape["fsdp"] == 8
    return jax.shard_map(
        functools.partial(on_device, ring),
        mesh=mesh,
        in_specs=(
            rows, P(("rep", "fsdp")), rows, cube, flat, cube, flat, flat, flat, flat, flat, cube,
            flat, cube, flat, flat, flat,
        ),
        out_specs=(
            rows, rows, cube, flat, cube, flat, flat, flat, flat, flat, cube, flat, cube, flat,
            flat, flat,
        ),
        check_vma=False,
    )
```

```python
import functools

import jax
import jax.numpy as jnp
import numpy as np
from jax import lax
from jax.experimental import pallas as pl
from jax.experimental.pallas import tpu as pltpu
from jax.sharding import PartitionSpec as P

HEADS = 12
HD = 64
WINDOW = 14
SIDE = 64
LAYERS = 2
GRID = 5
RELS = 2 * WINDOW - 1
EPSILON = 1e-06
PITCH = 16
SPAN = WINDOW * PITCH
PAIRS = HEADS // 2
LANES = 2 * HD
F32 = jnp.float32
BF16 = jnp.bfloat16
CHUNK = 768
ROWS_STEP = 64
VMEM_LIMIT = 56 * 1024 * 1024
SLAB = 384
RIDERS = 8
LARGE = 256 * 1024


def dot_nn(a, b):
    return lax.dot_general(a, b, (((1,), (0,)), ((), ())), preferred_element_type=F32)


def dot_nt(a, b):
    return lax.dot_general(a, b, (((1,), (1,)), ((), ())), preferred_element_type=F32)


def dot_tn(a, b):
    return lax.dot_general(a, b, (((0,), (0,)), ((), ())), preferred_element_type=F32)


def norm_rows(values):
    centre = jnp.mean(values, -1, keepdims=True)
    centered = values - centre
    inverse = lax.rsqrt(jnp.mean(centered * centered, -1, keepdims=True) + EPSILON)
    return centered * inverse, inverse


def norm_back(grad, normed, inverse, gain):
    scaled = grad * gain
    return inverse * (
        scaled
        - jnp.mean(scaled, -1, keepdims=True)
        - normed * jnp.mean(scaled * normed, -1, keepdims=True)
    )


def each(count, step, body):
    def run(index, carry):
        body(pl.multiple_of(index * step, step))
        return carry

    lax.fori_loop(0, count, run, 0)


def each_index(count, body):
    def run(index, carry):
        body(index)
        return carry

    lax.fori_loop(0, count, run, 0)


def in_fours(count, body):
    def several(index):
        for i in range(4):
            body(4 * index + i)

    each_index(count // 4, several)


def half_lane():
    return lax.broadcasted_iota(jnp.int32, (SPAN, LANES), 1)


def split_heads(pair):
    lane = half_lane()
    zero = jnp.zeros_like(pair)
    return jnp.concatenate(
        [jnp.where(lane < HD, pair, zero), jnp.where(lane < HD, zero, pair)], axis=0
    )


def join_heads(stacked):
    return jnp.where(half_lane() < HD, stacked[:SPAN], stacked[SPAN:])


def shift_rows(table):
    by_row = jnp.concatenate(
        [
            pltpu.roll(table[i * PITCH : (i + 1) * PITCH], i, axis=1) if i else table[:PITCH]
            for i in range(WINDOW)
        ],
        axis=0,
    )
    by_col = pltpu.roll(
        table.reshape(WINDOW, PITCH, LANES), 0, axis=2, stride=1, stride_axis=1
    ).reshape(SPAN, LANES)
    return jnp.where(half_lane() < HD, by_row, by_col)


def key_tables():
    ahead = np.zeros((SPAN, LANES), np.float32)
    back = np.zeros((SPAN, LANES), np.float32)
    for k in range(WINDOW):
        for m in range(PITCH):
            row = k * PITCH + m
            ahead[row, WINDOW - 1 + k] = 1.0
            back[row, WINDOW - 1 - k] = 1.0
            if m < WINDOW:
                ahead[row, HD + WINDOW - 1 + m] = 1.0
                back[row, HD + WINDOW - 1 - m] = 1.0
            else:
                ahead[row, LANES - 1] = -1e30
    return jnp.asarray(ahead, BF16), jnp.asarray(back, BF16)


class Flow:
    def __init__(self, ins, in_sem, outs, out_sem):
        self.ins = {}
        for i, (given, taken) in enumerate(ins):
            copy = pltpu.make_async_copy(given, taken, in_sem.at[i])
            copy.start()
            self.ins[id(taken)] = copy
        self.outs = {
            id(made): pltpu.make_async_copy(made, given, out_sem.at[i])
            for i, (made, given) in enumerate(outs)
        }
        self.sent = []

    def need(self, *refs):
        for ref in refs:
            copy = self.ins.pop(id(ref), None)
            if copy is not None:
                copy.wait()

    def emit(self, *refs):
        for ref in refs:
            copy = self.outs.pop(id(ref), None)
            if copy is not None:
                copy.start()
                self.sent.append(copy)

    def finish(self):
        for copy in self.ins.values():
            copy.wait()
        for copy in self.outs.values():
            copy.start()
        for copy in (*self.outs.values(), *self.sent):
            copy.wait()


def attend_kernel(source, flow, *refs):
    (x_ref, live_ref, vec_ref, table_ref, keys_ref), refs = refs[:5], refs[5:]
    weight_refs, refs = refs[: source.count], refs[source.count :]
    (mid_ref, h1_ref, q_ref, k_ref, v_ref, p_ref, att_ref), refs = refs[:7], refs[7:]
    token_ref, w_ref, sem = refs
    token_ref[...] = jnp.zeros_like(token_ref)
    ready = source.load("attend", weight_refs, w_ref, sem)
    width = x_ref.shape[1]
    flow.need(x_ref)

    def first_norm(start):
        rows = pl.ds(start, ROWS_STEP)
        normed, _ = norm_rows(x_ref[rows, :].astype(F32))
        shaped = (normed * vec_ref[0:1, :] + vec_ref[1:2, :]) * live_ref[rows, :]
        h1_ref[rows, :] = shaped.astype(BF16)

    each(x_ref.shape[0] // ROWS_STEP, ROWS_STEP, first_norm)
    flow.emit(h1_ref)
    ready()
    for index, (out_ref, bias) in enumerate(((q_ref, 2), (k_ref, None), (v_ref, 3))):

        def project(start, index=index, out_ref=out_ref, bias=bias):
            cols = pl.ds(start, CHUNK)
            made = dot_nn(h1_ref[...], w_ref[index, :, cols])
            if bias is not None:
                made = made + vec_ref[bias : bias + 1, cols]
            out_ref[:, cols] = made.astype(BF16)

        each(width // CHUNK, CHUNK, project)
        flow.emit(out_ref)

    def attend(index):
        rows = pl.ds(pl.multiple_of(index // PAIRS * SPAN, SPAN), SPAN)
        cols = pl.ds(pl.multiple_of(index % PAIRS * LANES, LANES), LANES)
        queries = q_ref[rows, cols]
        offsets = dot_nn(queries, table_ref[...])
        lane = half_lane()
        sides = []
        for half in range(2):
            moved = shift_rows(offsets[:, half * LANES : (half + 1) * LANES])
            sides.append(jnp.where(lane == LANES - 1, 1.0, moved).astype(BF16))
        left = jnp.concatenate(
            [split_heads(queries) * HD ** (-0.5), jnp.concatenate(sides, axis=0)], axis=1
        )
        right = jnp.concatenate([k_ref[rows, cols], keys_ref[...]], axis=1)
        scores = dot_nt(left, right)
        shifted = jnp.exp(scores - jnp.max(scores, -1, keepdims=True))
        probs = shifted * (1.0 / jnp.sum(shifted, -1, keepdims=True))
        low = probs.astype(BF16)
        p_ref[index] = low
        att_ref[rows, cols] = join_heads(dot_nn(low, v_ref[rows, cols])).astype(BF16)

    in_fours(x_ref.shape[0] // SPAN * PAIRS, attend)
    flow.emit(p_ref, att_ref)

    def finish(start):
        cols = pl.ds(start, CHUNK)
        branch = dot_nn(att_ref[...], w_ref[3, :, cols]) + vec_ref[4:5, cols]
        mid_ref[:, cols] = x_ref[:, cols].astype(F32) + live_ref[...] * branch

    each(width // CHUNK, CHUNK, finish)


def mlp_kernel(plan, source, top, flow, *refs):
    (mid_ref, live_ref, vec_ref, bias_ref), refs = refs[:4], refs[4:]
    if top:
        (grad_ref,), refs = refs[:1], refs[1:]
    weight_refs, refs = refs[: source.count], refs[source.count :]
    if top:
        (h2_ref, act_ref, slope_ref, sums_ref), refs = refs[:4], refs[4:]
        sink_refs, refs = refs[: plan.sinks], refs[plan.sinks :]
        (w1_ref, dm_ref, sem), refs = refs[:3], refs[3:]
        sink = plan.sink(sink_refs, refs, False)
    else:
        out_ref, h2_ref, act_ref, slope_ref, w1_ref, w2_ref, sem, sem2 = refs
    ready1 = source.load("fc1", weight_refs, w1_ref, sem)
    if not top:
        ready2 = source.load("fc2", weight_refs, w2_ref, sem2)
    width = mid_ref.shape[1]
    hidden_width = act_ref.shape[1]
    flow.need(mid_ref)

    def second_norm(start):
        rows = pl.ds(start, ROWS_STEP)
        normed, _ = norm_rows(mid_ref[rows, :])
        h2_ref[rows, :] = (normed * vec_ref[5:6, :] + vec_ref[6:7, :]).astype(BF16)

    each(mid_ref.shape[0] // ROWS_STEP, ROWS_STEP, second_norm)
    flow.emit(h2_ref)
    ready1()

    def expand(index):
        start = pl.multiple_of(index * CHUNK, CHUNK)
        cols = pl.ds(start, CHUNK)
        inner = pl.ds(pl.multiple_of(start % width, CHUNK), CHUNK)
        hidden = dot_nn(h2_ref[...], w1_ref[start // width, :, inner]) + bias_ref[:, cols]
        below = 0.5 * (1.0 + lax.erf(hidden * (0.5**0.5)))
        bell = jnp.exp(-0.5 * hidden * hidden) * (0.5 / np.pi) ** 0.5
        act_ref[:, cols] = (hidden * below).astype(BF16)
        slope_ref[:, cols] = (below + hidden * bell).astype(BF16)

    each_index(hidden_width // CHUNK, expand)
    flow.emit(act_ref, slope_ref)
    if top:
        sums_ref[...] = jnp.zeros_like(sums_ref)
        flow.need(grad_ref)
        second_weight(grad_ref, live_ref, act_ref, dm_ref, sums_ref, sink)
        sink.wait()
    else:
        ready2()
        contract(act_ref, w2_ref, vec_ref, mid_ref, live_ref, out_ref)


def contract(act_ref, w2_ref, vec_ref, mid_ref, live_ref, out_ref):
    def run(start):
        cols = pl.ds(start, CHUNK)
        made = dot_nn(act_ref[...], w2_ref[:, cols]) + vec_ref[7:8, cols]
        out_ref[:, cols] = mid_ref[:, cols] + live_ref[...] * made

    each(out_ref.shape[1] // CHUNK, CHUNK, run)


def out_kernel(source, flow, act_ref, vec_ref, mid_ref, live_ref, *refs):
    weight_refs, (out_ref, w2_ref, sem) = refs[: source.count], refs[source.count :]
    source.load("fc2", weight_refs, w2_ref, sem)()
    flow.need(act_ref, mid_ref)
    contract(act_ref, w2_ref, vec_ref, mid_ref, live_ref, out_ref)


def second_weight(grad_ref, live_ref, act_ref, dm_ref, sums_ref, sink):
    dm_ref[...] = (live_ref[...] * grad_ref[...].astype(F32)).astype(BF16)
    sums_ref[7:8, :] = jnp.sum(dm_ref[...].astype(F32), 0, keepdims=True)

    def run(index):
        rows = pl.ds(pl.multiple_of(index * SLAB, SLAB), SLAB)
        sink.rows(index, dot_tn(act_ref[:, rows], dm_ref[...]).astype(BF16))

    each_index(act_ref.shape[1] // SLAB, run)
    sink.send_all()


def hidden_back(flow, ready, sink, h2_ref, slope_ref, dh_ref, hsum_ref, w2_ref, dm_ref):
    width = h2_ref.shape[1]
    hidden_width = slope_ref.shape[1]
    flow.need(slope_ref)
    ready()

    def inner_grad(start):
        cols = pl.ds(start, CHUNK)
        made = (dot_nt(dm_ref[...], w2_ref[cols, :]) * slope_ref[:, cols].astype(F32)).astype(BF16)
        dh_ref[:, cols] = made
        hsum_ref[:, cols] = jnp.sum(made.astype(F32), 0, keepdims=True)

    each(hidden_width // CHUNK, CHUNK, inner_grad)
    flow.emit(dh_ref)
    flow.need(h2_ref)
    for block in range(hidden_width // width):

        def first_weight(start, block=block):
            cols = pl.ds(start, CHUNK)
            outer = pl.ds(pl.multiple_of(block * width + start, CHUNK), CHUNK)
            sink.cols(block, cols, dot_tn(h2_ref[...], dh_ref[:, outer]).astype(BF16))

        each(width // CHUNK, CHUNK, first_weight)
        sink.send(block)


def hidden_back_kernel(plan, source, flow, *refs):
    (grad_ref, act_ref, live_ref, h2_ref, slope_ref), refs = refs[:5], refs[5:]
    weight_refs, refs = refs[: source.count], refs[source.count :]
    (dh_ref, sums_ref, hsum_ref), refs = refs[:3], refs[3:]
    sink_refs, (w2_ref, dm_ref, sem), refs = refs[:2], refs[2:5], refs[5:]
    more, sink = plan.two_sinks(sink_refs, refs, True)
    ready = source.load("fc2", weight_refs, w2_ref, sem)
    sums_ref[...] = jnp.zeros_like(sums_ref)
    flow.need(grad_ref, act_ref)
    second_weight(grad_ref, live_ref, act_ref, dm_ref, sums_ref, more)
    hidden_back(flow, ready, sink, h2_ref, slope_ref, dh_ref, hsum_ref, w2_ref, dm_ref)
    more.wait()
    sink.wait()


def middle_back_kernel(source, flow, *refs):
    (grad_ref, mid_ref, vec_ref, dh_ref), refs = refs[:4], refs[4:]
    weight_refs, refs = refs[: source.count], refs[source.count :]
    dmid_ref, sums_ref, w1_ref, ds_ref, sem = refs
    ready = source.load("fc1", weight_refs, w1_ref, sem)
    flow.need(dh_ref)
    sums_ref[...] = jnp.zeros_like(sums_ref)
    middle_back(
        flow, ready, grad_ref, mid_ref, vec_ref, dh_ref, dmid_ref, sums_ref, w1_ref, ds_ref
    )


def middle_back(
    flow, ready, grad_ref, mid_ref, vec_ref, dh_ref, dmid_ref, sums_ref, w1_ref, ds_ref
):
    width = mid_ref.shape[1]
    hidden_width = dh_ref.shape[1]
    ready()

    def back_in(start):
        rows = pl.ds(start, CHUNK)
        made = dot_nt(dh_ref[:, 0:width], w1_ref[0, rows, :])
        for block in range(1, hidden_width // width):
            made += dot_nt(
                dh_ref[:, block * width : (block + 1) * width], w1_ref[block, rows, :]
            )
        ds_ref[:, rows] = made

    each(width // CHUNK, CHUNK, back_in)
    flow.need(mid_ref, grad_ref)

    def back_norm(start):
        rows = pl.ds(start, ROWS_STEP)
        normed, inverse = norm_rows(mid_ref[rows, :])
        grad = ds_ref[rows, :]
        sums_ref[5:6, :] += jnp.sum(grad * normed, 0, keepdims=True)
        sums_ref[6:7, :] += jnp.sum(grad, 0, keepdims=True)
        dmid_ref[rows, :] = grad_ref[rows, :].astype(F32) + norm_back(
            grad, normed, inverse, vec_ref[5:6, :]
        )

    each(mid_ref.shape[0] // ROWS_STEP, ROWS_STEP, back_norm)


def top_back_kernel(plan, source, flow, *refs):
    (grad_ref, mid_ref, live_ref, vec_ref, h2_ref, slope_ref), refs = refs[:6], refs[6:]
    weight_refs, refs = refs[: source.count], refs[source.count :]
    (dmid_ref, sums_ref, hsum_ref), refs = refs[:3], refs[3:]
    sink_refs, refs = refs[: plan.sinks], refs[plan.sinks :]
    (w1_ref, w2_ref, dm_ref, dh_ref, ds_ref, sem, sem2), refs = refs[:7], refs[7:]
    sink = plan.sink(sink_refs, refs, False)
    ready2 = source.load("fc2", weight_refs, w2_ref, sem2)
    ready1 = source.load("fc1", weight_refs, w1_ref, sem)
    sums_ref[...] = jnp.zeros_like(sums_ref)
    flow.need(grad_ref)
    dm_ref[...] = (live_ref[...] * grad_ref[...].astype(F32)).astype(BF16)
    hidden_back(flow, ready2, sink, h2_ref, slope_ref, dh_ref, hsum_ref, w2_ref, dm_ref)
    middle_back(
        flow, ready1, grad_ref, mid_ref, vec_ref, dh_ref, dmid_ref, sums_ref, w1_ref, ds_ref
    )
    sink.wait()


def scores_back_kernel(source, flow, *refs):
    (
        dmid_ref, live_ref, table_ref, keys_ref, q_ref, k_ref, v_ref, p_ref,
    ), refs = refs[:8], refs[8:]
    weight_refs, refs = refs[: source.count], refs[source.count :]
    db_ref, dq_ref, dk_ref, dv_ref, sums_ref, rel_ref, w_ref, da_ref, sem = refs
    ready = source.load("proj", weight_refs, w_ref, sem)
    width = dmid_ref.shape[1]
    flow.need(dmid_ref)
    db_ref[...] = (live_ref[...] * dmid_ref[...]).astype(BF16)
    flow.emit(db_ref)
    sums_ref[...] = jnp.zeros_like(sums_ref)
    sums_ref[0:1, :] = jnp.sum(db_ref[...].astype(F32), 0, keepdims=True)
    rel_ref[...] = jnp.zeros_like(rel_ref)
    ready()

    def back_out(start):
        rows = pl.ds(start, CHUNK)
        da_ref[:, rows] = dot_nt(db_ref[...], w_ref[rows, :]).astype(BF16)

    each(width // CHUNK, CHUNK, back_out)
    flow.need(v_ref, p_ref, k_ref, q_ref)

    def attend(index):
        rows = pl.ds(pl.multiple_of(index // PAIRS * SPAN, SPAN), SPAN)
        cols = pl.ds(pl.multiple_of(index % PAIRS * LANES, LANES), LANES)
        low = p_ref[index]
        probs = low.astype(F32)
        outer = split_heads(da_ref[rows, cols])
        queries = split_heads(q_ref[rows, cols])
        d_probs = dot_nt(outer, v_ref[rows, cols])
        dv_ref[rows, cols] = dot_tn(low, outer).astype(BF16)
        mean = jnp.sum(d_probs * probs, -1, keepdims=True)
        d_scores = (probs * (d_probs - mean)).astype(BF16)
        both = dot_nn(d_scores, jnp.concatenate([k_ref[rows, cols], keys_ref[...]], axis=1))
        moved = [
            shift_rows(both[half * SPAN : (half + 1) * SPAN, LANES:]).astype(BF16)
            for half in range(2)
        ]
        rel_part = dot_nt(jnp.concatenate(moved, axis=1), table_ref[...])
        direct = join_heads(both[:, :LANES]) * HD ** (-0.5)
        dq_ref[rows, cols] = (direct + rel_part).astype(BF16)
        dk_ref[rows, cols] = (dot_tn(d_scores, queries) * HD ** (-0.5)).astype(BF16)
        rel_ref[...] += dot_tn(jnp.concatenate(moved, axis=0), queries)

    in_fours(dmid_ref.shape[0] // SPAN * PAIRS, attend)
    flow.emit(dq_ref, dk_ref, dv_ref)
    sums_ref[1:2, :] = jnp.sum(dq_ref[...].astype(F32), 0, keepdims=True)
    sums_ref[2:3, :] = jnp.sum(dv_ref[...].astype(F32), 0, keepdims=True)


def first_weights(flow, sink, h1_ref, att_ref, db_ref, dq_ref, dk_ref, dv_ref):
    pairs = ((h1_ref, dq_ref), (h1_ref, dk_ref), (h1_ref, dv_ref), (att_ref, db_ref))
    for index, (left_ref, right_ref) in enumerate(pairs):
        flow.need(left_ref, right_ref)

        def weight(start, index=index, left_ref=left_ref, right_ref=right_ref):
            cols = pl.ds(start, CHUNK)
            sink.cols(index, cols, dot_tn(left_ref[...], right_ref[:, cols]).astype(BF16))

        each(h1_ref.shape[1] // CHUNK, CHUNK, weight)
        sink.send(index)


def first_weights_kernel(plan, flow, *refs):
    sink = plan.sink(refs[6 : 6 + plan.sinks], refs[6 + plan.sinks :], True)
    first_weights(flow, sink, *refs[:6])
    sink.wait()


def first_back(
    flow, ready, dmid_ref, x_ref, live_ref, vec_ref, dq_ref, dk_ref, dv_ref, next_ref, sums_ref,
    w_ref, dh_ref,
):
    width = x_ref.shape[1]
    flow.need(dq_ref, dk_ref, dv_ref)
    ready()

    def back_in(start):
        rows = pl.ds(start, CHUNK)
        made = dot_nt(dq_ref[...], w_ref[0, rows, :])
        made += dot_nt(dk_ref[...], w_ref[1, rows, :])
        made += dot_nt(dv_ref[...], w_ref[2, rows, :])
        dh_ref[:, rows] = made * live_ref[...]

    each(width // CHUNK, CHUNK, back_in)
    flow.need(x_ref, dmid_ref)
    sums_ref[...] = jnp.zeros_like(sums_ref)

    def back_norm(start):
        rows = pl.ds(start, ROWS_STEP)
        normed, inverse = norm_rows(x_ref[rows, :].astype(F32))
        grad = dh_ref[rows, :]
        sums_ref[3:4, :] += jnp.sum(grad * normed, 0, keepdims=True)
        sums_ref[4:5, :] += jnp.sum(grad, 0, keepdims=True)
        next_ref[rows, :] = dmid_ref[rows, :] + norm_back(grad, normed, inverse, vec_ref[0:1, :])

    each(x_ref.shape[0] // ROWS_STEP, ROWS_STEP, back_norm)


def first_back_kernel(source, flow, *refs):
    ins, refs = refs[:7], refs[7:]
    weight_refs, refs = refs[: source.count], refs[source.count :]
    next_ref, sums_ref, w_ref, dh_ref, sem = refs
    ready = source.load("attend", weight_refs, w_ref, sem)
    first_back(flow, ready, *ins, next_ref, sums_ref, w_ref, dh_ref)


def first_all_kernel(plan, source, flow, *refs):
    (dmid_ref, x_ref, live_ref, vec_ref, h1_ref, att_ref, db_ref), refs = refs[:7], refs[7:]
    (dq_ref, dk_ref, dv_ref), refs = refs[:3], refs[3:]
    weight_refs, refs = refs[: source.count], refs[source.count :]
    (next_ref, sums_ref), refs = refs[:2], refs[2:]
    sink_refs, refs = refs[: plan.sinks], refs[plan.sinks :]
    (w_ref, dh_ref, sem), refs = refs[:3], refs[3:]
    sink = plan.sink(sink_refs, refs, True)
    ready = source.load("attend", weight_refs, w_ref, sem)
    first_weights(flow, sink, h1_ref, att_ref, db_ref, dq_ref, dk_ref, dv_ref)
    first_back(
        flow, ready, dmid_ref, x_ref, live_ref, vec_ref, dq_ref, dk_ref, dv_ref, next_ref,
        sums_ref, w_ref, dh_ref,
    )
    sink.wait()


VM = pl.BlockSpec(memory_space=pltpu.VMEM)
ANY = pl.BlockSpec(memory_space=pltpu.HBM)


def shape(dims, kind):
    return jax.ShapeDtypeStruct(tuple(dims), kind)


class Source:
    def __init__(self, **parts):
        self.parts = parts
        self.arrays = []
        self.places = {}
        for name, (arrays, _, _) in parts.items():
            found = []
            for array in arrays:
                known = [i for i, other in enumerate(self.arrays) if other is array]
                if not known:
                    known = [len(self.arrays)]
                    self.arrays.append(array)
                found.append(known[0])
            self.places[name] = found
        self.count = len(self.arrays)

    def semaphores(self, name):
        whole = self.parts[name][1] is None
        return pltpu.SemaphoreType.DMA((4 if whole else 8 if name == "proj" else 32,))

    def load(self, name, refs, target, sem):
        arrays, offset, rotated = self.parts[name]
        refs = [refs[i] for i in self.places[name]]
        if offset is not None and name == "proj":
            return load_proj(refs, target, offset, rotated, sem)
        if offset is None:
            pairs = whole_pairs(name, refs, target)
        else:
            pairs = [pair for _, _, pair in piece_pairs(name, refs, target, offset, rotated)]
        copies = [
            pltpu.make_async_copy(given, taken, sem.at[i])
            for i, (given, taken) in enumerate(pairs)
        ]
        for copy in copies:
            copy.start()

        def ready():
            for copy in copies:
                copy.wait()

        return ready


def whole_pairs(name, refs, target):
    if name == "fc2":
        return [(refs[0], target)]
    if name == "proj":
        return [(refs[1], target)]
    width = target.shape[1]
    pairs = []
    for ref in refs:
        for start in range(0, ref.shape[1], width):
            pairs.append((ref.at[:, pl.ds(start, width)], target.at[len(pairs)]))
    return pairs


def position():
    shard = lax.axis_index("fsdp")
    return lax.axis_index("rep"), shard >> 1, shard & 1


def piece_pairs(name, refs, target, offset, rotated):
    rep, level, core = position()
    pairs = []
    rows = target.shape[-2] // 8
    span = rows // 4 if name == "fc2" else rows
    for parity in range(2):
        for part, (away, levels) in enumerate(
            ((0, range(4)), (1, range(4)), (2, range(4)), (3, range(2)), (3, range(2, 4)))
        ):
            ref = refs[parity * 5 + part]
            for place, step in enumerate(levels):
                source_level = (level - step) & 3 if rotated else step
                shard = source_level * 2 + (core ^ parity)
                kind = rep ^ away
                if name == "fc2":
                    start = pl.multiple_of(shard * rows + kind * span, 16)
                    taken = target.at[pl.ds(start, span), :]
                else:
                    start = pl.multiple_of(shard * span, 16)
                    whole = target if name == "proj" else target.at[kind]
                    taken = whole.at[pl.ds(start, span), :]
                given = ref.at[place, pl.ds(offset, span), :]
                pairs.append((away, parity * 4 + step, (given, taken)))
    return pairs


def load_proj(refs, target, offset, rotated, sem):
    rep = lax.axis_index("rep")
    pairs = piece_pairs("proj", refs, target, offset, rotated)
    for away in range(4):

        @pl.when((rep ^ away) == 3)
        def _(away=away):
            for other, slot, pair in pairs:
                if other == away:
                    pltpu.make_async_copy(*pair, sem.at[slot]).start()

    def ready():
        for away, slot, pair in pairs:
            if away == 0:
                pltpu.make_async_copy(*pair, sem.at[slot]).wait()

    return ready


class WholeSink:
    def __init__(self, refs, scratch):
        self.ref = refs[0]
        self.held, self.sem = scratch[:2]
        self.sent = []

    def rows(self, index, value):
        self.held[pl.ds(pl.multiple_of(index * SLAB, SLAB), SLAB), :] = value

    def cols(self, block, cols, value):
        self.held[block, :, cols] = value

    def copy(self, given, taken):
        copy = pltpu.make_async_copy(given, taken, self.sem.at[len(self.sent)])
        copy.start()
        self.sent.append(copy)

    def send(self, block):
        self.copy(self.held.at[block], self.ref.at[block])

    def send_all(self):
        self.copy(self.held, self.ref)

    def wait(self):
        for copy in self.sent:
            copy.wait()


class PieceSink:
    def __init__(self, refs, scratch, rotated, offset=0):
        self.refs, self.rotated, self.offset = refs, rotated, offset
        self.held, self.sem = scratch[:2]
        self.position = position()
        self.sent = []

    def rows(self, index, value):
        span = self.held.shape[3]
        for block in range(4):
            self.held[index & 1, block, index >> 1] = value[block * span : (block + 1) * span]

    def cols(self, block, cols, value):
        span = self.held.shape[3]
        for shard in range(8):
            self.held[shard & 1, block, shard >> 1, :, cols] = value[
                shard * span : (shard + 1) * span
            ]

    def send(self, block):
        rep, level, core = self.position
        for parity in range(2):
            given = self.held.at[core ^ parity, block]
            span = self.held.shape[3]
            taken = self.refs[parity].at[rep ^ block, :, pl.ds(self.offset, span)]
            moves = [(given, taken)]
            if self.rotated:
                moves = [(given.at[(level + step) & 3], taken.at[step]) for step in range(4)]
            for move in moves:
                copy = pltpu.make_async_copy(*move, self.sem.at[len(self.sent)])
                copy.start()
                self.sent.append(copy)

    def send_all(self):
        for block in range(4):
            self.send(block)

    def wait(self):
        for copy in self.sent:
            copy.wait()


class WholePlan:
    sinks = 1

    def sink(self, refs, scratch, rotated=False):
        return WholeSink(refs, scratch)

    def sink_outs(self, dims):
        return [shape(dims, BF16)], [ANY], [pltpu.VMEM(dims, BF16), pltpu.SemaphoreType.DMA((4,))]

    def two_sinks(self, refs, scratch, rotated):
        return WholeSink(refs[:1], scratch), WholeSink(refs[1:], scratch[2:])

    def two_outs(self, hidden, width):
        one = self.sink_outs((hidden, width))
        two = self.sink_outs((hidden // width, width, width))
        return one[0] + two[0], one[1] + two[1], one[2] + two[2]


class PiecePlan:
    sinks = 2

    def sink(self, refs, scratch, rotated=False):
        return PieceSink(refs, scratch, rotated)

    def sink_outs(self, dims):
        width = dims[-1]
        span = int(np.prod(dims)) // width // 32
        outs = [shape((4, 4, span, width), BF16)] * 2
        scratch = [pltpu.VMEM((2, 4, 4, span, width), BF16), pltpu.SemaphoreType.DMA((32,))]
        return outs, [ANY] * 2, scratch

    def two_sinks(self, refs, scratch, rotated):
        span = scratch[0].shape[3]
        return PieceSink(refs, scratch, rotated), PieceSink(refs, scratch[2:], rotated, span)

    def two_outs(self, hidden, width):
        span = hidden // 32
        outs = [shape((4, 4, 2 * span, width), BF16)] * 2
        scratch = [pltpu.VMEM((2, 4, 4, span, width), BF16), pltpu.SemaphoreType.DMA((32,))] * 2
        return outs, [ANY] * 2, scratch


def large(array):
    return int(np.prod(array.shape)) * np.dtype(array.dtype).itemsize >= LARGE


def call(kernel, resident, source, outs, scratch, micros, sinks=(), after=()):
    sink_outs, sink_specs, sink_scratch = [], [], []
    for more_outs, more_specs, more_scratch in sinks:
        sink_outs += more_outs
        sink_specs += more_specs
        sink_scratch += more_scratch
    in_moves = [i for i, a in enumerate(resident) if large(a)]
    out_moves = [i for i, a in enumerate(outs) if large(a)]
    buffers = [pltpu.VMEM(resident[i].shape, resident[i].dtype) for i in in_moves]
    buffers += [pltpu.VMEM(outs[i].shape, outs[i].dtype) for i in out_moves]
    semaphores = [
        pltpu.SemaphoreType.DMA((max(len(moves), 1),)) for moves in (in_moves, out_moves)
    ]
    count = len(resident)
    first = count + source.count

    def body(*refs):
        ins, weights = list(refs[:count]), refs[count:first]
        refs = refs[first + len(after) :]
        made, refs = list(refs[: len(outs)]), refs[len(outs) :]
        sunk, refs = refs[: len(sink_outs)], refs[len(sink_outs) :]
        held, refs = refs[: len(buffers)], refs[len(buffers) :]
        in_sem, out_sem, *rest = refs
        in_held, out_held = held[: len(in_moves)], held[len(in_moves) :]
        flow = Flow(
            [(ins[i], ref) for i, ref in zip(in_moves, in_held)],
            in_sem,
            [(ref, made[i]) for i, ref in zip(out_moves, out_held)],
            out_sem,
        )
        for i, ref in zip(in_moves, in_held):
            ins[i] = ref
        for i, ref in zip(out_moves, out_held):
            made[i] = ref
        kernel(flow, *ins, *weights, *made, *sunk, *rest)
        flow.finish()

    run = pl.pallas_call(
        body,
        out_shape=tuple([*outs, *sink_outs]),
        in_specs=[ANY if large(a) else VM for a in resident]
        + [ANY] * (source.count + len(after)),
        out_specs=tuple([*[ANY if large(a) else VM for a in outs], *sink_specs]),
        scratch_shapes=[*buffers, *semaphores, *scratch, *sink_scratch],
        compiler_params=pltpu.CompilerParams(vmem_limit_bytes=VMEM_LIMIT),
        cost_estimate=pl.CostEstimate(
            flops=int(micros * 1e10), bytes_accessed=1 << 20, transcendentals=0
        ),
    )
    return run(*resident, *source.arrays, *after)


def attend_forward(x, live, vec, table, keys, source, after):
    rows, width = x.shape
    outs = (
        shape((rows, width), F32),
        *[shape((rows, width), BF16)] * 4,
        shape((rows // SPAN * PAIRS, 2 * SPAN, SPAN), BF16),
        shape((rows, width), BF16),
        shape((8, LANES), F32),
    )
    scratch = [pltpu.VMEM((4, width, width), BF16), source.semaphores("attend")]
    return call(
        functools.partial(attend_kernel, source),
        (x, live, vec, table, keys), source, outs, scratch, 20, (), after,
    )


def mlp_forward(plan, top, mid, live, vec, bias, grad, source, after):
    rows, width = mid.shape
    hidden = bias.shape[1]
    outs = [
        shape((rows, width), BF16), shape((rows, hidden), BF16), shape((rows, hidden), BF16),
    ]
    scratch = [pltpu.VMEM((hidden // width, width, width), BF16)]
    resident = [mid, live, vec, bias]
    sinks = []
    if top:
        resident.append(grad)
        outs.append(shape((8, width), F32))
        scratch += [pltpu.VMEM((rows, width), BF16), source.semaphores("fc1")]
        sinks.append(plan.sink_outs((hidden, width)))
    else:
        outs.insert(0, shape((rows, width), F32))
        scratch += [
            pltpu.VMEM((hidden, width), BF16), source.semaphores("fc1"),
            source.semaphores("fc2"),
        ]
    return call(
        functools.partial(mlp_kernel, plan, source, top),
        resident, source, outs, scratch, 16, sinks, after,
    )


def mlp_output(act, vec, mid, live, source, after):
    hidden, width = act.shape[1], mid.shape[1]
    scratch = [pltpu.VMEM((hidden, width), BF16), source.semaphores("fc2")]
    return call(
        functools.partial(out_kernel, source), (act, vec, mid, live), source,
        [shape(mid.shape, F32)], scratch, 5, (), after,
    )[0]


def hidden_backward(plan, grad, act, live, h2, slope, source, after):
    rows, width = h2.shape
    hidden = slope.shape[1]
    outs = [shape((rows, hidden), BF16), shape((8, width), F32), shape((1, hidden), F32)]
    scratch = [
        pltpu.VMEM((hidden, width), BF16), pltpu.VMEM((rows, width), BF16),
        source.semaphores("fc2"),
    ]
    return call(
        functools.partial(hidden_back_kernel, plan, source),
        (grad, act, live, h2, slope), source, outs, scratch, 18,
        [plan.two_outs(hidden, width)], after,
    )


def top_backward(plan, grad, mid, live, vec, h2, slope, source, after):
    rows, width = mid.shape
    hidden = slope.shape[1]
    outs = [shape((rows, width), F32), shape((8, width), F32), shape((1, hidden), F32)]
    scratch = [
        pltpu.VMEM((hidden // width, width, width), BF16), pltpu.VMEM((hidden, width), BF16),
        pltpu.VMEM((rows, width), BF16), pltpu.VMEM((rows, hidden), BF16),
        pltpu.VMEM((rows, width), F32), source.semaphores("fc1"), source.semaphores("fc2"),
    ]
    return call(
        functools.partial(top_back_kernel, plan, source),
        (grad, mid, live, vec, h2, slope), source, outs, scratch, 19,
        [plan.sink_outs((hidden // width, width, width))], after,
    )


def middle_backward(grad, mid, vec, dh, source, after):
    rows, width = mid.shape
    hidden = dh.shape[1]
    outs = [shape((rows, width), F32), shape((8, width), F32)]
    scratch = [
        pltpu.VMEM((hidden // width, width, width), BF16), pltpu.VMEM((rows, width), F32),
        source.semaphores("fc1"),
    ]
    return call(
        functools.partial(middle_back_kernel, source),
        (grad, mid, vec, dh), source, outs, scratch, 10, (), after,
    )


def scores_backward(dmid, live, table, keys, q, k, v, p, source, after):
    rows, width = dmid.shape
    outs = [*[shape((rows, width), BF16)] * 4, shape((8, width), F32), shape((LANES, LANES), F32)]
    scratch = [
        pltpu.VMEM((width, width), BF16), pltpu.VMEM((rows, width), BF16),
        source.semaphores("proj"),
    ]
    return call(
        functools.partial(scores_back_kernel, source),
        (dmid, live, table, keys, q, k, v, p), source, outs, scratch, 15, (), after,
    )


def weights_backward(plan, h1, att, db, dq, dk, dv, after):
    width = h1.shape[1]
    return call(
        functools.partial(first_weights_kernel, plan), (h1, att, db, dq, dk, dv),
        Source(), [], [], 8, [plan.sink_outs((4, width, width))], after,
    )


def first_backward(dmid, x, live, vec, dq, dk, dv, source, after):
    rows, width = x.shape
    outs = [shape((rows, width), F32), shape((8, width), F32)]
    scratch = [
        pltpu.VMEM((4, width, width), BF16), pltpu.VMEM((rows, width), F32),
        source.semaphores("attend"),
    ]
    return call(
        functools.partial(first_back_kernel, source),
        (dmid, x, live, vec, dq, dk, dv), source, outs, scratch, 10, (), after,
    )


def first_all_backward(plan, dmid, x, live, vec, h1, att, db, dq, dk, dv, source, after):
    rows, width = x.shape
    outs = [shape((rows, width), F32), shape((8, width), F32)]
    scratch = [
        pltpu.VMEM((4, width, width), BF16), pltpu.VMEM((rows, width), F32),
        source.semaphores("attend"),
    ]
    return call(
        functools.partial(first_all_kernel, plan, source),
        (dmid, x, live, vec, h1, att, db, dq, dk, dv), source, outs, scratch, 14,
        [plan.sink_outs((4, width, width))], after,
    )


def live_rows(slot_table):
    places = jnp.arange(PITCH, dtype=jnp.int32)
    rows_inside = slot_table[:, None] // GRID * WINDOW + places[None, :WINDOW] < SIDE
    cols_inside = slot_table[:, None] % GRID * WINDOW + places[None, :] < SIDE
    cols_inside = cols_inside & (places < WINDOW)[None, :]
    both_inside = rows_inside[:, :, None] & cols_inside[:, None, :]
    return both_inside.astype(F32).reshape(slot_table.shape[0] * SPAN, 1)


def spread(values):
    width = values.shape[1]
    grid = values.reshape(-1, WINDOW, width)
    return jnp.pad(grid, ((0, 0), (0, PITCH - WINDOW), (0, 0))).reshape(-1, width)


def gather_back(values):
    width = values.shape[1]
    return values.reshape(-1, PITCH, width)[:, :WINDOW].reshape(-1, width)


def relative_tables(rel_height, rel_width):
    stacked = jnp.stack([rel_height, rel_width], 1).reshape(LAYERS, 2, RELS, HD)

    def spread_table(rows):
        padded = jnp.pad(rows, ((0, 0), (0, 0), (0, HD - RELS), (0, 0)))
        one = padded.reshape(LAYERS, LANES, HD).transpose(0, 2, 1)
        none = jnp.zeros_like(one)
        return jnp.concatenate(
            [jnp.concatenate([one, none], 2), jnp.concatenate([none, one], 2)], 1
        )

    return spread_table(stacked[:, :, ::-1]), spread_table(stacked)


def whole_weights(weights):
    qkv, proj, fc1, fc2 = weights
    layers = []
    for layer in range(LAYERS):
        q, p, a, b = (
            lax.all_gather(w[layer], "fsdp", axis=0, tiled=True) for w in (qkv, proj, fc1, fc2)
        )
        layers.append(
            dict(attend=((q, p), None, False), proj=((q, p), None, False), fc1=((a,), None, False), fc2=((b,), None, False))
        )
    return layers


def whole_small(parts):
    packed = jnp.concatenate(parts, axis=1)
    return lax.all_gather(packed, "fsdp", axis=0, tiled=False)


def whole_reduce(value, axis):
    return lax.psum(lax.psum_scatter(value, "fsdp", scatter_dimension=axis, tiled=True), "rep")


def whole_sums(grads):
    (g,), (g2, g1) = grads
    return whole_reduce(g, 1), whole_reduce(g1, 1), whole_reduce(g2, 0)


def named(g, g1, g2):
    return jnp.concatenate([g[0], g[1], g[2]], 1), g[3], jnp.concatenate(list(g1), 1), g2


def permute(value, axis, move):
    return lax.ppermute(value, axis, [(i, move(i)) for i in range({"rep": 4, "fsdp": 8}[axis])])


def to_x(value):
    return permute(value, "rep", lambda i: i ^ 1)


def to_y(value):
    return permute(value, "rep", lambda i: i ^ 2)


def to_xy(value):
    return permute(value, "rep", lambda i: i ^ 3)


def to_core(value):
    return permute(value, "fsdp", lambda i: i ^ 1)


def to_level(value, step):
    return permute(value, "fsdp", lambda i: (i + 2 * step) % 8)


LEVELS = [[0, 2, 4, 6], [1, 3, 5, 7]]


def nothing(value):
    return jnp.minimum(jnp.abs(value), 0)


def swap(value, flag, axis):
    first = lax.slice_in_dim(value, 0, 1, axis=axis)
    second = lax.slice_in_dim(value, 1, 2, axis=axis)
    return jnp.where(flag == 1, jnp.concatenate([second, first], axis), value)


def by_replica(value, rep):
    rest = value.shape[1:]
    value = value.reshape(2, 2, *rest)
    value = swap(swap(value, rep & 1, 1), rep >> 1, 0)
    return value.reshape(4, *rest)


def turn(value, start, axis):
    size = value.shape[axis]
    return lax.dynamic_slice_in_dim(
        jnp.concatenate([value, value], axis), start, size, axis
    )


def own_blocks(weights, layer, rep):
    qkv, proj, fc1, fc2 = (w[layer] for w in weights)
    width = proj.shape[1]
    span = proj.shape[0]
    first = lax.dynamic_slice_in_dim(jnp.concatenate([qkv, proj], 1), rep * width, width, 1)
    second = lax.dynamic_slice_in_dim(fc1, rep * width, width, 1)
    third = lax.dynamic_slice_in_dim(fc2, rep * span, span, 0)
    return first, second, third


class Across:
    def __init__(self, held):
        self.held = held
        self.x, self.y = to_x(held), to_y(held)

    def cross(self, token=None):
        low, high = self.y[:2], self.x[2:]
        if token is not None:
            low, high = low + token, high + token
        self.low, self.high = to_x(low), to_y(high)
        return low, high

    def finish(self, token=None):
        low, high = self.low, self.high
        if token is not None:
            low, high = low + token, high + token
        pieces = (self.held, self.x, self.y, low, high)
        return pieces + tuple(to_core(piece) for piece in pieces)


class PieceWeights:
    def __init__(self, weights, small):
        rep, level, core = position()
        blocks = [own_blocks(weights, layer, rep) for layer in range(LAYERS)]
        span, width = blocks[0][0].shape
        size = small.shape[0] // 4
        rider = lax.dynamic_slice_in_dim(small, rep * size, size, 0)
        rider = jnp.pad(rider, (0, RIDERS * width - size)).reshape(RIDERS, width)
        first = jnp.concatenate([*blocks[0][:2], rider], 0)[None]
        self.span = span
        held = jnp.concatenate([first] + [to_level(first, step) for step in (1, 2, 3)], 0)
        self.rest = lax.all_gather(
            jnp.concatenate([blocks[0][2], blocks[1][0]], 0) + nothing(jnp.max(jnp.abs(held[1:, 0, 0]))), "fsdp",
            axis=0, tiled=True, axis_index_groups=LEVELS,
        ).reshape(4, 2 * span, width)
        self.fc1 = lax.all_gather(
            weights[2][1] + nothing(self.rest[0, 0, 0]), "fsdp", axis=0, tiled=True
        )
        self.top = weights[3][1]
        one = Across(held)
        one.cross()
        self.one = one.finish()
        riders = jnp.stack(
            [
                jnp.concatenate([t[:, 2 * span :] for t in self.one[5 * p : 5 * p + 5]], 0).reshape(
                    4, 4, RIDERS * width
                )[:, :, :size]
                for p in range(2)
            ]
        )
        riders = by_replica(swap(riders, core, 0).transpose(1, 0, 2, 3), rep)
        turned = jnp.concatenate([riders[:, :, i : i + 1] for i in (3, 2, 1, 0)], 2)
        riders = turn(turned, 3 - level, 2)
        self.small = riders.transpose(2, 1, 0, 3).reshape(8, LAYERS, -1)

    def before(self, name):
        if name == "attend_0":
            self.next = Across(self.rest)
            return (self.rest,)
        if name == "mlp_0":
            self.two = self.next.finish()
        return ()

    def passed(self, name, token):
        if name == "attend_0":
            token = token[0, 0].astype(BF16)
            self.next.cross(token)
            self.fc2 = lax.all_gather(self.top + token, "fsdp", axis=0, tiled=True)

    def source(self, layer, *names):
        if layer == 0:
            parts = dict(
                attend=lambda: (self.one, 0, True),
                proj=lambda: (self.one, 0, True),
                fc1=lambda: (self.one, self.span, True),
                fc2=lambda: (self.two, 0, False),
            )
        else:
            parts = dict(
                attend=lambda: (self.two, self.span, False),
                proj=lambda: (self.two, self.span, False),
                fc1=lambda: ((self.fc1,), None, False),
                fc2=lambda: ((self.fc2,), None, False),
            )
        return Source(**{name: parts[name]() for name in names})


class WholeWeights:
    def __init__(self, weights, small):
        self.small = whole_small(small)
        self.layers = whole_weights(weights)

    def before(self, name):
        return ()

    def passed(self, name, token):
        pass

    def source(self, layer, *names):
        return Source(**{name: self.layers[layer][name] for name in names})


class ReplicaSum:
    def __init__(self, *pairs):
        self.pairs = [(keep, to_core(send)) for keep, send in pairs]
        self.step = 0

    def both(self, away, part):
        sums = [
            keep[away, part].astype(F32) + got[away, part].astype(F32) for keep, got in self.pairs
        ]
        return sums[0] if len(sums) == 1 else jnp.concatenate(sums, -2)

    def advance(self, hold=0):
        low, high = slice(0, 2), slice(2, 4)
        self.step += 1
        if self.step == 1:
            send_x = (self.both(slice(1, 4, 2), low) + hold).astype(BF16)
            send_y = (self.both(slice(2, 4), high) + hold).astype(BF16)
            self.x, self.y = to_x(send_x), to_y(send_y)
            return [send_x, send_y]
        if self.step == 2:
            send_y = (self.both(2, low) + self.x[1].astype(F32) + hold).astype(BF16)
            send_x = (self.both(1, high) + self.y[1].astype(F32) + hold).astype(BF16)
            self.last_y, self.last_x = to_y(send_y), to_x(send_x)
            return [send_x, send_y]
        if self.step == 4:
            low, high = self.result
            sends = (low[1], high[0], high[1])
            self.levels = [to_level(send, step + 1) for step, send in enumerate(sends)]
            return list(sends)
        if self.step == 5:
            total = self.result[0][0].astype(F32)
            for got in self.levels:
                total = total + got.astype(F32)
            self.total = total.astype(BF16)
            return [self.total]
        self.result = [
            (self.both(0, low) + self.x[0].astype(F32) + self.last_y.astype(F32)).astype(BF16),
            (self.both(0, high) + self.y[0].astype(F32) + self.last_x.astype(F32)).astype(BF16),
        ]
        return self.result


class ReplicaAll:
    def __init__(self, *parts):
        self.parts = list(parts)
        self.moves = [to_x, to_y]
        self.got = None

    def advance(self, hold=0):
        if self.got is not None:
            self.add(hold)
        else:
            self.parts = [part + jnp.asarray(hold, BF16) for part in self.parts]
        self.got = [move(part) for move, part in zip(self.moves, self.parts)]
        return self.parts

    def add(self, hold=0):
        self.moves = self.moves[::-1]
        self.parts = [
            (part.astype(F32) + got.astype(F32) + hold).astype(BF16)
            for part, got in zip(self.parts, self.got)
        ]


class PieceSums:
    def __init__(self, plan):
        self.plan = plan
        self.sums = {}

    def add(self, name, pair):
        self.sums[name] = ReplicaSum(pair)

    def add_top(self, g2, g1, g):
        g2 = lax.psum_scatter(g2, "fsdp", scatter_dimension=0, tiled=True)
        g1 = lax.psum_scatter(g1, "fsdp", scatter_dimension=1, tiled=True)
        g = lax.psum_scatter(g, "fsdp", scatter_dimension=1, tiled=True)
        half = g2.shape[0] // 2
        self.sums["top"] = ReplicaAll(g2[:half], g2[half:])
        self.sums["next"] = ReplicaAll(g1, g)

    def advance(self, hold, *names):
        found = []
        for name in names:
            found += self.sums[name].advance(hold)
        return found

    def finish(self, sums):
        last, mlp, top, following = (
            self.sums[name] for name in ("attend", "mlp", "top", "next")
        )
        riders = ReplicaSum(pack_riders(self.plan, sums, mlp.advance()))
        last.advance()
        for _ in range(3):
            riders.advance()
        mlp.advance()
        mlp.advance()
        crossed = last.advance()[0]
        last.advance()
        first = last.result[0][0, 0, 0]
        last.result = [jnp.concatenate(pair, 1) for pair in zip(last.result, riders.result)]
        last.advance()
        following.advance(nothing(crossed[0, 0, 0]))
        late = to_replicas(mlp.total + nothing(first))
        last.advance()
        self.token = last.total[:1]
        following.advance()
        following.add()
        top.add()
        big = assemble_late((*top.parts, following.parts[0]), late)
        return assemble_last(to_replicas(last.total), following.parts[1:]), big


def to_replicas(value):
    return value, to_x(value), to_y(value), to_xy(value)


def load_replicas(refs, held, sem):
    rep = lax.axis_index("rep")
    copies = [
        pltpu.make_async_copy(ref, held.at[rep ^ away], sem.at[away])
        for away, ref in enumerate(refs)
    ]
    for copy in copies:
        copy.start()
    return copies


def late_kernel(flow, low_ref, high_ref, g1_ref, *refs):
    held, sem = refs[6:]
    fc1_ref, fc2_ref = refs[4:6]
    copies = load_replicas(refs[:4], held, sem)
    width = fc2_ref.shape[2]
    span = g1_ref.shape[1]
    flow.need(low_ref, high_ref, g1_ref)
    half = low_ref.shape[0]
    fc2_ref[1, :half] = low_ref[...].astype(F32)
    fc2_ref[1, half:] = high_ref[...].astype(F32)
    for block in range(4):
        fc1_ref[1, :, block * width : (block + 1) * width] = g1_ref[block].astype(F32)
    for copy in copies:
        copy.wait()
    for block in range(4):
        fc1_ref[0, :, block * width : (block + 1) * width] = held[block, span:].astype(F32)
        fc2_ref[0, block * span : (block + 1) * span, :] = held[block, :span].astype(F32)


def assemble_late(top, late):
    _, span, width = top[2].shape
    return call(
        late_kernel, top, Pieces(late),
        [shape((LAYERS, span, 4 * width), F32), shape((LAYERS, 4 * span, width), F32)],
        [pltpu.VMEM((4, *late[0].shape), BF16), pltpu.SemaphoreType.DMA((4,))], 4,
    )


class Pieces:
    def __init__(self, arrays):
        self.arrays, self.count = arrays, len(arrays)


def last_kernel(flow, g_ref, *refs):
    last_refs, refs = refs[:4], refs[4:]
    (qkv_ref, proj_ref), refs = refs[:2], refs[2:]
    small_refs, (held, sem) = refs[:10], refs[10:]
    copies = load_replicas(last_refs, held, sem)
    width = proj_ref.shape[2]
    span = g_ref.shape[1]
    flow.need(g_ref)

    def put(layer, blocks):
        for i, block in enumerate(blocks[:3]):
            qkv_ref[layer, :, i * width : (i + 1) * width] = block.astype(F32)
        proj_ref[layer] = blocks[3].astype(F32)

    put(1, [g_ref[i] for i in range(4)])
    for copy in copies:
        copy.wait()
    put(0, [held[i, :span] for i in range(4)])
    unit = width // 8
    heads = held[0, span:].astype(F32)
    others = held[1, span:].astype(F32)
    rel = held[2, span:].astype(F32)
    qv, pb, n1g, n1b, n2g, n2b, f1b, f2b, rh, rw = small_refs
    size = rh.shape[1]
    for layer in range(LAYERS):
        for ref, row in ((pb, 0), (n1g, 3), (n1b, 4), (n2g, 5), (n2b, 6), (f2b, 7)):
            ref[layer : layer + 1, :] = heads[row : row + 1, layer * unit : (layer + 1) * unit]
        qv[layer : layer + 1, :] = others[layer : layer + 1, : 2 * unit]
        f1b[layer : layer + 1, :] = others[layer : layer + 1, 2 * unit : 6 * unit]
        rh[layer : layer + 1, :] = rel[2 * layer : 2 * layer + 1, :size]
        rw[layer : layer + 1, :] = rel[2 * layer + 1 : 2 * layer + 2, :size]


def assemble_last(last, parts):
    _, span, width = parts[0].shape
    unit = width // 8
    sizes = (2 * unit, *[unit] * 5, 4 * unit, unit, RELS * HD // 8, RELS * HD // 8)
    outs = [shape((LAYERS, span, 3 * width), F32), shape((LAYERS, span, width), F32)]
    outs += [shape((LAYERS, size), F32) for size in sizes]
    return call(
        last_kernel, parts, Pieces(last), outs,
        [pltpu.VMEM((4, *last[0].shape), BF16), pltpu.SemaphoreType.DMA((4,))], 4,
    )


def pack_kernel(plan, flow, *refs):
    (
        (heads_ref, hidden_ref, rel_ref), (heads1_ref, hidden1_ref, rel1_ref)
    ), refs = (refs[:3], refs[3:6]), refs[6:]
    sink = plan.sink(refs[: plan.sinks], refs[plan.sinks :], True)
    held = sink.held
    held[...] = jnp.zeros_like(held)
    layers = ((heads_ref, hidden_ref, rel_ref), (heads1_ref, hidden1_ref, rel1_ref))
    span = heads_ref.shape[1] // 8
    for layer, (heads, hidden, rel) in enumerate(layers):
        for shard in range(8):
            core, level = shard & 1, shard >> 1
            cut = heads[:, shard * span : (shard + 1) * span]
            held[core, 0, level, :, layer * span : (layer + 1) * span] = cut.astype(BF16)
            first = shard % 4 * 2 * span
            row = 1 if shard < 4 else 2
            pair = heads[row : row + 1, first : first + 2 * span]
            held[core, 1, level, layer : layer + 1, 0 : 2 * span] = pair.astype(BF16)
            start = shard * 4 * span
            held[core, 1, level, layer : layer + 1, 2 * span : 6 * span] = hidden[
                :, start : start + 4 * span
            ].astype(BF16)
            held[core, 2, level, 2 * layer : 2 * layer + 2, 0 : rel.shape[2]] = rel[
                shard
            ].astype(BF16)
    sink.send_all()
    sink.wait()


def pack_riders(plan, sums, after):
    resident = []
    width = sums[0][0].shape[1]
    for heads, hidden, rel in sums:
        resident += [heads, hidden, rel]
    return call(
        functools.partial(pack_kernel, plan), resident, Source(), [], [], 3,
        [plan.sink_outs((32, RIDERS, width))], after,
    )


class WholeSums:
    def __init__(self, plan):
        self.pairs = {}

    def add(self, name, pair):
        self.pairs[name] = pair

    def add_top(self, g2, g1, g):
        self.top = whole_reduce(g, 1), whole_reduce(g1, 1), whole_reduce(g2, 0)

    def advance(self, hold, *names):
        return ()

    def finish(self, sums):
        self.token = sums[0][0][:1]
        big = [
            named(*whole_sums((self.pairs["attend"], self.pairs["mlp"]))), named(*self.top)
        ]
        shards = lax.axis_size("fsdp")
        parts = []
        for heads, hidden, rel in sums:
            rel = rel.transpose(1, 0, 2).reshape(2, -1)
            rows = (
                jnp.concatenate([heads[1], heads[2]]), heads[0], heads[3], heads[4], heads[5],
                heads[6], hidden[0], heads[7], rel[0], rel[1],
            )
            parts.append([row.reshape(shards, -1) for row in rows])
        cuts = np.cumsum([0] + [part.shape[1] for part in parts[0]])
        small = jnp.stack([jnp.concatenate(rows, 1) for rows in parts])
        mine = whole_reduce(small.astype(BF16), 1).astype(F32)[:, 0]
        stacked = [
            jnp.stack([big[layer][i] for layer in range(LAYERS)]).astype(F32) for i in range(4)
        ]
        small = [mine[:, a:b] for a, b in zip(cuts, cuts[1:])]
        return (*stacked[:2], *small), stacked[2:]


def on_device(
    ring, windows, slot_table, cotangent, qkv_weight, qv_bias, proj_weight, proj_bias,
    norm1_gain, norm1_bias, norm2_gain, norm2_bias, fc1_weight, fc1_bias, fc2_weight, fc2_bias,
    rel_height, rel_width,
):
    width = windows.shape[1]
    weights = (qkv_weight, proj_weight, fc1_weight, fc2_weight)
    parts = (
        qv_bias, proj_bias, norm1_gain, norm1_bias, norm2_gain, norm2_bias, fc1_bias, fc2_bias,
        rel_height, rel_width,
    )
    cuts = np.cumsum([0] + [part.shape[1] for part in parts])
    if ring:
        plan = PiecePlan()
        pending = PieceSums(plan)
        held = PieceWeights(weights, jnp.concatenate(parts, 1).reshape(-1))
    else:
        plan = WholePlan()
        pending = WholeSums(plan)
        held = WholeWeights(weights, parts)
    small = held.small
    (
        qv_bias_w, proj_bias_w, norm1_gain_w, norm1_bias_w, norm2_gain_w, norm2_bias_w,
        fc1_bias_w, fc2_bias_w, rel_height_w, rel_width_w,
    ) = [
        small[:, :, a:b].transpose(1, 0, 2).reshape(LAYERS, -1) for a, b in zip(cuts, cuts[1:])
    ]
    vec = jnp.stack(
        [norm1_gain_w, norm1_bias_w, qv_bias_w[:, :width], qv_bias_w[:, width:], proj_bias_w,
         norm2_gain_w, norm2_bias_w, fc2_bias_w], 1
    ).astype(F32)
    hidden_bias = fc1_bias_w.astype(F32)[:, None, :]
    ahead, back = relative_tables(rel_height_w, rel_width_w)
    keys_ahead, keys_back = key_tables()
    live = live_rows(slot_table)
    current = spread(windows)
    grad = spread(cotangent)
    whole = WholePlan()
    kept = []
    for layer in range(LAYERS):
        top = layer == LAYERS - 1
        after = held.before(f"attend_{layer}")
        if layer == 0:
            after = (*after, back)
        mid, h1, q, k, v, p, att, token = attend_forward(
            current, live, vec[layer], ahead[layer], keys_ahead, held.source(layer, "attend"),
            after,
        )
        held.passed(f"attend_{layer}", token)
        used = ("fc1",) if top else ("fc1", "fc2")
        after = held.before(f"mlp_{layer}")
        made = mlp_forward(
            whole, top, mid, live, vec[layer], hidden_bias[layer], grad,
            held.source(layer, *used), after,
        )
        following = None
        if top:
            h2, act, slope, top_sums, top_g2 = made
        else:
            following, h2, act, slope = made
        kept.append((current, mid, h1, q, k, v, p, att, h2, act, slope))
        current = following
    sums = [None] * LAYERS
    steps = {"middle_0": ("top",), "scores_0": ("top", "mlp"), "first_0": ("mlp",)}

    def ahead_of(name, past):
        return pending.advance(nothing(past.astype(F32)), *steps.get(name, ()))

    for layer in reversed(range(LAYERS)):
        top = layer == LAYERS - 1
        x, mid, h1, q, k, v, p, att, h2, act, slope = kept[layer]
        if top:
            dmid, sums2, hsum, top_g1 = top_backward(
                whole, grad, mid, live, vec[layer], h2, slope, held.source(layer, "fc1", "fc2"),
                (),
            )
            sums3 = top_sums
        else:
            dh, sums3, hsum, *pair = hidden_backward(
                plan, grad, act, live, h2, slope, held.source(layer, "fc2"), ()
            )
            pending.add("mlp", pair)
            dmid, sums2 = middle_backward(
                grad, mid, vec[layer], dh, held.source(layer, "fc1"), ahead_of("middle_0", sums3[0, 0])
            )
        db, dq, dk, dv, sums1, rel = scores_backward(
            dmid, live, back[layer], keys_back, q, k, v, p, held.source(layer, "proj"),
            ahead_of(f"scores_{layer}", sums2[0, 0]),
        )
        if top:
            grad, sums4, top_g = first_all_backward(
                whole, dmid, x, live, vec[layer], h1, att, db, dq, dk, dv,
                held.source(layer, "attend"), (),
            )
            pending.add_top(top_g2, top_g1, top_g)
        else:
            pair = weights_backward(plan, h1, att, db, dq, dk, dv, ())
            pending.add("attend", pair)
            grad, sums4 = first_backward(
                dmid, x, live, vec[layer], dq, dk, dv, held.source(layer, "attend"),
                ahead_of("first_0", pair[0][(0,) * pair[0].ndim]),
            )
        rel = rel[:, :HD] + rel[:, HD:]
        rel = jnp.stack([rel[:RELS].reshape(8, -1), rel[HD : HD + RELS].reshape(8, -1)], 1)
        sums[layer] = (sums1 + sums2 + sums3 + sums4, hsum, rel)
    input_grad = gather_back(grad).astype(BF16)
    (qkv_grad, proj_grad, *small), (fc1_grad, fc2_grad) = pending.finish(sums)
    output = gather_back(
        mlp_output(
            kept[-1][9], vec[-1], kept[-1][1], live, held.source(LAYERS - 1, "fc2"),
            (pending.token,),
        )
    ).astype(BF16)
    qv, pb, n1g, n1b, n2g, n2b, f1b, f2b, rh, rw = small
    return (
        output, input_grad, qkv_grad, qv, proj_grad, pb, n1g, n1b, n2g, n2b, fc1_grad, f1b,
        fc2_grad, f2b, rh, rw,
    )


def solution(mesh):
    rows = P(("rep", "fsdp"), None)
    cube = P(None, "fsdp", None)
    flat = P(None, "fsdp")
    ring = mesh.shape["rep"] == 4 and mesh.shape["fsdp"] == 8
    return jax.shard_map(
        functools.partial(on_device, ring),
        mesh=mesh,
        in_specs=(
            rows, P(("rep", "fsdp")), rows, cube, flat, cube, flat, flat, flat, flat, flat, cube,
            flat, cube, flat, flat, flat,
        ),
        out_specs=(
            rows, rows, cube, flat, cube, flat, flat, flat, flat, flat, cube, flat, cube, flat,
            flat, flat,
        ),
        check_vma=False,
    )
```

```python
import functools

import jax
import jax.numpy as jnp
import numpy as np
from jax import lax
from jax.experimental import pallas as pl
from jax.experimental.pallas import tpu as pltpu
from jax.sharding import PartitionSpec as P

HEADS = 12
HD = 64
WINDOW = 14
SIDE = 64
LAYERS = 2
GRID = 5
RELS = 2 * WINDOW - 1
EPSILON = 1e-06
PITCH = 16
SPAN = WINDOW * PITCH
PAIRS = HEADS // 2
LANES = 2 * HD
F32 = jnp.float32
BF16 = jnp.bfloat16
CHUNK = 768
ROWS_STEP = 64
VMEM_LIMIT = 56 * 1024 * 1024
SLAB = 384
RIDERS = 8
LARGE = 256 * 1024


def dot_nn(a, b):
    return lax.dot_general(a, b, (((1,), (0,)), ((), ())), preferred_element_type=F32)


def dot_nt(a, b):
    return lax.dot_general(a, b, (((1,), (1,)), ((), ())), preferred_element_type=F32)


def dot_tn(a, b):
    return lax.dot_general(a, b, (((0,), (0,)), ((), ())), preferred_element_type=F32)


def norm_rows(values):
    centre = jnp.mean(values, -1, keepdims=True)
    centered = values - centre
    inverse = lax.rsqrt(jnp.mean(centered * centered, -1, keepdims=True) + EPSILON)
    return centered * inverse, inverse


def norm_back(grad, normed, inverse, gain):
    scaled = grad * gain
    return inverse * (
        scaled
        - jnp.mean(scaled, -1, keepdims=True)
        - normed * jnp.mean(scaled * normed, -1, keepdims=True)
    )


def each(count, step, body):
    def run(index, carry):
        body(pl.multiple_of(index * step, step))
        return carry

    lax.fori_loop(0, count, run, 0)


def each_index(count, body):
    def run(index, carry):
        body(index)
        return carry

    lax.fori_loop(0, count, run, 0)


def in_fours(count, body):
    def several(index):
        for i in range(4):
            body(4 * index + i)

    each_index(count // 4, several)


def half_lane():
    return lax.broadcasted_iota(jnp.int32, (SPAN, LANES), 1)


def split_heads(pair):
    lane = half_lane()
    zero = jnp.zeros_like(pair)
    return jnp.concatenate(
        [jnp.where(lane < HD, pair, zero), jnp.where(lane < HD, zero, pair)], axis=0
    )


def join_heads(stacked):
    return jnp.where(half_lane() < HD, stacked[:SPAN], stacked[SPAN:])


def shift_rows(table):
    by_row = jnp.concatenate(
        [
            pltpu.roll(table[i * PITCH : (i + 1) * PITCH], i, axis=1) if i else table[:PITCH]
            for i in range(WINDOW)
        ],
        axis=0,
    )
    by_col = pltpu.roll(
        table.reshape(WINDOW, PITCH, LANES), 0, axis=2, stride=1, stride_axis=1
    ).reshape(SPAN, LANES)
    return jnp.where(half_lane() < HD, by_row, by_col)


def key_tables():
    ahead = np.zeros((SPAN, LANES), np.float32)
    back = np.zeros((SPAN, LANES), np.float32)
    for k in range(WINDOW):
        for m in range(PITCH):
            row = k * PITCH + m
            ahead[row, WINDOW - 1 + k] = 1.0
            back[row, WINDOW - 1 - k] = 1.0
            if m < WINDOW:
                ahead[row, HD + WINDOW - 1 + m] = 1.0
                back[row, HD + WINDOW - 1 - m] = 1.0
            else:
                ahead[row, LANES - 1] = -1e30
    return jnp.asarray(ahead, BF16), jnp.asarray(back, BF16)


class Flow:
    def __init__(self, ins, in_sem, outs, out_sem):
        self.ins = {}
        for i, (given, taken) in enumerate(ins):
            copy = pltpu.make_async_copy(given, taken, in_sem.at[i])
            copy.start()
            self.ins[id(taken)] = copy
        self.outs = {
            id(made): pltpu.make_async_copy(made, given, out_sem.at[i])
            for i, (made, given) in enumerate(outs)
        }
        self.sent = []

    def need(self, *refs):
        for ref in refs:
            copy = self.ins.pop(id(ref), None)
            if copy is not None:
                copy.wait()

    def emit(self, *refs):
        for ref in refs:
            copy = self.outs.pop(id(ref), None)
            if copy is not None:
                copy.start()
                self.sent.append(copy)

    def finish(self):
        for copy in self.ins.values():
            copy.wait()
        for copy in self.outs.values():
            copy.start()
        for copy in (*self.outs.values(), *self.sent):
            copy.wait()


def attend_kernel(source, flow, *refs):
    (x_ref, live_ref, vec_ref, table_ref, keys_ref), refs = refs[:5], refs[5:]
    weight_refs, refs = refs[: source.count], refs[source.count :]
    (mid_ref, h1_ref, q_ref, k_ref, v_ref, p_ref, att_ref), refs = refs[:7], refs[7:]
    token_ref, w_ref, sem = refs
    token_ref[...] = jnp.zeros_like(token_ref)
    ready = source.load("attend", weight_refs, w_ref, sem)
    width = x_ref.shape[1]
    flow.need(x_ref)

    def first_norm(start):
        rows = pl.ds(start, ROWS_STEP)
        normed, _ = norm_rows(x_ref[rows, :].astype(F32))
        shaped = (normed * vec_ref[0:1, :] + vec_ref[1:2, :]) * live_ref[rows, :]
        h1_ref[rows, :] = shaped.astype(BF16)

    each(x_ref.shape[0] // ROWS_STEP, ROWS_STEP, first_norm)
    flow.emit(h1_ref)
    ready()
    for index, (out_ref, bias) in enumerate(((q_ref, 2), (k_ref, None), (v_ref, 3))):

        def project(start, index=index, out_ref=out_ref, bias=bias):
            cols = pl.ds(start, CHUNK)
            made = dot_nn(h1_ref[...], w_ref[index, :, cols])
            if bias is not None:
                made = made + vec_ref[bias : bias + 1, cols]
            out_ref[:, cols] = made.astype(BF16)

        each(width // CHUNK, CHUNK, project)
        flow.emit(out_ref)

    def attend(index):
        rows = pl.ds(pl.multiple_of(index // PAIRS * SPAN, SPAN), SPAN)
        cols = pl.ds(pl.multiple_of(index % PAIRS * LANES, LANES), LANES)
        queries = q_ref[rows, cols]
        offsets = dot_nn(queries, table_ref[...])
        lane = half_lane()
        sides = []
        for half in range(2):
            moved = shift_rows(offsets[:, half * LANES : (half + 1) * LANES])
            sides.append(jnp.where(lane == LANES - 1, 1.0, moved).astype(BF16))
        left = jnp.concatenate(
            [split_heads(queries) * HD ** (-0.5), jnp.concatenate(sides, axis=0)], axis=1
        )
        right = jnp.concatenate([k_ref[rows, cols], keys_ref[...]], axis=1)
        scores = dot_nt(left, right)
        shifted = jnp.exp(scores - jnp.max(scores, -1, keepdims=True))
        probs = shifted * (1.0 / jnp.sum(shifted, -1, keepdims=True))
        low = probs.astype(BF16)
        p_ref[index] = low
        att_ref[rows, cols] = join_heads(dot_nn(low, v_ref[rows, cols])).astype(BF16)

    in_fours(x_ref.shape[0] // SPAN * PAIRS, attend)
    flow.emit(p_ref, att_ref)

    def finish(start):
        cols = pl.ds(start, CHUNK)
        branch = dot_nn(att_ref[...], w_ref[3, :, cols]) + vec_ref[4:5, cols]
        mid_ref[:, cols] = x_ref[:, cols].astype(F32) + live_ref[...] * branch

    each(width // CHUNK, CHUNK, finish)


def mlp_kernel(plan, source, top, flow, *refs):
    (mid_ref, live_ref, vec_ref, bias_ref), refs = refs[:4], refs[4:]
    if top:
        (grad_ref,), refs = refs[:1], refs[1:]
    weight_refs, refs = refs[: source.count], refs[source.count :]
    if top:
        (h2_ref, act_ref, slope_ref, sums_ref), refs = refs[:4], refs[4:]
        sink_refs, refs = refs[: plan.sinks], refs[plan.sinks :]
        (w1_ref, dm_ref, sem), refs = refs[:3], refs[3:]
        sink = plan.sink(sink_refs, refs, False)
    else:
        out_ref, h2_ref, act_ref, slope_ref, w1_ref, w2_ref, sem, sem2 = refs
    ready1 = source.load("fc1", weight_refs, w1_ref, sem)
    if not top:
        ready2 = source.load("fc2", weight_refs, w2_ref, sem2)
    width = mid_ref.shape[1]
    hidden_width = act_ref.shape[1]
    flow.need(mid_ref)

    def second_norm(start):
        rows = pl.ds(start, ROWS_STEP)
        normed, _ = norm_rows(mid_ref[rows, :])
        h2_ref[rows, :] = (normed * vec_ref[5:6, :] + vec_ref[6:7, :]).astype(BF16)

    each(mid_ref.shape[0] // ROWS_STEP, ROWS_STEP, second_norm)
    flow.emit(h2_ref)
    ready1()

    def expand(index):
        start = pl.multiple_of(index * CHUNK, CHUNK)
        cols = pl.ds(start, CHUNK)
        inner = pl.ds(pl.multiple_of(start % width, CHUNK), CHUNK)
        hidden = dot_nn(h2_ref[...], w1_ref[start // width, :, inner]) + bias_ref[:, cols]
        below = 0.5 * (1.0 + lax.erf(hidden * (0.5**0.5)))
        bell = jnp.exp(-0.5 * hidden * hidden) * (0.5 / np.pi) ** 0.5
        act_ref[:, cols] = (hidden * below).astype(BF16)
        slope_ref[:, cols] = (below + hidden * bell).astype(BF16)

    each_index(hidden_width // CHUNK, expand)
    flow.emit(act_ref, slope_ref)
    if top:
        sums_ref[...] = jnp.zeros_like(sums_ref)
        flow.need(grad_ref)
        second_weight(grad_ref, live_ref, act_ref, dm_ref, sums_ref, sink)
        sink.wait()
    else:
        ready2()
        contract(act_ref, w2_ref, vec_ref, mid_ref, live_ref, out_ref)


def contract(act_ref, w2_ref, vec_ref, mid_ref, live_ref, out_ref):
    def run(start):
        cols = pl.ds(start, CHUNK)
        made = dot_nn(act_ref[...], w2_ref[:, cols]) + vec_ref[7:8, cols]
        out_ref[:, cols] = mid_ref[:, cols] + live_ref[...] * made

    each(out_ref.shape[1] // CHUNK, CHUNK, run)


def out_kernel(source, flow, act_ref, vec_ref, mid_ref, live_ref, *refs):
    weight_refs, (out_ref, w2_ref, sem) = refs[: source.count], refs[source.count :]
    source.load("fc2", weight_refs, w2_ref, sem)()
    flow.need(act_ref, mid_ref)
    contract(act_ref, w2_ref, vec_ref, mid_ref, live_ref, out_ref)


def second_weight(grad_ref, live_ref, act_ref, dm_ref, sums_ref, sink):
    dm_ref[...] = (live_ref[...] * grad_ref[...].astype(F32)).astype(BF16)
    sums_ref[7:8, :] = jnp.sum(dm_ref[...].astype(F32), 0, keepdims=True)

    def run(index):
        rows = pl.ds(pl.multiple_of(index * SLAB, SLAB), SLAB)
        sink.rows(index, dot_tn(act_ref[:, rows], dm_ref[...]).astype(BF16))

    each_index(act_ref.shape[1] // SLAB, run)
    sink.send_all()


def hidden_back(flow, ready, sink, h2_ref, slope_ref, dh_ref, hsum_ref, w2_ref, dm_ref):
    width = h2_ref.shape[1]
    hidden_width = slope_ref.shape[1]
    flow.need(slope_ref)
    ready()

    def inner_grad(start):
        cols = pl.ds(start, CHUNK)
        made = (dot_nt(dm_ref[...], w2_ref[cols, :]) * slope_ref[:, cols].astype(F32)).astype(BF16)
        dh_ref[:, cols] = made
        hsum_ref[:, cols] = jnp.sum(made.astype(F32), 0, keepdims=True)

    each(hidden_width // CHUNK, CHUNK, inner_grad)
    flow.emit(dh_ref)
    flow.need(h2_ref)
    for block in range(hidden_width // width):

        def first_weight(start, block=block):
            cols = pl.ds(start, CHUNK)
            outer = pl.ds(pl.multiple_of(block * width + start, CHUNK), CHUNK)
            sink.cols(block, cols, dot_tn(h2_ref[...], dh_ref[:, outer]).astype(BF16))

        each(width // CHUNK, CHUNK, first_weight)
        sink.send(block)


def hidden_back_kernel(plan, source, flow, *refs):
    (grad_ref, act_ref, live_ref, h2_ref, slope_ref), refs = refs[:5], refs[5:]
    weight_refs, refs = refs[: source.count], refs[source.count :]
    (dh_ref, sums_ref, hsum_ref), refs = refs[:3], refs[3:]
    sink_refs, (w2_ref, dm_ref, sem), refs = refs[:2], refs[2:5], refs[5:]
    more, sink = plan.two_sinks(sink_refs, refs, True)
    ready = source.load("fc2", weight_refs, w2_ref, sem)
    sums_ref[...] = jnp.zeros_like(sums_ref)
    flow.need(grad_ref, act_ref)
    second_weight(grad_ref, live_ref, act_ref, dm_ref, sums_ref, more)
    hidden_back(flow, ready, sink, h2_ref, slope_ref, dh_ref, hsum_ref, w2_ref, dm_ref)
    more.wait()
    sink.wait()


def middle_back_kernel(source, flow, *refs):
    (grad_ref, mid_ref, vec_ref, dh_ref), refs = refs[:4], refs[4:]
    weight_refs, refs = refs[: source.count], refs[source.count :]
    dmid_ref, sums_ref, w1_ref, ds_ref, sem = refs
    ready = source.load("fc1", weight_refs, w1_ref, sem)
    flow.need(dh_ref)
    sums_ref[...] = jnp.zeros_like(sums_ref)
    middle_back(
        flow, ready, grad_ref, mid_ref, vec_ref, dh_ref, dmid_ref, sums_ref, w1_ref, ds_ref
    )


def middle_back(
    flow, ready, grad_ref, mid_ref, vec_ref, dh_ref, dmid_ref, sums_ref, w1_ref, ds_ref
):
    width = mid_ref.shape[1]
    hidden_width = dh_ref.shape[1]
    ready()

    def back_in(start):
        rows = pl.ds(start, CHUNK)
        made = dot_nt(dh_ref[:, 0:width], w1_ref[0, rows, :])
        for block in range(1, hidden_width // width):
            made += dot_nt(
                dh_ref[:, block * width : (block + 1) * width], w1_ref[block, rows, :]
            )
        ds_ref[:, rows] = made

    each(width // CHUNK, CHUNK, back_in)
    flow.need(mid_ref, grad_ref)

    def back_norm(start):
        rows = pl.ds(start, ROWS_STEP)
        normed, inverse = norm_rows(mid_ref[rows, :])
        grad = ds_ref[rows, :]
        sums_ref[5:6, :] += jnp.sum(grad * normed, 0, keepdims=True)
        sums_ref[6:7, :] += jnp.sum(grad, 0, keepdims=True)
        dmid_ref[rows, :] = grad_ref[rows, :].astype(F32) + norm_back(
            grad, normed, inverse, vec_ref[5:6, :]
        )

    each(mid_ref.shape[0] // ROWS_STEP, ROWS_STEP, back_norm)


def top_back_kernel(plan, source, flow, *refs):
    (grad_ref, mid_ref, live_ref, vec_ref, h2_ref, slope_ref), refs = refs[:6], refs[6:]
    weight_refs, refs = refs[: source.count], refs[source.count :]
    (dmid_ref, sums_ref, hsum_ref), refs = refs[:3], refs[3:]
    sink_refs, refs = refs[: plan.sinks], refs[plan.sinks :]
    (w1_ref, w2_ref, dm_ref, dh_ref, ds_ref, sem, sem2), refs = refs[:7], refs[7:]
    sink = plan.sink(sink_refs, refs, False)
    ready2 = source.load("fc2", weight_refs, w2_ref, sem2)
    ready1 = source.load("fc1", weight_refs, w1_ref, sem)
    sums_ref[...] = jnp.zeros_like(sums_ref)
    flow.need(grad_ref)
    dm_ref[...] = (live_ref[...] * grad_ref[...].astype(F32)).astype(BF16)
    hidden_back(flow, ready2, sink, h2_ref, slope_ref, dh_ref, hsum_ref, w2_ref, dm_ref)
    middle_back(
        flow, ready1, grad_ref, mid_ref, vec_ref, dh_ref, dmid_ref, sums_ref, w1_ref, ds_ref
    )
    sink.wait()


def scores_back_kernel(source, flow, *refs):
    (
        dmid_ref, live_ref, table_ref, keys_ref, q_ref, k_ref, v_ref, p_ref,
    ), refs = refs[:8], refs[8:]
    weight_refs, refs = refs[: source.count], refs[source.count :]
    db_ref, dq_ref, dk_ref, dv_ref, sums_ref, rel_ref, w_ref, da_ref, sem = refs
    ready = source.load("proj", weight_refs, w_ref, sem)
    width = dmid_ref.shape[1]
    flow.need(dmid_ref)
    db_ref[...] = (live_ref[...] * dmid_ref[...]).astype(BF16)
    flow.emit(db_ref)
    sums_ref[...] = jnp.zeros_like(sums_ref)
    sums_ref[0:1, :] = jnp.sum(db_ref[...].astype(F32), 0, keepdims=True)
    rel_ref[...] = jnp.zeros_like(rel_ref)
    ready()

    def back_out(start):
        rows = pl.ds(start, CHUNK)
        da_ref[:, rows] = dot_nt(db_ref[...], w_ref[rows, :]).astype(BF16)

    each(width // CHUNK, CHUNK, back_out)
    flow.need(v_ref, p_ref, k_ref, q_ref)

    def attend(index):
        rows = pl.ds(pl.multiple_of(index // PAIRS * SPAN, SPAN), SPAN)
        cols = pl.ds(pl.multiple_of(index % PAIRS * LANES, LANES), LANES)
        low = p_ref[index]
        probs = low.astype(F32)
        outer = split_heads(da_ref[rows, cols])
        queries = split_heads(q_ref[rows, cols])
        d_probs = dot_nt(outer, v_ref[rows, cols])
        dv_ref[rows, cols] = dot_tn(low, outer).astype(BF16)
        mean = jnp.sum(d_probs * probs, -1, keepdims=True)
        d_scores = (probs * (d_probs - mean)).astype(BF16)
        both = dot_nn(d_scores, jnp.concatenate([k_ref[rows, cols], keys_ref[...]], axis=1))
        moved = [
            shift_rows(both[half * SPAN : (half + 1) * SPAN, LANES:]).astype(BF16)
            for half in range(2)
        ]
        rel_part = dot_nt(jnp.concatenate(moved, axis=1), table_ref[...])
        direct = join_heads(both[:, :LANES]) * HD ** (-0.5)
        dq_ref[rows, cols] = (direct + rel_part).astype(BF16)
        dk_ref[rows, cols] = (dot_tn(d_scores, queries) * HD ** (-0.5)).astype(BF16)
        rel_ref[...] += dot_tn(jnp.concatenate(moved, axis=0), queries)

    in_fours(dmid_ref.shape[0] // SPAN * PAIRS, attend)
    flow.emit(dq_ref, dk_ref, dv_ref)
    sums_ref[1:2, :] = jnp.sum(dq_ref[...].astype(F32), 0, keepdims=True)
    sums_ref[2:3, :] = jnp.sum(dv_ref[...].astype(F32), 0, keepdims=True)


def first_weights(flow, sink, h1_ref, att_ref, db_ref, dq_ref, dk_ref, dv_ref):
    pairs = ((h1_ref, dq_ref), (h1_ref, dk_ref), (h1_ref, dv_ref), (att_ref, db_ref))
    for index, (left_ref, right_ref) in enumerate(pairs):
        flow.need(left_ref, right_ref)

        def weight(start, index=index, left_ref=left_ref, right_ref=right_ref):
            cols = pl.ds(start, CHUNK)
            sink.cols(index, cols, dot_tn(left_ref[...], right_ref[:, cols]).astype(BF16))

        each(h1_ref.shape[1] // CHUNK, CHUNK, weight)
        sink.send(index)


def first_weights_kernel(plan, flow, *refs):
    sink = plan.sink(refs[6 : 6 + plan.sinks], refs[6 + plan.sinks :], True)
    first_weights(flow, sink, *refs[:6])
    sink.wait()


def first_back(
    flow, ready, dmid_ref, x_ref, live_ref, vec_ref, dq_ref, dk_ref, dv_ref, next_ref, sums_ref,
    w_ref, dh_ref,
):
    width = x_ref.shape[1]
    flow.need(dq_ref, dk_ref, dv_ref)
    ready()

    def back_in(start):
        rows = pl.ds(start, CHUNK)
        made = dot_nt(dq_ref[...], w_ref[0, rows, :])
        made += dot_nt(dk_ref[...], w_ref[1, rows, :])
        made += dot_nt(dv_ref[...], w_ref[2, rows, :])
        dh_ref[:, rows] = made * live_ref[...]

    each(width // CHUNK, CHUNK, back_in)
    flow.need(x_ref, dmid_ref)
    sums_ref[...] = jnp.zeros_like(sums_ref)

    def back_norm(start):
        rows = pl.ds(start, ROWS_STEP)
        normed, inverse = norm_rows(x_ref[rows, :].astype(F32))
        grad = dh_ref[rows, :]
        sums_ref[3:4, :] += jnp.sum(grad * normed, 0, keepdims=True)
        sums_ref[4:5, :] += jnp.sum(grad, 0, keepdims=True)
        next_ref[rows, :] = dmid_ref[rows, :] + norm_back(grad, normed, inverse, vec_ref[0:1, :])

    each(x_ref.shape[0] // ROWS_STEP, ROWS_STEP, back_norm)


def first_back_kernel(source, flow, *refs):
    ins, refs = refs[:7], refs[7:]
    weight_refs, refs = refs[: source.count], refs[source.count :]
    next_ref, sums_ref, w_ref, dh_ref, sem = refs
    ready = source.load("attend", weight_refs, w_ref, sem)
    first_back(flow, ready, *ins, next_ref, sums_ref, w_ref, dh_ref)


def first_all_kernel(plan, source, flow, *refs):
    (dmid_ref, x_ref, live_ref, vec_ref, h1_ref, att_ref, db_ref), refs = refs[:7], refs[7:]
    (dq_ref, dk_ref, dv_ref), refs = refs[:3], refs[3:]
    weight_refs, refs = refs[: source.count], refs[source.count :]
    (next_ref, sums_ref), refs = refs[:2], refs[2:]
    sink_refs, refs = refs[: plan.sinks], refs[plan.sinks :]
    (w_ref, dh_ref, sem), refs = refs[:3], refs[3:]
    sink = plan.sink(sink_refs, refs, True)
    ready = source.load("attend", weight_refs, w_ref, sem)
    first_weights(flow, sink, h1_ref, att_ref, db_ref, dq_ref, dk_ref, dv_ref)
    first_back(
        flow, ready, dmid_ref, x_ref, live_ref, vec_ref, dq_ref, dk_ref, dv_ref, next_ref,
        sums_ref, w_ref, dh_ref,
    )
    sink.wait()


VM = pl.BlockSpec(memory_space=pltpu.VMEM)
ANY = pl.BlockSpec(memory_space=pltpu.HBM)


def shape(dims, kind):
    return jax.ShapeDtypeStruct(tuple(dims), kind)


class Source:
    def __init__(self, **parts):
        self.parts = parts
        self.arrays = []
        self.places = {}
        for name, (arrays, _, _) in parts.items():
            found = []
            for array in arrays:
                known = [i for i, other in enumerate(self.arrays) if other is array]
                if not known:
                    known = [len(self.arrays)]
                    self.arrays.append(array)
                found.append(known[0])
            self.places[name] = found
        self.count = len(self.arrays)

    def semaphores(self, name):
        whole = self.parts[name][1] is None
        return pltpu.SemaphoreType.DMA((4 if whole else 8 if name == "proj" else 32,))

    def load(self, name, refs, target, sem):
        arrays, offset, rotated = self.parts[name]
        refs = [refs[i] for i in self.places[name]]
        if offset is not None and name == "proj":
            return load_proj(refs, target, offset, rotated, sem)
        if offset is None:
            pairs = whole_pairs(name, refs, target)
        else:
            pairs = [pair for _, _, pair in piece_pairs(name, refs, target, offset, rotated)]
        copies = [
            pltpu.make_async_copy(given, taken, sem.at[i])
            for i, (given, taken) in enumerate(pairs)
        ]
        for copy in copies:
            copy.start()

        def ready():
            for copy in copies:
                copy.wait()

        return ready


def whole_pairs(name, refs, target):
    if name == "fc2":
        return [(refs[0], target)]
    if name == "proj":
        return [(refs[1], target)]
    width = target.shape[1]
    pairs = []
    for ref in refs:
        for start in range(0, ref.shape[1], width):
            pairs.append((ref.at[:, pl.ds(start, width)], target.at[len(pairs)]))
    return pairs


def position():
    shard = lax.axis_index("fsdp")
    return lax.axis_index("rep"), shard >> 1, shard & 1


def piece_pairs(name, refs, target, offset, rotated):
    rep, level, core = position()
    pairs = []
    rows = target.shape[-2] // 8
    span = rows // 4 if name == "fc2" else rows
    for parity in range(2):
        for part, (away, levels) in enumerate(
            ((0, range(4)), (1, range(4)), (2, range(4)), (3, range(2)), (3, range(2, 4)))
        ):
            ref = refs[parity * 5 + part]
            for place, step in enumerate(levels):
                source_level = (level - step) & 3 if rotated else step
                shard = source_level * 2 + (core ^ parity)
                kind = rep ^ away
                if name == "fc2":
                    start = pl.multiple_of(shard * rows + kind * span, 16)
                    taken = target.at[pl.ds(start, span), :]
                else:
                    start = pl.multiple_of(shard * span, 16)
                    whole = target if name == "proj" else target.at[kind]
                    taken = whole.at[pl.ds(start, span), :]
                given = ref.at[place, pl.ds(offset, span), :]
                pairs.append((away, parity * 4 + step, (given, taken)))
    return pairs


def load_proj(refs, target, offset, rotated, sem):
    rep = lax.axis_index("rep")
    pairs = piece_pairs("proj", refs, target, offset, rotated)
    for away in range(4):

        @pl.when((rep ^ away) == 3)
        def _(away=away):
            for other, slot, pair in pairs:
                if other == away:
                    pltpu.make_async_copy(*pair, sem.at[slot]).start()

    def ready():
        for away, slot, pair in pairs:
            if away == 0:
                pltpu.make_async_copy(*pair, sem.at[slot]).wait()

    return ready


class WholeSink:
    def __init__(self, refs, scratch):
        self.ref = refs[0]
        self.held, self.sem = scratch[:2]
        self.sent = []

    def rows(self, index, value):
        self.held[pl.ds(pl.multiple_of(index * SLAB, SLAB), SLAB), :] = value

    def cols(self, block, cols, value):
        self.held[block, :, cols] = value

    def copy(self, given, taken):
        copy = pltpu.make_async_copy(given, taken, self.sem.at[len(self.sent)])
        copy.start()
        self.sent.append(copy)

    def send(self, block):
        self.copy(self.held.at[block], self.ref.at[block])

    def send_all(self):
        self.copy(self.held, self.ref)

    def wait(self):
        for copy in self.sent:
            copy.wait()


class PieceSink:
    def __init__(self, refs, scratch, rotated, offset=0):
        self.refs, self.rotated, self.offset = refs, rotated, offset
        self.held, self.sem = scratch[:2]
        self.position = position()
        self.sent = []

    def rows(self, index, value):
        span = self.held.shape[3]
        for block in range(4):
            self.held[index & 1, block, index >> 1] = value[block * span : (block + 1) * span]

    def cols(self, block, cols, value):
        span = self.held.shape[3]
        for shard in range(8):
            self.held[shard & 1, block, shard >> 1, :, cols] = value[
                shard * span : (shard + 1) * span
            ]

    def send(self, block):
        rep, level, core = self.position
        for parity in range(2):
            given = self.held.at[core ^ parity, block]
            span = self.held.shape[3]
            taken = self.refs[parity].at[rep ^ block, :, pl.ds(self.offset, span)]
            moves = [(given, taken)]
            if self.rotated:
                moves = [(given.at[(level + step) & 3], taken.at[step]) for step in range(4)]
            for move in moves:
                copy = pltpu.make_async_copy(*move, self.sem.at[len(self.sent)])
                copy.start()
                self.sent.append(copy)

    def send_all(self):
        for block in range(4):
            self.send(block)

    def wait(self):
        for copy in self.sent:
            copy.wait()


class WholePlan:
    sinks = 1

    def sink(self, refs, scratch, rotated=False):
        return WholeSink(refs, scratch)

    def sink_outs(self, dims):
        return [shape(dims, BF16)], [ANY], [pltpu.VMEM(dims, BF16), pltpu.SemaphoreType.DMA((4,))]

    def two_sinks(self, refs, scratch, rotated):
        return WholeSink(refs[:1], scratch), WholeSink(refs[1:], scratch[2:])

    def two_outs(self, hidden, width):
        one = self.sink_outs((hidden, width))
        two = self.sink_outs((hidden // width, width, width))
        return one[0] + two[0], one[1] + two[1], one[2] + two[2]


class PiecePlan:
    sinks = 2

    def sink(self, refs, scratch, rotated=False):
        return PieceSink(refs, scratch, rotated)

    def sink_outs(self, dims):
        width = dims[-1]
        span = int(np.prod(dims)) // width // 32
        outs = [shape((4, 4, span, width), BF16)] * 2
        scratch = [pltpu.VMEM((2, 4, 4, span, width), BF16), pltpu.SemaphoreType.DMA((32,))]
        return outs, [ANY] * 2, scratch

    def two_sinks(self, refs, scratch, rotated):
        span = scratch[0].shape[3]
        return PieceSink(refs, scratch, rotated), PieceSink(refs, scratch[2:], rotated, span)

    def two_outs(self, hidden, width):
        span = hidden // 32
        outs = [shape((4, 4, 2 * span, width), BF16)] * 2
        scratch = [pltpu.VMEM((2, 4, 4, span, width), BF16), pltpu.SemaphoreType.DMA((32,))] * 2
        return outs, [ANY] * 2, scratch


def large(array):
    return int(np.prod(array.shape)) * np.dtype(array.dtype).itemsize >= LARGE


def call(kernel, resident, source, outs, scratch, micros, sinks=(), after=()):
    sink_outs, sink_specs, sink_scratch = [], [], []
    for more_outs, more_specs, more_scratch in sinks:
        sink_outs += more_outs
        sink_specs += more_specs
        sink_scratch += more_scratch
    in_moves = [i for i, a in enumerate(resident) if large(a)]
    out_moves = [i for i, a in enumerate(outs) if large(a)]
    buffers = [pltpu.VMEM(resident[i].shape, resident[i].dtype) for i in in_moves]
    buffers += [pltpu.VMEM(outs[i].shape, outs[i].dtype) for i in out_moves]
    semaphores = [
        pltpu.SemaphoreType.DMA((max(len(moves), 1),)) for moves in (in_moves, out_moves)
    ]
    count = len(resident)
    first = count + source.count

    def body(*refs):
        ins, weights = list(refs[:count]), refs[count:first]
        refs = refs[first + len(after) :]
        made, refs = list(refs[: len(outs)]), refs[len(outs) :]
        sunk, refs = refs[: len(sink_outs)], refs[len(sink_outs) :]
        held, refs = refs[: len(buffers)], refs[len(buffers) :]
        in_sem, out_sem, *rest = refs
        in_held, out_held = held[: len(in_moves)], held[len(in_moves) :]
        flow = Flow(
            [(ins[i], ref) for i, ref in zip(in_moves, in_held)],
            in_sem,
            [(ref, made[i]) for i, ref in zip(out_moves, out_held)],
            out_sem,
        )
        for i, ref in zip(in_moves, in_held):
            ins[i] = ref
        for i, ref in zip(out_moves, out_held):
            made[i] = ref
        kernel(flow, *ins, *weights, *made, *sunk, *rest)
        flow.finish()

    run = pl.pallas_call(
        body,
        out_shape=tuple([*outs, *sink_outs]),
        in_specs=[ANY if large(a) else VM for a in resident]
        + [ANY] * (source.count + len(after)),
        out_specs=tuple([*[ANY if large(a) else VM for a in outs], *sink_specs]),
        scratch_shapes=[*buffers, *semaphores, *scratch, *sink_scratch],
        compiler_params=pltpu.CompilerParams(vmem_limit_bytes=VMEM_LIMIT),
        cost_estimate=pl.CostEstimate(
            flops=int(micros * 1e10), bytes_accessed=1 << 20, transcendentals=0
        ),
    )
    return run(*resident, *source.arrays, *after)


def attend_forward(x, live, vec, table, keys, source, after):
    rows, width = x.shape
    outs = (
        shape((rows, width), F32),
        *[shape((rows, width), BF16)] * 4,
        shape((rows // SPAN * PAIRS, 2 * SPAN, SPAN), BF16),
        shape((rows, width), BF16),
        shape((8, LANES), F32),
    )
    scratch = [pltpu.VMEM((4, width, width), BF16), source.semaphores("attend")]
    return call(
        functools.partial(attend_kernel, source),
        (x, live, vec, table, keys), source, outs, scratch, 20, (), after,
    )


def mlp_forward(plan, top, mid, live, vec, bias, grad, source, after):
    rows, width = mid.shape
    hidden = bias.shape[1]
    outs = [
        shape((rows, width), BF16), shape((rows, hidden), BF16), shape((rows, hidden), BF16),
    ]
    scratch = [pltpu.VMEM((hidden // width, width, width), BF16)]
    resident = [mid, live, vec, bias]
    sinks = []
    if top:
        resident.append(grad)
        outs.append(shape((8, width), F32))
        scratch += [pltpu.VMEM((rows, width), BF16), source.semaphores("fc1")]
        sinks.append(plan.sink_outs((hidden, width)))
    else:
        outs.insert(0, shape((rows, width), F32))
        scratch += [
            pltpu.VMEM((hidden, width), BF16), source.semaphores("fc1"),
            source.semaphores("fc2"),
        ]
    return call(
        functools.partial(mlp_kernel, plan, source, top),
        resident, source, outs, scratch, 16, sinks, after,
    )


def mlp_output(act, vec, mid, live, source, after):
    hidden, width = act.shape[1], mid.shape[1]
    scratch = [pltpu.VMEM((hidden, width), BF16), source.semaphores("fc2")]
    return call(
        functools.partial(out_kernel, source), (act, vec, mid, live), source,
        [shape(mid.shape, F32)], scratch, 5, (), after,
    )[0]


def hidden_backward(plan, grad, act, live, h2, slope, source, after):
    rows, width = h2.shape
    hidden = slope.shape[1]
    outs = [shape((rows, hidden), BF16), shape((8, width), F32), shape((1, hidden), F32)]
    scratch = [
        pltpu.VMEM((hidden, width), BF16), pltpu.VMEM((rows, width), BF16),
        source.semaphores("fc2"),
    ]
    return call(
        functools.partial(hidden_back_kernel, plan, source),
        (grad, act, live, h2, slope), source, outs, scratch, 18,
        [plan.two_outs(hidden, width)], after,
    )


def top_backward(plan, grad, mid, live, vec, h2, slope, source, after):
    rows, width = mid.shape
    hidden = slope.shape[1]
    outs = [shape((rows, width), F32), shape((8, width), F32), shape((1, hidden), F32)]
    scratch = [
        pltpu.VMEM((hidden // width, width, width), BF16), pltpu.VMEM((hidden, width), BF16),
        pltpu.VMEM((rows, width), BF16), pltpu.VMEM((rows, hidden), BF16),
        pltpu.VMEM((rows, width), F32), source.semaphores("fc1"), source.semaphores("fc2"),
    ]
    return call(
        functools.partial(top_back_kernel, plan, source),
        (grad, mid, live, vec, h2, slope), source, outs, scratch, 19,
        [plan.sink_outs((hidden // width, width, width))], after,
    )


def middle_backward(grad, mid, vec, dh, source, after):
    rows, width = mid.shape
    hidden = dh.shape[1]
    outs = [shape((rows, width), F32), shape((8, width), F32)]
    scratch = [
        pltpu.VMEM((hidden // width, width, width), BF16), pltpu.VMEM((rows, width), F32),
        source.semaphores("fc1"),
    ]
    return call(
        functools.partial(middle_back_kernel, source),
        (grad, mid, vec, dh), source, outs, scratch, 10, (), after,
    )


def scores_backward(dmid, live, table, keys, q, k, v, p, source, after):
    rows, width = dmid.shape
    outs = [*[shape((rows, width), BF16)] * 4, shape((8, width), F32), shape((LANES, LANES), F32)]
    scratch = [
        pltpu.VMEM((width, width), BF16), pltpu.VMEM((rows, width), BF16),
        source.semaphores("proj"),
    ]
    return call(
        functools.partial(scores_back_kernel, source),
        (dmid, live, table, keys, q, k, v, p), source, outs, scratch, 15, (), after,
    )


def weights_backward(plan, h1, att, db, dq, dk, dv, after):
    width = h1.shape[1]
    return call(
        functools.partial(first_weights_kernel, plan), (h1, att, db, dq, dk, dv),
        Source(), [], [], 8, [plan.sink_outs((4, width, width))], after,
    )


def first_backward(dmid, x, live, vec, dq, dk, dv, source, after):
    rows, width = x.shape
    outs = [shape((rows, width), F32), shape((8, width), F32)]
    scratch = [
        pltpu.VMEM((4, width, width), BF16), pltpu.VMEM((rows, width), F32),
        source.semaphores("attend"),
    ]
    return call(
        functools.partial(first_back_kernel, source),
        (dmid, x, live, vec, dq, dk, dv), source, outs, scratch, 10, (), after,
    )


def first_all_backward(plan, dmid, x, live, vec, h1, att, db, dq, dk, dv, source, after):
    rows, width = x.shape
    outs = [shape((rows, width), F32), shape((8, width), F32)]
    scratch = [
        pltpu.VMEM((4, width, width), BF16), pltpu.VMEM((rows, width), F32),
        source.semaphores("attend"),
    ]
    return call(
        functools.partial(first_all_kernel, plan, source),
        (dmid, x, live, vec, h1, att, db, dq, dk, dv), source, outs, scratch, 14,
        [plan.sink_outs((4, width, width))], after,
    )


def live_rows(slot_table):
    places = jnp.arange(PITCH, dtype=jnp.int32)
    rows_inside = slot_table[:, None] // GRID * WINDOW + places[None, :WINDOW] < SIDE
    cols_inside = slot_table[:, None] % GRID * WINDOW + places[None, :] < SIDE
    cols_inside = cols_inside & (places < WINDOW)[None, :]
    both_inside = rows_inside[:, :, None] & cols_inside[:, None, :]
    return both_inside.astype(F32).reshape(slot_table.shape[0] * SPAN, 1)


def spread(values):
    width = values.shape[1]
    grid = values.reshape(-1, WINDOW, width)
    return jnp.pad(grid, ((0, 0), (0, PITCH - WINDOW), (0, 0))).reshape(-1, width)


def gather_back(values):
    width = values.shape[1]
    return values.reshape(-1, PITCH, width)[:, :WINDOW].reshape(-1, width)


def relative_tables(rel_height, rel_width):
    stacked = jnp.stack([rel_height, rel_width], 1).reshape(LAYERS, 2, RELS, HD)

    def spread_table(rows):
        padded = jnp.pad(rows, ((0, 0), (0, 0), (0, HD - RELS), (0, 0)))
        one = padded.reshape(LAYERS, LANES, HD).transpose(0, 2, 1)
        none = jnp.zeros_like(one)
        return jnp.concatenate(
            [jnp.concatenate([one, none], 2), jnp.concatenate([none, one], 2)], 1
        )

    return spread_table(stacked[:, :, ::-1]), spread_table(stacked)


def whole_weights(weights):
    qkv, proj, fc1, fc2 = weights
    layers = []
    for layer in range(LAYERS):
        q, p, a, b = (
            lax.all_gather(w[layer], "fsdp", axis=0, tiled=True) for w in (qkv, proj, fc1, fc2)
        )
        layers.append(
            dict(attend=((q, p), None, False), proj=((q, p), None, False), fc1=((a,), None, False), fc2=((b,), None, False))
        )
    return layers


def whole_small(parts):
    packed = jnp.concatenate(parts, axis=1)
    return lax.all_gather(packed, "fsdp", axis=0, tiled=False)


def whole_reduce(value, axis):
    return lax.psum(lax.psum_scatter(value, "fsdp", scatter_dimension=axis, tiled=True), "rep")


def whole_sums(grads):
    (g,), (g2, g1) = grads
    return whole_reduce(g, 1), whole_reduce(g1, 1), whole_reduce(g2, 0)


def named(g, g1, g2):
    return jnp.concatenate([g[0], g[1], g[2]], 1), g[3], jnp.concatenate(list(g1), 1), g2


def permute(value, axis, move):
    return lax.ppermute(value, axis, [(i, move(i)) for i in range({"rep": 4, "fsdp": 8}[axis])])


def to_x(value):
    return permute(value, "rep", lambda i: i ^ 1)


def to_y(value):
    return permute(value, "rep", lambda i: i ^ 2)


def to_xy(value):
    return permute(value, "rep", lambda i: i ^ 3)


def to_core(value):
    return permute(value, "fsdp", lambda i: i ^ 1)


def to_level(value, step):
    return permute(value, "fsdp", lambda i: (i + 2 * step) % 8)


LEVELS = [[0, 2, 4, 6], [1, 3, 5, 7]]


def nothing(value):
    return jnp.minimum(jnp.abs(value), 0)


def swap(value, flag, axis):
    first = lax.slice_in_dim(value, 0, 1, axis=axis)
    second = lax.slice_in_dim(value, 1, 2, axis=axis)
    return jnp.where(flag == 1, jnp.concatenate([second, first], axis), value)


def by_replica(value, rep):
    rest = value.shape[1:]
    value = value.reshape(2, 2, *rest)
    value = swap(swap(value, rep & 1, 1), rep >> 1, 0)
    return value.reshape(4, *rest)


def turn(value, start, axis):
    size = value.shape[axis]
    return lax.dynamic_slice_in_dim(
        jnp.concatenate([value, value], axis), start, size, axis
    )


def own_blocks(weights, layer, rep):
    qkv, proj, fc1, fc2 = (w[layer] for w in weights)
    width = proj.shape[1]
    span = proj.shape[0]
    first = lax.dynamic_slice_in_dim(jnp.concatenate([qkv, proj], 1), rep * width, width, 1)
    second = lax.dynamic_slice_in_dim(fc1, rep * width, width, 1)
    third = lax.dynamic_slice_in_dim(fc2, rep * span, span, 0)
    return first, second, third


class Across:
    def __init__(self, held):
        self.held = held
        self.x, self.y = to_x(held), to_y(held)

    def cross(self, token=None):
        low, high = self.y[:2], self.x[2:]
        if token is not None:
            low, high = low + token, high + token
        self.low, self.high = to_x(low), to_y(high)
        return low, high

    def finish(self, token=None):
        low, high = self.low, self.high
        if token is not None:
            low, high = low + token, high + token
        pieces = (self.held, self.x, self.y, low, high)
        return pieces + tuple(to_core(piece) for piece in pieces)


class PieceWeights:
    def __init__(self, weights, small):
        rep, level, core = position()
        blocks = [own_blocks(weights, layer, rep) for layer in range(LAYERS)]
        span, width = blocks[0][0].shape
        size = small.shape[0] // 4
        rider = lax.dynamic_slice_in_dim(small, rep * size, size, 0)
        rider = jnp.pad(rider, (0, RIDERS * width - size)).reshape(RIDERS, width)
        first = jnp.concatenate([*blocks[0][:2], rider], 0)[None]
        self.span = span
        held = jnp.concatenate([first] + [to_level(first, step) for step in (1, 2, 3)], 0)
        self.rest = lax.all_gather(
            jnp.concatenate([blocks[0][2], blocks[1][0]], 0) + nothing(jnp.max(jnp.abs(held[1:, 0, 0]))), "fsdp",
            axis=0, tiled=True, axis_index_groups=LEVELS,
        ).reshape(4, 2 * span, width)
        self.fc1 = lax.all_gather(
            weights[2][1] + nothing(self.rest[0, 0, 0]), "fsdp", axis=0, tiled=True
        )
        self.top = weights[3][1]
        one = Across(held)
        one.cross()
        self.one = one.finish()
        riders = jnp.stack(
            [
                jnp.concatenate([t[:, 2 * span :] for t in self.one[5 * p : 5 * p + 5]], 0).reshape(
                    4, 4, RIDERS * width
                )[:, :, :size]
                for p in range(2)
            ]
        )
        riders = by_replica(swap(riders, core, 0).transpose(1, 0, 2, 3), rep)
        turned = jnp.concatenate([riders[:, :, i : i + 1] for i in (3, 2, 1, 0)], 2)
        riders = turn(turned, 3 - level, 2)
        self.small = riders.transpose(2, 1, 0, 3).reshape(8, LAYERS, -1)

    def before(self, name):
        if name == "attend_0":
            self.next = Across(self.rest)
            return (self.rest,)
        if name == "mlp_0":
            self.two = self.next.finish()
        return ()

    def passed(self, name, token):
        if name == "attend_0":
            token = token[0, 0].astype(BF16)
            self.next.cross(token)
            self.fc2 = lax.all_gather(self.top + token, "fsdp", axis=0, tiled=True)

    def source(self, layer, *names):
        if layer == 0:
            parts = dict(
                attend=lambda: (self.one, 0, True),
                proj=lambda: (self.one, 0, True),
                fc1=lambda: (self.one, self.span, True),
                fc2=lambda: (self.two, 0, False),
            )
        else:
            parts = dict(
                attend=lambda: (self.two, self.span, False),
                proj=lambda: (self.two, self.span, False),
                fc1=lambda: ((self.fc1,), None, False),
                fc2=lambda: ((self.fc2,), None, False),
            )
        return Source(**{name: parts[name]() for name in names})


class WholeWeights:
    def __init__(self, weights, small):
        self.small = whole_small(small)
        self.layers = whole_weights(weights)

    def before(self, name):
        return ()

    def passed(self, name, token):
        pass

    def source(self, layer, *names):
        return Source(**{name: self.layers[layer][name] for name in names})


class ReplicaSum:
    def __init__(self, *pairs):
        self.pairs = [(keep, to_core(send)) for keep, send in pairs]
        self.step = 0

    def both(self, away, part):
        sums = [
            keep[away, part].astype(F32) + got[away, part].astype(F32) for keep, got in self.pairs
        ]
        return sums[0] if len(sums) == 1 else jnp.concatenate(sums, -2)

    def advance(self, hold=0):
        low, high = slice(0, 2), slice(2, 4)
        self.step += 1
        if self.step == 1:
            send_x = (self.both(slice(1, 4, 2), low) + hold).astype(BF16)
            send_y = (self.both(slice(2, 4), high) + hold).astype(BF16)
            self.x, self.y = to_x(send_x), to_y(send_y)
            return [send_x, send_y]
        if self.step == 2:
            send_y = (self.both(2, low) + self.x[1].astype(F32) + hold).astype(BF16)
            send_x = (self.both(1, high) + self.y[1].astype(F32) + hold).astype(BF16)
            self.last_y, self.last_x = to_y(send_y), to_x(send_x)
            return [send_x, send_y]
        if self.step == 4:
            low, high = self.result
            sends = (low[1], high[0], high[1])
            self.levels = [to_level(send, step + 1) for step, send in enumerate(sends)]
            return list(sends)
        if self.step == 5:
            total = self.result[0][0].astype(F32)
            for got in self.levels:
                total = total + got.astype(F32)
            self.total = total.astype(BF16)
            return [self.total]
        self.result = [
            (part + hold).astype(BF16)
            for part in (
                self.both(0, low) + self.x[0].astype(F32) + self.last_y.astype(F32),
                self.both(0, high) + self.y[0].astype(F32) + self.last_x.astype(F32),
            )
        ]
        return self.result


class ReplicaAll:
    def __init__(self, *parts):
        self.parts = list(parts)
        self.moves = [to_x, to_y]
        self.got = None

    def advance(self, hold=0):
        if self.got is not None:
            self.add(hold)
        else:
            self.parts = [part + hold.astype(BF16) for part in self.parts]
        self.got = [move(part) for move, part in zip(self.moves, self.parts)]
        return self.parts

    def add(self, hold=0):
        self.moves = self.moves[::-1]
        self.parts = [
            (part.astype(F32) + got.astype(F32) + hold).astype(BF16)
            for part, got in zip(self.parts, self.got)
        ]


class PieceSums:
    def __init__(self, plan):
        self.plan = plan
        self.sums = {}

    def add(self, name, pair):
        self.sums[name] = ReplicaSum(pair)

    def add_top(self, g2, g1, g):
        g2 = lax.psum_scatter(g2, "fsdp", scatter_dimension=0, tiled=True)
        g1 = lax.psum_scatter(g1, "fsdp", scatter_dimension=1, tiled=True)
        g = lax.psum_scatter(g, "fsdp", scatter_dimension=1, tiled=True)
        half = g2.shape[0] // 2
        self.sums["top"] = ReplicaAll(g2[:half], g2[half:])
        self.sums["next"] = ReplicaAll(g1, g)

    def advance(self, hold, *names):
        found = []
        for name in names:
            found += self.sums[name].advance(hold)
        return found

    def finish(self, sums):
        last, mlp, top, following = (
            self.sums[name] for name in ("attend", "mlp", "top", "next")
        )
        riders = ReplicaSum(pack_riders(self.plan, sums, mlp.advance(nothing(sums[0][0][:1]))))
        last.advance()
        for _ in range(3):
            riders.advance()
        mlp.advance()
        mlp.advance()
        crossed = last.advance()[0]
        last.advance()
        first = last.result[0][0, :1]
        last.result = [jnp.concatenate(pair, 1) for pair in zip(last.result, riders.result)]
        last.advance()
        following.advance(nothing(crossed[0, :1]))
        late = to_replicas(mlp.total + nothing(first))
        last.advance()
        self.token = last.total[:1]
        following.advance()
        following.add()
        top.add()
        big = assemble_late((*top.parts, following.parts[0]), late)
        return assemble_last(to_replicas(last.total), following.parts[1:]), big


def to_replicas(value):
    return value, to_x(value), to_y(value), to_xy(value)


def load_replicas(refs, held, sem):
    rep = lax.axis_index("rep")
    copies = [
        pltpu.make_async_copy(ref, held.at[rep ^ away], sem.at[away])
        for away, ref in enumerate(refs)
    ]
    for copy in copies:
        copy.start()
    return copies


def late_kernel(flow, low_ref, high_ref, g1_ref, *refs):
    held, sem = refs[6:]
    fc1_ref, fc2_ref = refs[4:6]
    copies = load_replicas(refs[:4], held, sem)
    width = fc2_ref.shape[2]
    span = g1_ref.shape[1]
    flow.need(low_ref, high_ref, g1_ref)
    half = low_ref.shape[0]
    fc2_ref[1, :half] = low_ref[...].astype(F32)
    fc2_ref[1, half:] = high_ref[...].astype(F32)
    for block in range(4):
        fc1_ref[1, :, block * width : (block + 1) * width] = g1_ref[block].astype(F32)
    for copy in copies:
        copy.wait()
    for block in range(4):
        fc1_ref[0, :, block * width : (block + 1) * width] = held[block, span:].astype(F32)
        fc2_ref[0, block * span : (block + 1) * span, :] = held[block, :span].astype(F32)


def assemble_late(top, late):
    _, span, width = top[2].shape
    return call(
        late_kernel, top, Pieces(late),
        [shape((LAYERS, span, 4 * width), F32), shape((LAYERS, 4 * span, width), F32)],
        [pltpu.VMEM((4, *late[0].shape), BF16), pltpu.SemaphoreType.DMA((4,))], 4,
    )


class Pieces:
    def __init__(self, arrays):
        self.arrays, self.count = arrays, len(arrays)


def last_kernel(flow, g_ref, *refs):
    last_refs, refs = refs[:4], refs[4:]
    (qkv_ref, proj_ref), refs = refs[:2], refs[2:]
    small_refs, (held, sem) = refs[:10], refs[10:]
    copies = load_replicas(last_refs, held, sem)
    width = proj_ref.shape[2]
    span = g_ref.shape[1]
    flow.need(g_ref)

    def put(layer, blocks):
        for i, block in enumerate(blocks[:3]):
            qkv_ref[layer, :, i * width : (i + 1) * width] = block.astype(F32)
        proj_ref[layer] = blocks[3].astype(F32)

    put(1, [g_ref[i] for i in range(4)])
    for copy in copies:
        copy.wait()
    put(0, [held[i, :span] for i in range(4)])
    unit = width // 8
    heads = held[0, span:].astype(F32)
    others = held[1, span:].astype(F32)
    rel = held[2, span:].astype(F32)
    qv, pb, n1g, n1b, n2g, n2b, f1b, f2b, rh, rw = small_refs
    size = rh.shape[1]
    for layer in range(LAYERS):
        for ref, row in ((pb, 0), (n1g, 3), (n1b, 4), (n2g, 5), (n2b, 6), (f2b, 7)):
            ref[layer : layer + 1, :] = heads[row : row + 1, layer * unit : (layer + 1) * unit]
        qv[layer : layer + 1, :] = others[layer : layer + 1, : 2 * unit]
        f1b[layer : layer + 1, :] = others[layer : layer + 1, 2 * unit : 6 * unit]
        rh[layer : layer + 1, :] = rel[2 * layer : 2 * layer + 1, :size]
        rw[layer : layer + 1, :] = rel[2 * layer + 1 : 2 * layer + 2, :size]


def assemble_last(last, parts):
    _, span, width = parts[0].shape
    unit = width // 8
    sizes = (2 * unit, *[unit] * 5, 4 * unit, unit, RELS * HD // 8, RELS * HD // 8)
    outs = [shape((LAYERS, span, 3 * width), F32), shape((LAYERS, span, width), F32)]
    outs += [shape((LAYERS, size), F32) for size in sizes]
    return call(
        last_kernel, parts, Pieces(last), outs,
        [pltpu.VMEM((4, *last[0].shape), BF16), pltpu.SemaphoreType.DMA((4,))], 4,
    )


def pack_kernel(plan, flow, *refs):
    (
        (heads_ref, hidden_ref, rel_ref), (heads1_ref, hidden1_ref, rel1_ref)
    ), refs = (refs[:3], refs[3:6]), refs[6:]
    sink = plan.sink(refs[: plan.sinks], refs[plan.sinks :], True)
    held = sink.held
    held[...] = jnp.zeros_like(held)
    layers = ((heads_ref, hidden_ref, rel_ref), (heads1_ref, hidden1_ref, rel1_ref))
    span = heads_ref.shape[1] // 8
    for layer, (heads, hidden, rel) in enumerate(layers):
        for shard in range(8):
            core, level = shard & 1, shard >> 1
            cut = heads[:, shard * span : (shard + 1) * span]
            held[core, 0, level, :, layer * span : (layer + 1) * span] = cut.astype(BF16)
            first = shard % 4 * 2 * span
            row = 1 if shard < 4 else 2
            pair = heads[row : row + 1, first : first + 2 * span]
            held[core, 1, level, layer : layer + 1, 0 : 2 * span] = pair.astype(BF16)
            start = shard * 4 * span
            held[core, 1, level, layer : layer + 1, 2 * span : 6 * span] = hidden[
                :, start : start + 4 * span
            ].astype(BF16)
            held[core, 2, level, 2 * layer : 2 * layer + 2, 0 : rel.shape[2]] = rel[
                shard
            ].astype(BF16)
    sink.send_all()
    sink.wait()


def pack_riders(plan, sums, after):
    resident = []
    width = sums[0][0].shape[1]
    for heads, hidden, rel in sums:
        resident += [heads, hidden, rel]
    return call(
        functools.partial(pack_kernel, plan), resident, Source(), [], [], 3,
        [plan.sink_outs((32, RIDERS, width))], after,
    )


class WholeSums:
    def __init__(self, plan):
        self.pairs = {}

    def add(self, name, pair):
        self.pairs[name] = pair

    def add_top(self, g2, g1, g):
        self.top = whole_reduce(g, 1), whole_reduce(g1, 1), whole_reduce(g2, 0)

    def advance(self, hold, *names):
        return ()

    def finish(self, sums):
        self.token = sums[0][0][:1]
        big = [
            named(*whole_sums((self.pairs["attend"], self.pairs["mlp"]))), named(*self.top)
        ]
        shards = lax.axis_size("fsdp")
        parts = []
        for heads, hidden, rel in sums:
            rel = rel.transpose(1, 0, 2).reshape(2, -1)
            rows = (
                jnp.concatenate([heads[1], heads[2]]), heads[0], heads[3], heads[4], heads[5],
                heads[6], hidden[0], heads[7], rel[0], rel[1],
            )
            parts.append([row.reshape(shards, -1) for row in rows])
        cuts = np.cumsum([0] + [part.shape[1] for part in parts[0]])
        small = jnp.stack([jnp.concatenate(rows, 1) for rows in parts])
        mine = whole_reduce(small.astype(BF16), 1).astype(F32)[:, 0]
        stacked = [
            jnp.stack([big[layer][i] for layer in range(LAYERS)]).astype(F32) for i in range(4)
        ]
        small = [mine[:, a:b] for a, b in zip(cuts, cuts[1:])]
        return (*stacked[:2], *small), stacked[2:]


def on_device(
    ring, windows, slot_table, cotangent, qkv_weight, qv_bias, proj_weight, proj_bias,
    norm1_gain, norm1_bias, norm2_gain, norm2_bias, fc1_weight, fc1_bias, fc2_weight, fc2_bias,
    rel_height, rel_width,
):
    width = windows.shape[1]
    weights = (qkv_weight, proj_weight, fc1_weight, fc2_weight)
    parts = (
        qv_bias, proj_bias, norm1_gain, norm1_bias, norm2_gain, norm2_bias, fc1_bias, fc2_bias,
        rel_height, rel_width,
    )
    cuts = np.cumsum([0] + [part.shape[1] for part in parts])
    if ring:
        plan = PiecePlan()
        pending = PieceSums(plan)
        held = PieceWeights(weights, jnp.concatenate(parts, 1).reshape(-1))
    else:
        plan = WholePlan()
        pending = WholeSums(plan)
        held = WholeWeights(weights, parts)
    small = held.small
    (
        qv_bias_w, proj_bias_w, norm1_gain_w, norm1_bias_w, norm2_gain_w, norm2_bias_w,
        fc1_bias_w, fc2_bias_w, rel_height_w, rel_width_w,
    ) = [
        small[:, :, a:b].transpose(1, 0, 2).reshape(LAYERS, -1) for a, b in zip(cuts, cuts[1:])
    ]
    vec = jnp.stack(
        [norm1_gain_w, norm1_bias_w, qv_bias_w[:, :width], qv_bias_w[:, width:], proj_bias_w,
         norm2_gain_w, norm2_bias_w, fc2_bias_w], 1
    ).astype(F32)
    hidden_bias = fc1_bias_w.astype(F32)[:, None, :]
    ahead, back = relative_tables(rel_height_w, rel_width_w)
    keys_ahead, keys_back = key_tables()
    live = live_rows(slot_table)
    current = spread(windows)
    grad = spread(cotangent)
    whole = WholePlan()
    kept = []
    for layer in range(LAYERS):
        top = layer == LAYERS - 1
        after = held.before(f"attend_{layer}")
        if layer == 0:
            after = (*after, back)
        mid, h1, q, k, v, p, att, token = attend_forward(
            current, live, vec[layer], ahead[layer], keys_ahead, held.source(layer, "attend"),
            after,
        )
        held.passed(f"attend_{layer}", token)
        used = ("fc1",) if top else ("fc1", "fc2")
        after = held.before(f"mlp_{layer}")
        made = mlp_forward(
            whole, top, mid, live, vec[layer], hidden_bias[layer], grad,
            held.source(layer, *used), after,
        )
        following = None
        if top:
            h2, act, slope, top_sums, top_g2 = made
        else:
            following, h2, act, slope = made
        kept.append((current, mid, h1, q, k, v, p, att, h2, act, slope))
        current = following
    sums = [None] * LAYERS
    steps = {"middle_0": ("top",), "scores_0": ("top", "mlp"), "first_0": ("mlp",)}

    def ahead_of(name, past):
        return pending.advance(nothing(past.astype(F32)), *steps.get(name, ()))

    for layer in reversed(range(LAYERS)):
        top = layer == LAYERS - 1
        x, mid, h1, q, k, v, p, att, h2, act, slope = kept[layer]
        if top:
            dmid, sums2, hsum, top_g1 = top_backward(
                whole, grad, mid, live, vec[layer], h2, slope, held.source(layer, "fc1", "fc2"),
                (),
            )
            sums3 = top_sums
        else:
            dh, sums3, hsum, *pair = hidden_backward(
                plan, grad, act, live, h2, slope, held.source(layer, "fc2"), ()
            )
            pending.add("mlp", pair)
            dmid, sums2 = middle_backward(
                grad, mid, vec[layer], dh, held.source(layer, "fc1"), ahead_of("middle_0", sums3[:1])
            )
        db, dq, dk, dv, sums1, rel = scores_backward(
            dmid, live, back[layer], keys_back, q, k, v, p, held.source(layer, "proj"),
            ahead_of(f"scores_{layer}", sums2[:1]),
        )
        if top:
            grad, sums4, top_g = first_all_backward(
                whole, dmid, x, live, vec[layer], h1, att, db, dq, dk, dv,
                held.source(layer, "attend"), (),
            )
            pending.add_top(top_g2, top_g1, top_g)
        else:
            pair = weights_backward(plan, h1, att, db, dq, dk, dv, ())
            pending.add("attend", pair)
            grad, sums4 = first_backward(
                dmid, x, live, vec[layer], dq, dk, dv, held.source(layer, "attend"),
                ahead_of("first_0", pair[0][(0,) * (pair[0].ndim - 2)][:1]),
            )
        rel = rel[:, :HD] + rel[:, HD:]
        rel = jnp.stack([rel[:RELS].reshape(8, -1), rel[HD : HD + RELS].reshape(8, -1)], 1)
        sums[layer] = (sums1 + sums2 + sums3 + sums4, hsum, rel)
    (qkv_grad, proj_grad, *small), (fc1_grad, fc2_grad) = pending.finish(sums)
    output = gather_back(
        mlp_output(
            kept[-1][9], vec[-1], kept[-1][1], live, held.source(LAYERS - 1, "fc2"),
            (pending.token,),
        )
    ).astype(BF16)
    input_grad = gather_back(grad + nothing(pending.token.astype(F32))).astype(BF16)
    qv, pb, n1g, n1b, n2g, n2b, f1b, f2b, rh, rw = small
    return (
        output, input_grad, qkv_grad, qv, proj_grad, pb, n1g, n1b, n2g, n2b, fc1_grad, f1b,
        fc2_grad, f2b, rh, rw,
    )


def solution(mesh):
    rows = P(("rep", "fsdp"), None)
    cube = P(None, "fsdp", None)
    flat = P(None, "fsdp")
    ring = mesh.shape["rep"] == 4 and mesh.shape["fsdp"] == 8
    return jax.shard_map(
        functools.partial(on_device, ring),
        mesh=mesh,
        in_specs=(
            rows, P(("rep", "fsdp")), rows, cube, flat, cube, flat, flat, flat, flat, flat, cube,
            flat, cube, flat, flat, flat,
        ),
        out_specs=(
            rows, rows, cube, flat, cube, flat, flat, flat, flat, flat, cube, flat, cube, flat,
            flat, flat,
        ),
        check_vma=False,
    )
```
